32 devices in a mesh: frame: 8 (over z, core), video: 4 (over y, x).
Axes of the slice: x: 2, y: 2, z: 4, core: 2. Of those that a mesh axis runs over, the one named last changes fastest.
Arguments:
- video: bfloat16 [24, 8, 197, 768], P('video', 'frame'), may hold values from -6 to 6
- video_live: int32 [24], P('video'), may hold values 0 or 1
- cotangent: bfloat16 [24, 8, 198, 768], P('video', 'frame'), may hold values from -6 to 6
- message_proj: bfloat16 [768, 768], replicated, may hold values from -0.21875 to 0.21875
- message_bias: float32 [768], replicated, may hold values from -3 to 3
- message_gain: float32 [768], replicated, may hold values from 0.5 to 1.5
- message_shift: float32 [768], replicated, may hold values from -1.75 to 1.75
- message_qkv: bfloat16 [768, 2304], replicated, may hold values from -0.21875 to 0.21875
- message_out: bfloat16 [768, 768], replicated, may hold values from -0.4375 to 0.4375
- frame_gain: float32 [768], replicated, may hold values from 0.5 to 1.5
- frame_shift: float32 [768], replicated, may hold values from -1.75 to 1.75
- frame_qkv: bfloat16 [768, 2304], replicated, may hold values from -0.21875 to 0.21875
- frame_out: bfloat16 [768, 768], replicated, may hold values from -0.875 to 0.875
- dense_gain: float32 [768], replicated, may hold values from 0.5 to 1.5
- dense_shift: float32 [768], replicated, may hold values from -1.75 to 1.75
- dense_in: bfloat16 [768, 3072], replicated, may hold values from -0.21875 to 0.21875
- dense_in_bias: float32 [3072], replicated, may hold values from -3 to 3
- dense_out: bfloat16 [3072, 768], replicated, may hold values from -0.21875 to 0.21875
- dense_out_bias: float32 [768], replicated, may hold values from -3 to 3
Outputs:
- output: bfloat16 [24, 8, 198, 768], P('video', 'frame')
- grad_video: bfloat16 [24, 8, 197, 768], P('video', 'frame')
- grad_message_proj: float32 [768, 768], P('video')
- grad_message_bias: float32 [768], P('video')
- grad_message_gain: float32 [768], P('video')
- grad_message_shift: float32 [768], P('video')
- grad_message_qkv: float32 [768, 2304], P('video')
- grad_message_out: float32 [768, 768], P('video')
- grad_frame_gain: float32 [768], P('video')
- grad_frame_shift: float32 [768], P('video')
- grad_frame_qkv: float32 [768, 2304], P('video')
- grad_frame_out: float32 [768, 768], P('video')
- grad_dense_gain: float32 [768], P('video')
- grad_dense_shift: float32 [768], P('video')
- grad_dense_in: float32 [768, 3072], P('video')
- grad_dense_in_bias: float32 [3072], P('video')
- grad_dense_out: float32 [3072, 768], P('video')
- grad_dense_out_bias: float32 [768], P('video')
The draws below stay inside these ranges and needn't reach their ends.
Inputs may be any that keep to these rules, and one draw needn't show every extreme that they name: `video_live`: 1 marks a video whose output gradient counts, 0 a padded slot.
All inputs are finite; a program needn't handle non-finite values. No bound on the sum of `video_live` on one device may be relied on, other than what follows from the above.
Results may differ from the reference program's by a relative error of at most 0.025.
Values may be sent and summed in bfloat16 or wider, within the bound.
A program may use at most 192 MiB of HBM per device.

```python
import jax
import jax.numpy as jnp
from jax import lax

D = 768
HEADS = 12
HEAD_DIM = 64
FF = 3072
PATCHES = 197
TOKENS_F = 198
FRAMES = 8
VIDEOS = 24


def with_ends(result, rng, smallest, top_value):
    longest = result.shape.index(max(result.shape))
    spots = []
    for shift in (0, 1):
        where = [jax.random.randint(jax.random.fold_in(rng, axis), (), 0, length) for axis, length in enumerate(result.shape)]
        where[longest] = (where[longest] + shift) % result.shape[longest]
        spots.append(tuple(where))
    return result.at[spots[0]].set(smallest).at[spots[1]].set(top_value)


def shard_levels(rng, extent, pieces, low, high):
    loudness, own = 1.0, jax.random.fold_in(rng, 6)
    for dim, blocks in pieces:
        steps = jnp.exp(jax.random.uniform(jax.random.fold_in(own, dim), (blocks,), jnp.float32, low / len(pieces), high / len(pieces)))
        loudness = loudness * jnp.repeat(steps, extent[dim] // blocks).reshape([-1 if axis == dim else 1 for axis in range(len(extent))])
    return loudness


def gaussian(rng, shape, scale, bound, shards=(), held_as=jnp.bfloat16):
    level = shard_levels(rng, shape, shards, -0.22, 0.18) if shards else 1.0
    entries = jax.random.normal(rng, shape, jnp.float32) * scale * level
    return jnp.minimum(jnp.maximum(entries, -bound), bound).astype(held_as)


def setup_inputs(seed: int = 0) -> dict:
    streams_of = jax.random.split(jax.random.key(seed), 20)
    video = gaussian(streams_of[0], (VIDEOS, FRAMES, PATCHES, D), 1.0, 6.0, ((0, 4), (1, 8)))
    video_live = with_ends((jax.random.randint(streams_of[1], (VIDEOS,), 0, 4) < 3).astype(jnp.int32), jax.random.fold_in(streams_of[1], 1), 0, 1)
    cotangent = gaussian(streams_of[2], (VIDEOS, FRAMES, TOKENS_F, D), 1.0, 6.0, ((0, 4), (1, 8)))
    message_proj = gaussian(streams_of[3], (D, D), D ** -0.5, 0.21875)
    message_bias = gaussian(streams_of[4], (D,), 0.5, 3.0, (), jnp.float32)
    message_gain = jnp.clip(1.0 + 0.1 * jax.random.normal(streams_of[5], (D,), jnp.float32), 0.5, 1.5)
    message_shift = gaussian(streams_of[6], (D,), 0.3, 1.75, (), jnp.float32)
    message_qkv = gaussian(streams_of[7], (D, 3 * D), D ** -0.5, 0.21875)
    message_out = gaussian(streams_of[8], (D, D), (D // 4) ** -0.5, 0.4375)
    frame_gain = jnp.clip(1.0 + 0.1 * jax.random.normal(streams_of[9], (D,), jnp.float32), 0.5, 1.5)
    frame_shift = gaussian(streams_of[10], (D,), 0.3, 1.75, (), jnp.float32)
    frame_qkv = gaussian(streams_of[11], (D, 3 * D), D ** -0.5, 0.21875)
    frame_out = gaussian(streams_of[12], (D, D), (D // 14) ** -0.5, 0.875)
    dense_gain = jnp.clip(1.0 + 0.1 * jax.random.normal(streams_of[13], (D,), jnp.float32), 0.5, 1.5)
    dense_shift = gaussian(streams_of[14], (D,), 0.3, 1.75, (), jnp.float32)
    dense_in = gaussian(streams_of[15], (D, FF), D ** -0.5, 0.21875)
    dense_in_bias = gaussian(streams_of[16], (FF,), 0.5, 3.0, (), jnp.float32)
    dense_out = gaussian(streams_of[17], (FF, D), (FF // 4) ** -0.5, 0.21875)
    dense_out_bias = gaussian(streams_of[18], (D,), 0.5, 3.0, (), jnp.float32)
    return {"video": video, "video_live": video_live, "cotangent": cotangent, "message_proj": message_proj, "message_bias": message_bias, "message_gain": message_gain, "message_shift": message_shift, "message_qkv": message_qkv, "message_out": message_out, "frame_gain": frame_gain, "frame_shift": frame_shift, "frame_qkv": frame_qkv, "frame_out": frame_out, "dense_gain": dense_gain, "dense_shift": dense_shift, "dense_in": dense_in, "dense_in_bias": dense_in_bias, "dense_out": dense_out, "dense_out_bias": dense_out_bias}


EPS = 1e-05
HIGH = lax.Precision.HIGHEST

@jax.custom_vjp
def low(v):
    return lax.optimization_barrier(v.astype(jnp.bfloat16)).astype(jnp.float32)

@jax.custom_vjp
def low_back(v):
    return v

def low_keep(v):
    return (low(v), None)

def low_pass(kept, grad):
    return (grad,)

def back_keep(v):
    return (v, None)

def back_low(kept, grad):
    return (low(grad),)
low.defvjp(low_keep, low_pass)
low_back.defvjp(back_keep, back_low)

def layer_norm(values, gain, shift):
    center = values - lax.optimization_barrier(jnp.mean(values, axis=-1, keepdims=True))
    spread = lax.optimization_barrier(jnp.mean(center * center, axis=-1, keepdims=True))
    return center * lax.rsqrt(spread + EPS) * gain + shift

def linear(inputs, weight):
    return low_back(jnp.dot(low(inputs), weight, precision=HIGH))

def attend(packed):
    width = packed.shape[-1] // 3
    leading = packed.shape[:-1]
    query_rows = packed[..., :width].reshape(leading + (HEADS, HEAD_DIM))
    key_rows = packed[..., width:2 * width].reshape(leading + (HEADS, HEAD_DIM))
    value_rows = packed[..., 2 * width:].reshape(leading + (HEADS, HEAD_DIM))
    scores = low_back(jnp.einsum('...qhd,...khd->...hqk', low(query_rows), low(key_rows), precision=HIGH) * 0.125)
    probs = jax.nn.softmax(scores, axis=-1)
    mixed = jnp.einsum('...hqk,...khd->...qhd', low(probs), low(value_rows), precision=HIGH)
    return low_back(mixed).reshape(leading + (width,))

def forward(video, message_proj, message_bias, message_gain, message_shift, message_qkv, message_out, frame_gain, frame_shift, frame_qkv, frame_out, dense_gain, dense_shift, dense_in, dense_in_bias, dense_out, dense_out_bias):
    message = low(linear(video[:, :, 0, :], message_proj) + message_bias)
    normed = layer_norm(message, message_gain, message_shift)
    mixed = attend(linear(normed, message_qkv))
    message_next = message + linear(mixed, message_out)
    tokens = jnp.concatenate([video, message_next[:, :, None, :]], axis=2)
    normed = layer_norm(tokens, frame_gain, frame_shift)
    packed = linear(normed, frame_qkv)
    mixed = lax.map(jax.checkpoint(attend), packed)
    middle = tokens + linear(mixed, frame_out)
    normed = layer_norm(middle, dense_gain, dense_shift)
    inner = linear(normed, dense_in) + dense_in_bias
    active = inner * jax.nn.sigmoid(1.702 * inner)
    return middle + linear(active, dense_out) + dense_out_bias

def reference(video, video_live, cotangent, message_proj, message_bias, message_gain, message_shift, message_qkv, message_out, frame_gain, frame_shift, frame_qkv, frame_out, dense_gain, dense_shift, dense_in, dense_in_bias, dense_out, dense_out_bias):
    params = [weight.astype(jnp.float32) for weight in (message_proj, message_bias, message_gain, message_shift, message_qkv, message_out, frame_gain, frame_shift, frame_qkv, frame_out, dense_gain, dense_shift, dense_in, dense_in_bias, dense_out, dense_out_bias)]
    output, pullback = jax.vjp(forward, video.astype(jnp.float32), *params)
    weights_live = video_live.astype(jnp.float32)[:, None, None, None]
    grads = pullback(cotangent.astype(jnp.float32) * weights_live)
    return (output.astype(jnp.bfloat16), grads[0].astype(jnp.bfloat16), grads[1], grads[2], grads[3], grads[4], grads[5], grads[6], grads[7], grads[8], grads[9], grads[10], grads[11], grads[12], grads[13], grads[14], grads[15], grads[16])
```

```python
import functools
import jax
import jax.numpy as jnp
from jax import lax
from jax.experimental import pallas as pl
from jax.experimental.pallas import tpu as pltpu
bf=jnp.bfloat16; f32=jnp.float32
EPS=1e-5
def dot(a,b,ca=1,cb=0): return lax.dot_general(a,b,(((ca,),(cb,)),((),())),preferred_element_type=f32)
FR=6; T=208; RR=FR*T; RP=1280; D=768
def k2(MB, mid, cot, live, din0,din1,din2,din3, do0,do1,do2,do3, bin_, bout, gain, shift,
       out_ref, gmid_ref, gdi_ref, gdo_ref, gbin_ref, small_ref,
       sec, G, act, dinn, oacc, gsec):
    j=pl.program_id(0)
    @pl.when(j==0)
    def _():
        ob=jnp.zeros((1,D),f32)
        sec[pl.ds(RR,RP-RR),:]=jnp.zeros((RP-RR,D),bf)
        G[pl.ds(RR,RP-RR),:]=jnp.zeros((RP-RR,D),bf)
        act[pl.ds(RR,RP-RR),:]=jnp.zeros((RP-RR,512),bf)
        dinn[pl.ds(RR,RP-RR),:]=jnp.zeros((RP-RR,512),bf)
        for f in range(FR):
            x=mid[f*T:(f+1)*T,:]
            mu=jnp.mean(x,-1,keepdims=True); c=x-mu
            inv=lax.rsqrt(jnp.mean(c*c,-1,keepdims=True)+EPS)
            sec[f*T:(f+1)*T,:]=(c*inv*gain[...]+shift[...]).astype(bf)
            g=cot[f,0].astype(f32)*live[f].astype(f32)
            g=jnp.concatenate([g,jnp.zeros((T-198,D),f32)],0)
            ob=ob+jnp.sum(g,0,keepdims=True)
            G[f*T:(f+1)*T,:]=g.astype(bf)
            oacc[f*T:(f+1)*T,:]=x+bout[...]
            gsec[f*T:(f+1)*T,:]=jnp.zeros((T,D),f32)
        small_ref[0:1,:]=ob
    din=jnp.concatenate([din0[...],din1[...],din2[...],din3[...]],1)
    do=jnp.concatenate([do0[...],do1[...],do2[...],do3[...]],0)
    b=jnp.concatenate([bin_[0:1,:],bin_[1:2,:],bin_[2:3,:],bin_[3:4,:]],1) if False else bin_[0]
    bsum=jnp.zeros((1,512),f32)
    for r in range(RR//MB):
        s=slice(r*MB,(r+1)*MB)
        inner=dot(sec[s,:],din)+b
        ga=dot(G[s,:],do,1,1)
        sg=0.5*jnp.tanh(0.851*inner)+0.5
        ac=inner*sg
        act[s,:]=ac.astype(bf)
        di=ga*(sg+1.702*ac*(1.0-sg))
        bsum=bsum+jnp.sum(di,0,keepdims=True)
        dinn[s,:]=di.astype(bf)
    gbin_ref[0]=bsum
    for r in range(RR//MB):
        s=slice(r*MB,(r+1)*MB)
        oacc[s,:]+=dot(act[s,:],do)
        gsec[s,:]+=dot(dinn[s,:],din,1,1)
    gdo_ref[0]=dot(G[...],act[...],0,0).astype(bf)
    gdi_ref[0]=dot(sec[...],dinn[...],0,0).astype(bf)
    @pl.when(j==pl.num_programs(0)-1)
    def _():
        gg=jnp.zeros((1,D),f32); gs=jnp.zeros((1,D),f32)
        for f in range(FR):
            s=slice(f*T,(f+1)*T)
            out_ref[f,0]=oacc[s,:][:198].astype(bf)
            x=mid[s,:]
            mu=jnp.mean(x,-1,keepdims=True); c=x-mu
            inv=lax.rsqrt(jnp.mean(c*c,-1,keepdims=True)+EPS)
            sc=c*inv
            go=gsec[s,:]
            gg=gg+jnp.sum(go*sc,0,keepdims=True); gs=gs+jnp.sum(go,0,keepdims=True)
            gsc=go*gain[...]
            gi=inv*(gsc-jnp.mean(gsc,-1,keepdims=True)-sc*jnp.mean(gsc*sc,-1,keepdims=True))
            gmid_ref[s,:]=G[s,:].astype(f32)+gi
        small_ref[1:2,:]=gg; small_ref[2:3,:]=gs
def call_k2(mid,cot,live,din,do,bin_,bout,gain,shift,MB=624):
    full=lambda *s: pl.BlockSpec(s,lambda j:(0,)*len(s))
    nq=din.shape[1]//512
    vm=pl.BlockSpec(memory_space=pltpu.VMEM)
    specs=[full(RR,D),full(FR,1,198,D),pl.BlockSpec(memory_space=pltpu.SMEM)]
    for q in range(4): specs.append(pl.BlockSpec((D,128),lambda j,q=q:(0,q*6+j)))
    for q in range(4): specs.append(pl.BlockSpec((128,D),lambda j,q=q:(q*6+j,0)))
    specs+= [pl.BlockSpec((1,1,512),lambda j:(j,0,0)),full(1,D),full(1,D),full(1,D)]
    b3=bin_.reshape(4,6,128).transpose(1,0,2).reshape(6,1,512)
    return pl.pallas_call(functools.partial(k2,MB),grid=(6,),in_specs=specs,
      out_specs=[full(FR,1,198,D),full(RR,D),pl.BlockSpec((1,D,512),lambda j:(j,0,0)),pl.BlockSpec((1,D,512),lambda j:(j,0,0)),pl.BlockSpec((1,1,512),lambda j:(j,0,0)),full(8,D)],
      out_shape=[jax.ShapeDtypeStruct((FR,1,198,D),bf),jax.ShapeDtypeStruct((RR,D),f32),jax.ShapeDtypeStruct((6,D,512),bf),jax.ShapeDtypeStruct((6,D,512),bf),jax.ShapeDtypeStruct((6,1,512),f32),jax.ShapeDtypeStruct((8,D),f32)],
      scratch_shapes=[pltpu.VMEM((RP,D),bf),pltpu.VMEM((RP,D),bf),pltpu.VMEM((RP,512),bf),pltpu.VMEM((RP,512),bf),pltpu.VMEM((RR,D),f32),pltpu.VMEM((RR,D),f32)],
      compiler_params=pltpu.CompilerParams(vmem_limit_bytes=61<<20,dimension_semantics=("arbitrary",)),
    )(mid,cot,live,din,din,din,din,do,do,do,do,b3,bout.reshape(1,D),gain.reshape(1,D),shift.reshape(1,D))
from jax.sharding import PartitionSpec as P
HEADS=12
HEAD_DIM=64
NEG=-1e30

def half_masks(rows):
    lane=lax.broadcasted_iota(jnp.int32,(rows,128),1)
    return lane<64
def k1(vid, mnext, wq, wk, wv, wo, gain, shift,
       qkv_ref, pt_ref, first_ref, mixed_ref, mid_ref):
    h=pl.program_id(0)
    @pl.when(h==0)
    def _():
        first_ref[pl.ds(RR,RP-RR),:]=jnp.zeros((RP-RR,D),bf)
        mixed_ref[:,pl.ds(RR,RP-RR),:]=jnp.zeros((6,RP-RR,128),bf)
        for f in range(FR):
            mid_ref[f*T+192:(f+1)*T,:]=jnp.zeros((T-192,D),f32)
            mid_ref[f*T:f*T+197,:]=vid[f,0].astype(f32)
            mid_ref[f*T+197:f*T+198,:]=mnext[f:f+1,:]
            x=mid_ref[f*T:(f+1)*T,:]
            mu=jnp.mean(x,-1,keepdims=True); c=x-mu
            inv=lax.rsqrt(jnp.mean(c*c,-1,keepdims=True)+EPS)
            first_ref[f*T:(f+1)*T,:]=(c*inv*gain[...]+shift[...]).astype(bf)
    w=jnp.concatenate([wq[...],wk[...],wv[...]],1)
    qkv_ref[0,0:RR,:]=dot(first_ref[0:RR,:],w).astype(bf)
    qkv_ref[0,RR:RP,:]=jnp.zeros((RP-RR,384),bf)
    lo=half_masks(T)
    keep=lax.broadcasted_iota(jnp.int32,(16,T),0)<6
    zero=jnp.zeros((T,128),bf)
    for f in range(FR):
        s=slice(f*T,(f+1)*T)
        q=qkv_ref[0,s,0:128]*jnp.asarray(0.125,bf); k=qkv_ref[0,s,128:256]; v=qkv_ref[0,s,256:384]
        ps=[]; vs=[]
        for e in range(2):
            m=lo if e==0 else jnp.logical_not(lo)
            st=dot(k,jnp.where(m,q,zero),1,1)
            top=st[:192]; bot=jnp.where(keep,st[192:],NEG)
            mx=jnp.maximum(jnp.max(top,0,keepdims=True),jnp.max(bot,0,keepdims=True))
            top=jnp.exp(top-mx); bot=jnp.exp(bot-mx)
            tot=jnp.sum(top,0,keepdims=True)+jnp.sum(bot,0,keepdims=True)
            p=(jnp.concatenate([top,bot],0)*(1.0/tot)).astype(bf)
            pt_ref[0,f*2+e]=p
            ps.append(p); vs.append(jnp.where(m,v,zero))
        o=dot(jnp.concatenate(ps,0),jnp.concatenate(vs,0),0,0)
        mixed_ref[h,s,:]=o.astype(bf)
    @pl.when(h==5)
    def _():
        mx=jnp.concatenate([mixed_ref[i,0:RR,:] for i in range(6)],1)
        mid_ref[...]+=dot(mx,wo[...])
def call_k1(video,mnext,qkv,wo,gain,shift):
    full=lambda *s: pl.BlockSpec(s,lambda j:(0,)*len(s))
    blk=lambda *s: pl.BlockSpec((1,)+s,lambda j:(j,)+(0,)*len(s))
    specs=[full(FR,1,197,D),full(FR,D)]+[pl.BlockSpec((D,128),lambda j,o=o:(0,o*6+j)) for o in range(3)]+[full(D,D),full(1,D),full(1,D)]
    return pl.pallas_call(k1,grid=(6,),in_specs=specs,
      out_specs=[blk(RP,384),blk(12,T,T),full(RP,D),full(6,RP,128),full(RR,D)],
      out_shape=[jax.ShapeDtypeStruct((6,RP,384),bf),jax.ShapeDtypeStruct((6,12,T,T),bf),jax.ShapeDtypeStruct((RP,D),bf),jax.ShapeDtypeStruct((6,RP,128),bf),jax.ShapeDtypeStruct((RR,D),f32)],
      compiler_params=pltpu.CompilerParams(vmem_limit_bytes=61<<20,dimension_semantics=("arbitrary",)),
    )(video,mnext,qkv,qkv,qkv,wo,gain.reshape(1,D),shift.reshape(1,D))
def k3(vid, mnext, gmid, qkv, pt, first, mixed, wq, wk, wv, wo, gain, shift,
       gtok_ref, gf_ref, small_ref, glow, dO, dpk, wqkv):
    h=pl.program_id(0)
    @pl.when(h==0)
    def _():
        glow[pl.ds(RR,RP-RR),:]=jnp.zeros((RP-RR,D),bf)
        dpk[:,pl.ds(RR,RP-RR),:]=jnp.zeros((6,RP-RR,384),bf)
        glow[0:RR,:]=gmid[...].astype(bf)
        d=dot(glow[0:RR,:],wo[...],1,1).astype(bf)
        for i in range(6): dO[i]=d[:,i*128:(i+1)*128]
    lo=half_masks(T)
    zero=jnp.zeros((T,128),bf)
    for f in range(FR):
        s=slice(f*T,(f+1)*T)
        q=qkv[0,s,0:128]; k=qkv[0,s,128:256]; v=qkv[0,s,256:384]
        do=dO[h,s,:]
        dss=[]; ks=[]; dk=0.; dv=0.
        for e in range(2):
            m=lo if e==0 else jnp.logical_not(lo)
            doe=jnp.where(m,do,zero)
            pb=pt[0,f*2+e]
            p=pb.astype(f32)
            dp=dot(v,doe,1,1)
            delta=jnp.sum(dp*p,0,keepdims=True)
            ds=(p*(dp-delta)).astype(bf)
            dk=dk+dot(ds,jnp.where(m,q,zero))
            dv=dv+dot(pb,doe)
            dss.append(ds); ks.append(jnp.where(m,k,zero))
        dq=dot(jnp.concatenate(dss,0),jnp.concatenate(ks,0),0,0)*0.125
        dpk[h,s,0:128]=dq.astype(bf)
        dpk[h,s,128:256]=(dk*0.125).astype(bf)
        dpk[h,s,256:384]=dv.astype(bf)
    for i in range(6):
        @pl.when(h==i)
        def _():
            wqkv[:,i*128:(i+1)*128]=wq[...]; wqkv[:,D+i*128:D+(i+1)*128]=wk[...]; wqkv[:,2*D+i*128:2*D+(i+1)*128]=wv[...]
            mx=jnp.concatenate([mixed[t] for t in range(6)],1)
            gf_ref[0,:,384:512]=dot(mx,glow[:,i*128:(i+1)*128],0,0).astype(bf)
    gf_ref[0,:,0:384]=dot(first[...],dpk[h],0,0).astype(bf)
    @pl.when(h==5)
    def _():
        dx=jnp.concatenate([dpk[i,0:RR,g*128:(g+1)*128] for g in range(3) for i in range(6)],1)
        gtok_ref[...]=dot(dx,wqkv[...],1,1)
        gg=jnp.zeros((1,D),f32); gs=jnp.zeros((1,D),f32)
        for f in range(FR):
            s=slice(f*T,(f+1)*T)
            x=jnp.concatenate([vid[f,0].astype(f32),mnext[f:f+1,:],jnp.zeros((T-198,D),f32)],0)
            mu=jnp.mean(x,-1,keepdims=True); c=x-mu
            inv=lax.rsqrt(jnp.mean(c*c,-1,keepdims=True)+EPS)
            sc=c*inv
            go=gtok_ref[s,:]
            gg=gg+jnp.sum(go*sc,0,keepdims=True); gs=gs+jnp.sum(go,0,keepdims=True)
            gsc=go*gain[...]
            gi=inv*(gsc-jnp.mean(gsc,-1,keepdims=True)-sc*jnp.mean(gsc*sc,-1,keepdims=True))
            gtok_ref[s,:]=gmid[s,:]+gi
        small_ref[0:1,:]=gg; small_ref[1:2,:]=gs
def call_k3(video,mnext,gmid,qkvs,pt,first,mixed,qkv,wo,gain):
    full=lambda *s: pl.BlockSpec(s,lambda j:(0,)*len(s))
    blk=lambda *s: pl.BlockSpec((1,)+s,lambda j:(j,)+(0,)*len(s))
    specs=[full(FR,1,197,D),full(FR,D),full(RR,D),blk(RP,384),blk(12,T,T),full(RP,D),full(6,RP,128)]+[pl.BlockSpec((D,128),lambda j,o=o:(0,o*6+j)) for o in range(3)]+[full(D,D),full(1,D),full(1,D)]
    return pl.pallas_call(k3,grid=(6,),in_specs=specs,
      out_specs=[full(RR,D),blk(D,512),full(8,D)],
      out_shape=[jax.ShapeDtypeStruct((RR,D),f32),jax.ShapeDtypeStruct((6,D,512),bf),jax.ShapeDtypeStruct((8,D),f32)],
      scratch_shapes=[pltpu.VMEM((RP,D),bf),pltpu.VMEM((6,RR,128),bf),pltpu.VMEM((6,RP,384),bf),pltpu.VMEM((D,3*D),bf)],
      compiler_params=pltpu.CompilerParams(vmem_limit_bytes=61<<20,dimension_semantics=("arbitrary",)),
    )(video,mnext,gmid,qkvs,pt,first,mixed,qkv,qkv,qkv,wo,gain.reshape(1,D),gain.reshape(1,D))


def column_sum(values):
    return jnp.sum(values.reshape(-1, values.shape[-1]), axis=0)


def matmul(left, right):
    return jnp.dot(left, right, preferred_element_type=f32)


def back_matmul(grad_low, weight):
    return lax.dot_general(grad_low, weight, (((grad_low.ndim - 1,), (1,)), ((), ())), preferred_element_type=f32)


def weight_grad(inputs_low, grad_low):
    left = inputs_low.reshape(-1, inputs_low.shape[-1])
    right = grad_low.reshape(-1, grad_low.shape[-1])
    return lax.dot_general(left, right, (((0,), (0,)), ((), ())), preferred_element_type=f32)


def norm_forward(values, gain, shift):
    center = values - jnp.mean(values, axis=-1, keepdims=True)
    inverse = lax.rsqrt(jnp.mean(center * center, axis=-1, keepdims=True) + EPS)
    scaled = center * inverse
    return (scaled * gain + shift, scaled, inverse)


def norm_backward(grad_out, scaled, inverse, gain):
    grad_scaled = grad_out * gain
    grad_in = inverse * (
        grad_scaled
        - jnp.mean(grad_scaled, axis=-1, keepdims=True)
        - scaled * jnp.mean(grad_scaled * scaled, axis=-1, keepdims=True)
    )
    return (grad_in, column_sum(grad_out * scaled), column_sum(grad_out))


def split_heads(values):
    return values.reshape(values.shape[:-1] + (HEADS, HEAD_DIM))


def attend_forward(query_rows, key_rows, value_rows):
    scores = jnp.einsum("bqhd,bkhd->bhqk", query_rows, key_rows, preferred_element_type=f32) * 0.125
    largest = jnp.max(scores, axis=-1, keepdims=True)
    raised = jnp.exp(scores - largest)
    total = jnp.sum(raised, axis=-1, keepdims=True)
    probs_low = (raised / total).astype(bf)
    mixed = jnp.einsum("bhqk,bkhd->bqhd", probs_low, value_rows, preferred_element_type=f32)
    return (mixed, largest + jnp.log(total))


def attend_backward(query_rows, key_rows, value_rows, log_total, grad_mixed):
    scores = jnp.einsum("bqhd,bkhd->bhqk", query_rows, key_rows, preferred_element_type=f32) * 0.125
    probs = jnp.exp(scores - log_total)
    grad_probs = jnp.einsum("bqhd,bkhd->bhqk", grad_mixed, value_rows, preferred_element_type=f32)
    grad_scores = probs * (grad_probs - jnp.sum(grad_probs * probs, axis=-1, keepdims=True))
    grad_low = grad_scores.astype(bf)
    grad_query = jnp.einsum("bhqk,bkhd->bqhd", grad_low, key_rows, preferred_element_type=f32) * 0.125
    grad_key = jnp.einsum("bhqk,bqhd->bkhd", grad_low, query_rows, preferred_element_type=f32) * 0.125
    grad_value = jnp.einsum("bhqk,bqhd->bkhd", probs.astype(bf), grad_mixed, preferred_element_type=f32)
    return (grad_query, grad_key, grad_value)


def message_forward(video, message_proj, message_bias, message_gain, message_shift, message_qkv, message_out):
    width = video.shape[-1]
    batch, frames_local = video.shape[:2]
    class_rows = video[:, :, 0, :]
    message = (matmul(class_rows, message_proj) + message_bias).astype(bf)
    message_wide = message.astype(f32)
    normed_own, scaled_own, inverse_own = norm_forward(message_wide, message_gain, message_shift)
    normed_low = normed_own.astype(bf)
    everyone = lax.all_gather(message, "frame", axis=1, tiled=True)
    normed_all = norm_forward(everyone.astype(f32), message_gain, message_shift)[0]
    key_value = matmul(normed_all.astype(bf), message_qkv[:, width:]).astype(bf)
    query = split_heads(matmul(normed_low, message_qkv[:, :width]).astype(bf))
    key = split_heads(key_value[..., :width])
    value = split_heads(key_value[..., width:])
    mixed, total = attend_forward(query, key, value)
    mixed_low = mixed.reshape(batch, frames_local, width).astype(bf)
    message_next = message_wide + matmul(mixed_low, message_out)
    return message_next, (class_rows, normed_low, scaled_own, inverse_own, query, key, value, mixed_low, total)


def message_backward(kept, grad_next, message_proj, message_gain, message_qkv, message_out):
    class_rows, normed_low, scaled_own, inverse_own, query, key, value, mixed_low, total = kept
    batch, frames_local, width = grad_next.shape
    frames_all = key.shape[1]
    grad_next_low = grad_next.astype(bf)
    grad_mixed = split_heads(back_matmul(grad_next_low, message_out).astype(bf))
    grad_q, grad_k, grad_v = attend_backward(query, key, value, total, grad_mixed)
    key_value_grad = jnp.concatenate(
        [grad_k.reshape(batch, frames_all, width), grad_v.reshape(batch, frames_all, width)], axis=-1
    )
    own = lax.psum_scatter(key_value_grad.astype(bf), "frame", scatter_dimension=1, tiled=True)
    packed = jnp.concatenate([grad_q.reshape(batch, frames_local, width).astype(bf), own], axis=-1)
    grad_in, grad_gain, grad_shift = norm_backward(
        back_matmul(packed, message_qkv), scaled_own, inverse_own, message_gain
    )
    grad_message = grad_next + grad_in
    grad_message_low = grad_message.astype(bf)
    grad_class = back_matmul(grad_message_low, message_proj)
    rows = jnp.concatenate([class_rows, normed_low, mixed_low, grad_message_low, packed, grad_next_low], axis=-1)
    rows = rows.reshape(batch * frames_local, -1)
    return grad_class, rows, column_sum(grad_message), grad_gain, grad_shift


def local(
    video,
    video_live,
    cotangent,
    message_proj,
    message_bias,
    message_gain,
    message_shift,
    message_qkv,
    message_out,
    frame_gain,
    frame_shift,
    frame_qkv,
    frame_out,
    dense_gain,
    dense_shift,
    dense_in,
    dense_in_bias,
    dense_out,
    dense_out_bias,
):
    batch, frames_local, patches, width = video.shape
    hidden = dense_in.shape[1]
    groups = lax.axis_size("video")
    message_next, kept = message_forward(
        video, message_proj, message_bias, message_gain, message_shift, message_qkv, message_out
    )
    next_rows = message_next.reshape(batch * frames_local, width)
    packed, probs, first, mixed, middle = call_k1(video, next_rows, frame_qkv, frame_out, frame_gain, frame_shift)
    output, grad_middle, part_in, part_out, part_bias, dense_small = call_k2(
        middle, cotangent, video_live, dense_in, dense_out, dense_in_bias, dense_out_bias, dense_gain, dense_shift
    )
    grad_tokens, part_frame, frame_small = call_k3(
        video, next_rows, grad_middle, packed, probs, first, mixed, frame_qkv, frame_out, frame_gain
    )
    grad_tokens = grad_tokens.reshape(batch, frames_local, T, width)
    grad_next = grad_tokens[:, :, patches]
    grad_class, rows, sum_bias, sum_gain, sum_shift = message_backward(
        kept, grad_next, message_proj, message_gain, message_qkv, message_out
    )
    grad_input = jnp.concatenate(
        [grad_tokens[:, :, :1] + grad_class[:, :, None, :], grad_tokens[:, :, 1:patches]], axis=2
    ).astype(bf)

    def total(value):
        share = lax.psum_scatter(value, "video", scatter_dimension=0, tiled=True)
        return lax.psum(share, "frame").astype(f32)

    grad_in = total(part_in.reshape(6, width, 4, 128).transpose(1, 2, 0, 3).reshape(width, hidden))
    grad_out = total(part_out.reshape(6, width, 4, 128).transpose(2, 0, 3, 1).reshape(hidden, width))
    part_frame = part_frame.reshape(6, width, 4, 128).transpose(1, 2, 0, 3).reshape(width, 4 * width)
    grad_frame = total(part_frame)
    vector = jnp.concatenate(
        [
            sum_bias,
            sum_gain,
            sum_shift,
            frame_small[0],
            frame_small[1],
            dense_small[1],
            dense_small[2],
            dense_small[0],
            part_bias.reshape(6, 4, 128).transpose(1, 0, 2).reshape(hidden),
        ]
    )
    vector = lax.psum(vector, ("video", "frame"))
    place = lax.axis_index("video")
    cut = width // groups

    def mine(start, length):
        return lax.dynamic_slice_in_dim(vector, start + place * (length // groups), length // groups)

    gathered = lax.all_gather(rows, ("video", "frame"), axis=0, tiled=True)

    def outer(left, first_column, last_column):
        part = lax.dynamic_slice_in_dim(gathered, left * width + place * cut, cut, axis=1)
        return weight_grad(part, gathered[:, first_column:last_column])

    return (
        output,
        grad_input,
        outer(0, 3 * width, 4 * width),
        mine(0, width),
        mine(width, width),
        mine(2 * width, width),
        outer(1, 4 * width, 7 * width),
        outer(2, 7 * width, 8 * width),
        mine(3 * width, width),
        mine(4 * width, width),
        grad_frame[:, : 3 * width],
        grad_frame[:, 3 * width :],
        mine(5 * width, width),
        mine(6 * width, width),
        grad_in,
        mine(8 * width, hidden),
        grad_out,
        mine(7 * width, width),
    )


def solution(mesh):
    in_specs = (
        P("video", "frame", None, None),
        P("video"),
        P("video", "frame", None, None),
        P(),
        P(),
        P(),
        P(),
        P(),
        P(),
        P(),
        P(),
        P(),
        P(),
        P(),
        P(),
        P(),
        P(),
        P(),
        P(),
    )
    out_specs = (
        P("video", "frame", None, None),
        P("video", "frame", None, None),
        P("video", None),
        P("video"),
        P("video"),
        P("video"),
        P("video", None),
        P("video", None),
        P("video"),
        P("video"),
        P("video", None),
        P("video", None),
        P("video"),
        P("video"),
        P("video", None),
        P("video"),
        P("video", None),
        P("video"),
    )
    return jax.shard_map(local, mesh=mesh, in_specs=in_specs, out_specs=out_specs, check_vma=False)
```

```python
import functools
import jax
import jax.numpy as jnp
from jax import lax
from jax.experimental import pallas as pl
from jax.experimental.pallas import tpu as pltpu
bf=jnp.bfloat16; f32=jnp.float32
EPS=1e-5
def dot(a,b,ca=1,cb=0): return lax.dot_general(a,b,(((ca,),(cb,)),((),())),preferred_element_type=f32)
FR=6; T=208; RR=FR*T; RP=1280; D=768
def k2(MB, mid, cot, live, din0,din1,din2,din3, do0,do1,do2,do3, bin_, bout, gain, shift,
       out_ref, gmid_ref, gdi_ref, gdo_ref, gbin_ref, small_ref,
       sec, G, act, dinn, oacc, gsec):
    j=pl.program_id(0)
    @pl.when(j==0)
    def _():
        ob=jnp.zeros((1,D),f32)
        sec[pl.ds(RR,RP-RR),:]=jnp.zeros((RP-RR,D),bf)
        G[pl.ds(RR,RP-RR),:]=jnp.zeros((RP-RR,D),bf)
        act[pl.ds(RR,RP-RR),:]=jnp.zeros((RP-RR,512),bf)
        dinn[pl.ds(RR,RP-RR),:]=jnp.zeros((RP-RR,512),bf)
        for f in range(FR):
            x=mid[f*T:(f+1)*T,:]
            mu=jnp.mean(x,-1,keepdims=True); c=x-mu
            inv=lax.rsqrt(jnp.mean(c*c,-1,keepdims=True)+EPS)
            sec[f*T:(f+1)*T,:]=(c*inv*gain[...]+shift[...]).astype(bf)
            g=cot[f,0].astype(f32)*live[f].astype(f32)
            g=jnp.concatenate([g,jnp.zeros((T-198,D),f32)],0)
            ob=ob+jnp.sum(g,0,keepdims=True)
            G[f*T:(f+1)*T,:]=g.astype(bf)
            oacc[f*T:(f+1)*T,:]=x+bout[...]
            gsec[f*T:(f+1)*T,:]=jnp.zeros((T,D),f32)
        small_ref[0:1,:]=ob
    din=jnp.concatenate([din0[...],din1[...],din2[...],din3[...]],1)
    do=jnp.concatenate([do0[...],do1[...],do2[...],do3[...]],0)
    b=jnp.concatenate([bin_[0:1,:],bin_[1:2,:],bin_[2:3,:],bin_[3:4,:]],1) if False else bin_[0]
    bsum=jnp.zeros((1,512),f32)
    for r in range(RR//MB):
        s=slice(r*MB,(r+1)*MB)
        inner=dot(sec[s,:],din)+b
        ga=dot(G[s,:],do,1,1)
        sg=0.5*jnp.tanh(0.851*inner)+0.5
        ac=inner*sg
        act[s,:]=ac.astype(bf)
        di=ga*(sg+1.702*ac*(1.0-sg))
        bsum=bsum+jnp.sum(di,0,keepdims=True)
        dinn[s,:]=di.astype(bf)
    gbin_ref[0]=bsum
    for r in range(RR//MB):
        s=slice(r*MB,(r+1)*MB)
        oacc[s,:]+=dot(act[s,:],do)
        gsec[s,:]+=dot(dinn[s,:],din,1,1)
    gdo_ref[0]=dot(G[...],act[...],0,0).astype(bf)
    gdi_ref[0]=dot(sec[...],dinn[...],0,0).astype(bf)
    @pl.when(j==pl.num_programs(0)-1)
    def _():
        gg=jnp.zeros((1,D),f32); gs=jnp.zeros((1,D),f32)
        for f in range(FR):
            s=slice(f*T,(f+1)*T)
            out_ref[f,0]=oacc[s,:][:198].astype(bf)
            x=mid[s,:]
            mu=jnp.mean(x,-1,keepdims=True); c=x-mu
            inv=lax.rsqrt(jnp.mean(c*c,-1,keepdims=True)+EPS)
            sc=c*inv
            go=gsec[s,:]
            gg=gg+jnp.sum(go*sc,0,keepdims=True); gs=gs+jnp.sum(go,0,keepdims=True)
            gsc=go*gain[...]
            gi=inv*(gsc-jnp.mean(gsc,-1,keepdims=True)-sc*jnp.mean(gsc*sc,-1,keepdims=True))
            gmid_ref[s,:]=G[s,:].astype(f32)+gi
        small_ref[1:2,:]=gg; small_ref[2:3,:]=gs
def call_k2(mid,cot,live,din,do,bin_,bout,gain,shift,MB=624):
    full=lambda *s: pl.BlockSpec(s,lambda j:(0,)*len(s))
    nq=din.shape[1]//512
    vm=pl.BlockSpec(memory_space=pltpu.VMEM)
    specs=[full(RR,D),full(FR,1,198,D),pl.BlockSpec(memory_space=pltpu.SMEM)]
    for q in range(4): specs.append(pl.BlockSpec((D,128),lambda j,q=q:(0,q*6+j)))
    for q in range(4): specs.append(pl.BlockSpec((128,D),lambda j,q=q:(q*6+j,0)))
    specs+= [pl.BlockSpec((1,1,512),lambda j:(j,0,0)),full(1,D),full(1,D),full(1,D)]
    b3=bin_.reshape(4,6,128).transpose(1,0,2).reshape(6,1,512)
    return pl.pallas_call(functools.partial(k2,MB),grid=(6,),in_specs=specs,
      out_specs=[full(FR,1,198,D),full(RR,D),pl.BlockSpec((1,D,512),lambda j:(j,0,0)),pl.BlockSpec((1,D,512),lambda j:(j,0,0)),pl.BlockSpec((1,1,512),lambda j:(j,0,0)),full(8,D)],
      out_shape=[jax.ShapeDtypeStruct((FR,1,198,D),bf),jax.ShapeDtypeStruct((RR,D),f32),jax.ShapeDtypeStruct((6,D,512),bf),jax.ShapeDtypeStruct((6,D,512),bf),jax.ShapeDtypeStruct((6,1,512),f32),jax.ShapeDtypeStruct((8,D),f32)],
      scratch_shapes=[pltpu.VMEM((RP,D),bf),pltpu.VMEM((RP,D),bf),pltpu.VMEM((RP,512),bf),pltpu.VMEM((RP,512),bf),pltpu.VMEM((RR,D),f32),pltpu.VMEM((RR,D),f32)],
      compiler_params=pltpu.CompilerParams(vmem_limit_bytes=61<<20,dimension_semantics=("arbitrary",)),
    )(mid,cot,live,din,din,din,din,do,do,do,do,b3,bout.reshape(1,D),gain.reshape(1,D),shift.reshape(1,D))
from jax.sharding import PartitionSpec as P
HEADS=12
HEAD_DIM=64
NEG=-1e30
VMEM_LIMIT=63<<20

def half_masks(rows):
    lane=lax.broadcasted_iota(jnp.int32,(rows,128),1)
    return lane<64
def k1(vid, mnext, wq, wk, wv, wo, gain, shift,
       qkv_ref, pt_ref, first_ref, mixed_ref, mid_ref, tok_ref):
    h=pl.program_id(0)
    @pl.when(h==0)
    def _():
        first_ref[pl.ds(RR,RP-RR),:]=jnp.zeros((RP-RR,D),bf)
        mixed_ref[pl.ds(RR,RP-RR),:]=jnp.zeros((RP-RR,D),bf)
        for f in range(FR):
            mid_ref[f*T+192:(f+1)*T,:]=jnp.zeros((T-192,D),f32)
            mid_ref[f*T:f*T+197,:]=vid[f,0].astype(f32)
            mid_ref[f*T+197:f*T+198,:]=mnext[f:f+1,:]
            x=mid_ref[f*T:(f+1)*T,:]
            tok_ref[f*T:(f+1)*T,:]=x.astype(bf)
            mu=jnp.mean(x,-1,keepdims=True); c=x-mu
            inv=lax.rsqrt(jnp.mean(c*c,-1,keepdims=True)+EPS)
            first_ref[f*T:(f+1)*T,:]=(c*inv*gain[...]+shift[...]).astype(bf)
    w=jnp.concatenate([wq[...],wk[...],wv[...]],1)
    qkv_ref[0,0:RR,:]=dot(first_ref[0:RR,:],w).astype(bf)
    qkv_ref[0,RR:RP,:]=jnp.zeros((RP-RR,384),bf)
    lo=half_masks(T)
    keep=lax.broadcasted_iota(jnp.int32,(16,T),0)<6
    zero=jnp.zeros((T,128),bf)
    for f in range(FR):
        s=slice(f*T,(f+1)*T)
        q=qkv_ref[0,s,0:128]*jnp.asarray(0.125,bf); k=qkv_ref[0,s,128:256]; v=qkv_ref[0,s,256:384]
        ps=[]; vs=[]
        for e in range(2):
            m=lo if e==0 else jnp.logical_not(lo)
            st=dot(k,jnp.where(m,q,zero),1,1)
            top=st[:192]; bot=jnp.where(keep,st[192:],NEG)
            mx=jnp.maximum(jnp.max(top,0,keepdims=True),jnp.max(bot,0,keepdims=True))
            top=jnp.exp(top-mx); bot=jnp.exp(bot-mx)
            tot=jnp.sum(top,0,keepdims=True)+jnp.sum(bot,0,keepdims=True)
            p=(jnp.concatenate([top,bot],0)*(1.0/tot)).astype(bf)
            pt_ref[0,f*2+e]=p
            ps.append(p); vs.append(jnp.where(m,v,zero))
        o=dot(jnp.concatenate(ps,0),jnp.concatenate(vs,0),0,0)
        mixed_ref[s,pl.ds(pl.multiple_of(h*128,128),128)]=o.astype(bf)
    @pl.when(h==5)
    def _():
        mid_ref[...]+=dot(mixed_ref[0:RR,:],wo[...])
def call_k1(video,mnext,qkv,wo,gain,shift):
    full=lambda *s: pl.BlockSpec(s,lambda j:(0,)*len(s))
    blk=lambda *s: pl.BlockSpec((1,)+s,lambda j:(j,)+(0,)*len(s))
    specs=[full(FR,1,197,D),full(FR,D)]+[pl.BlockSpec((D,128),lambda j,o=o:(0,o*6+j)) for o in range(3)]+[full(D,D),full(1,D),full(1,D)]
    return pl.pallas_call(k1,grid=(6,),in_specs=specs,
      out_specs=[blk(RP,384),blk(12,T,T),full(RP,D),full(RP,D),full(RR,D),full(RR,D)],
      out_shape=[jax.ShapeDtypeStruct((6,RP,384),bf),jax.ShapeDtypeStruct((6,12,T,T),bf),jax.ShapeDtypeStruct((RP,D),bf),jax.ShapeDtypeStruct((RP,D),bf),jax.ShapeDtypeStruct((RR,D),f32),jax.ShapeDtypeStruct((RR,D),bf)],
      compiler_params=pltpu.CompilerParams(vmem_limit_bytes=61<<20,dimension_semantics=("arbitrary",)),
    )(video,mnext,qkv,qkv,qkv,wo,gain.reshape(1,D),shift.reshape(1,D))
def k3(vid, mnext, gmid, qkv, pt, first, mixed, wq, wk, wv, wo, gain, shift,
       gtok_ref, gf_ref, small_ref, glow, dO, dpk, wqkv):
    h=pl.program_id(0)
    @pl.when(h==0)
    def _():
        glow[pl.ds(RR,RP-RR),:]=jnp.zeros((RP-RR,D),bf)
        dpk[:,pl.ds(RR,RP-RR),:]=jnp.zeros((6,RP-RR,384),bf)
        glow[0:RR,:]=gmid[...].astype(bf)
        d=dot(glow[0:RR,:],wo[...],1,1).astype(bf)
        for i in range(6): dO[i]=d[:,i*128:(i+1)*128]
    lo=half_masks(T)
    zero=jnp.zeros((T,128),bf)
    for f in range(FR):
        s=slice(f*T,(f+1)*T)
        q=qkv[0,s,0:128]; k=qkv[0,s,128:256]; v=qkv[0,s,256:384]
        do=dO[h,s,:]
        dss=[]; ks=[]; dk=0.; dv=0.
        for e in range(2):
            m=lo if e==0 else jnp.logical_not(lo)
            doe=jnp.where(m,do,zero)
            pb=pt[0,f*2+e]
            p=pb.astype(f32)
            dp=dot(v,doe,1,1)
            delta=jnp.sum(dp*p,0,keepdims=True)
            ds=(p*(dp-delta)).astype(bf)
            dk=dk+dot(ds,jnp.where(m,q,zero))
            dv=dv+dot(pb,doe)
            dss.append(ds); ks.append(jnp.where(m,k,zero))
        dq=dot(jnp.concatenate(dss,0),jnp.concatenate(ks,0),0,0)*0.125
        dpk[h,s,0:128]=dq.astype(bf)
        dpk[h,s,128:256]=(dk*0.125).astype(bf)
        dpk[h,s,256:384]=dv.astype(bf)
    for i in range(6):
        @pl.when(h==i)
        def _():
            wqkv[:,i*128:(i+1)*128]=wq[...]; wqkv[:,D+i*128:D+(i+1)*128]=wk[...]; wqkv[:,2*D+i*128:2*D+(i+1)*128]=wv[...]
            gf_ref[0,:,384:512]=dot(mixed[...],glow[:,i*128:(i+1)*128],0,0).astype(bf)
    gf_ref[0,:,0:384]=dot(first[...],dpk[h],0,0).astype(bf)
    @pl.when(h==5)
    def _():
        dx=jnp.concatenate([dpk[i,0:RR,g*128:(g+1)*128] for g in range(3) for i in range(6)],1)
        gtok_ref[...]=dot(dx,wqkv[...],1,1)
        gg=jnp.zeros((1,D),f32); gs=jnp.zeros((1,D),f32)
        for f in range(FR):
            s=slice(f*T,(f+1)*T)
            x=jnp.concatenate([vid[f,0].astype(f32),mnext[f:f+1,:],jnp.zeros((T-198,D),f32)],0)
            mu=jnp.mean(x,-1,keepdims=True); c=x-mu
            inv=lax.rsqrt(jnp.mean(c*c,-1,keepdims=True)+EPS)
            sc=c*inv
            go=gtok_ref[s,:]
            gg=gg+jnp.sum(go*sc,0,keepdims=True); gs=gs+jnp.sum(go,0,keepdims=True)
            gsc=go*gain[...]
            gi=inv*(gsc-jnp.mean(gsc,-1,keepdims=True)-sc*jnp.mean(gsc*sc,-1,keepdims=True))
            gtok_ref[s,:]=gmid[s,:]+gi
        small_ref[0:1,:]=gg; small_ref[1:2,:]=gs
def call_k3(video,mnext,gmid,qkvs,pt,first,mixed,qkv,wo,gain):
    full=lambda *s: pl.BlockSpec(s,lambda j:(0,)*len(s))
    blk=lambda *s: pl.BlockSpec((1,)+s,lambda j:(j,)+(0,)*len(s))
    specs=[full(FR,1,197,D),full(FR,D),full(RR,D),blk(RP,384),blk(12,T,T),full(RP,D),full(RP,D)]+[pl.BlockSpec((D,128),lambda j,o=o:(0,o*6+j)) for o in range(3)]+[full(D,D),full(1,D),full(1,D)]
    return pl.pallas_call(k3,grid=(6,),in_specs=specs,
      out_specs=[full(RR,D),blk(D,512),full(8,D)],
      out_shape=[jax.ShapeDtypeStruct((RR,D),f32),jax.ShapeDtypeStruct((6,D,512),bf),jax.ShapeDtypeStruct((8,D),f32)],
      scratch_shapes=[pltpu.VMEM((RP,D),bf),pltpu.VMEM((6,RR,128),bf),pltpu.VMEM((6,RP,384),bf),pltpu.VMEM((D,3*D),bf)],
      compiler_params=pltpu.CompilerParams(vmem_limit_bytes=61<<20,dimension_semantics=("arbitrary",)),
    )(video,mnext,gmid,qkvs,pt,first,mixed,qkv,qkv,qkv,wo,gain.reshape(1,D),gain.reshape(1,D))


UNITS = 18
DENSE_UNITS = 12
STEPS = 12
TICKS = 39
ROWS = 192


def add_norm_stats(values):
    mean = jnp.mean(values, -1, keepdims=True)
    center = values - mean
    inverse = lax.rsqrt(jnp.mean(center * center, -1, keepdims=True) + EPS)
    return center * inverse, inverse


def norm_back(grad, scaled, inverse, gain):
    grad_scaled = grad * gain
    return inverse * (
        grad_scaled
        - jnp.mean(grad_scaled, -1, keepdims=True)
        - scaled * jnp.mean(grad_scaled * scaled, -1, keepdims=True)
    )


def exchange(tick, where, U, RA, RB, RC, RD, RE, F, ssem, rsem, fsem, F_out):
    c, x, y, z0, z1, core, xn, yn, zn, zf = where

    def at(lag, body):
        s = tick - lag
        late = jnp.maximum(s - 13, 0)
        half = lax.div(late, 2)
        is_dense = jnp.logical_and(s >= 0, s < 12)
        is_frame = jnp.logical_and(jnp.logical_and(s >= 13, lax.rem(late, 2) == 0), half < 6)
        g = jnp.where(s < 12, jnp.maximum(s, 0), jnp.minimum(12 + half, UNITS - 1))

        @pl.when(jnp.logical_or(is_dense, is_frame))
        def _():
            body(g)

    def move(g, k, src, dst, target):
        return pltpu.make_async_remote_copy(
            src_ref=src,
            dst_ref=dst,
            send_sem=ssem.at[g, k],
            recv_sem=rsem.at[g, k],
            device_id=target,
            device_id_type=pl.DeviceIdType.MESH,
        )

    def a(g):
        return move(g, 0, U.at[lax.rem(g, 2), :, :, pl.ds(2 * (1 - c), 2)], RA.at[g], core)

    def b0(g):
        return move(g, 1, RA.at[g, :, 1 - x, 0], RB.at[g, 0], xn)

    def b1(g):
        return move(g, 2, RA.at[g, 1 - y, :, 1], RB.at[g, 1], yn)

    def c0(g):
        return move(g, 3, RB.at[g, 0, 1 - y], RC.at[g, 0], yn)

    def c1(g):
        return move(g, 4, RB.at[g, 1, 1 - x], RC.at[g, 1], xn)

    def d1(g):
        return move(g, 5, RC.at[g, 1 - z0], RD.at[g], zn)

    def d2(g):
        return move(g, 6, RD.at[g, pl.ds((1 - z1) * 96, 96)], RE.at[g], zf)

    def e2(g):
        piece = F.at[g, 2 * c + z0, pl.ds(z1 * 96, 96)]
        return move(g, 7, piece, piece, zf)

    def e1(g):
        piece = F.at[g, 2 * c + z0]
        return move(g, 8, piece, piece, zn)

    def last(g):
        piece = F.at[g, pl.ds(2 * c, 2)]
        return move(g, 9, piece, piece, core)

    def on_done(g):
        last(g).wait()
        pltpu.make_async_copy(F.at[g], F_out.at[g], fsem.at[g]).start()

    def on_last(g):
        e1(g).wait()
        last(g).start()

    def on_e1(g):
        e2(g).wait()
        e1(g).start()

    def on_e2(g):
        d2(g).wait()
        own = pl.ds(z1 * 96, 96)
        F[g, 2 * c + z0, own] = RE[g] + RD[g, own]
        e2(g).start()

    def on_d2(g):
        d1(g).wait()
        RD[g] = RD[g] + RC[g, z0]
        d2(g).start()

    def on_d1(g):
        c0(g).wait()
        c1(g).wait()
        RC[g, 0] = RC[g, 0] + RB[g, 0, y]
        RC[g, 1] = RC[g, 1] + RB[g, 1, x]
        d1(g).start()

    def on_c(g):
        b0(g).wait()
        b1(g).wait()
        RB[g, 0] = RB[g, 0] + RA[g, :, x, 0]
        RB[g, 1] = RB[g, 1] + RA[g, y, :, 1]
        c0(g).start()
        c1(g).start()

    def on_b(g):
        a(g).wait()
        RA[g] = RA[g] + U[lax.rem(g, 2), :, :, pl.ds(2 * c, 2)]
        b0(g).start()
        b1(g).start()

    def on_a(g):
        a(g).start()

    for lag, body in zip((0, 1, 3, 5, 7, 9, 11, 13, 15), (on_a, on_b, on_c, on_d1, on_d2, on_e2, on_e1, on_last, on_done)):
        at(lag, body)


def main_kernel(
    mid, cot, live, din0, din1, din2, din3, do0, do1, do2, do3, bin_, bout, gain2, shift2,
    qkv, pt, wq, wk, wv, first_hbm, mixed_hbm, wo_hbm, tok_hbm, mnext, gain1,
    out_hbm, gt_hbm, F_out, gbin_ref, small_ref, edge_ref,
    sec, G, act, dinn, oacc, gsec, CB, first, mixed, wo, dpk,
    U, RA, RB, RC, RD, RE, F, ssem, rsem, fsem, lsem,
):
    t = pl.program_id(0)
    f_at, v_at = lax.axis_index("frame"), lax.axis_index("video")
    c, z = lax.rem(f_at, 2), lax.div(f_at, 2)
    x, y = lax.rem(v_at, 2), lax.div(v_at, 2)
    z0, z1 = lax.rem(z, 2), lax.div(z, 2)
    core = (f_at + 1 - 2 * c, v_at)
    xn = (f_at, v_at + 1 - 2 * x)
    yn = (f_at, v_at + 2 - 4 * y)
    zn = (f_at + 2 - 4 * z0, v_at)
    zf = (f_at + 4 - 8 * z1, v_at)
    where = (c, x, y, z0, z1, core, xn, yn, zn, zf)

    def tick(n):
        exchange(n, where, U, RA, RB, RC, RD, RE, F, ssem, rsem, fsem, F_out)

    def fetch(k):
        src, dst = (
            (first_hbm, first),
            (mixed_hbm, mixed),
            (wo_hbm, wo),
            (tok_hbm, act.at[pl.ds(0, RR)]),
            (CB, out_hbm),
            (sec.at[pl.ds(0, RR)], gt_hbm),
            (cot, CB),
        )[k]
        return pltpu.make_async_copy(src, dst, lsem.at[k])

    tail = pl.ds(RR, RP - RR)

    @pl.when(t == 0)
    def _():
        fetch(6).start()
        barrier = pltpu.get_barrier_semaphore()
        for other in (core, xn, yn, zn, zf):
            pl.semaphore_signal(barrier, inc=1, device_id=other, device_id_type=pl.DeviceIdType.MESH)
        for k in range(3):
            fetch(k).start()
        sec[tail, :] = jnp.zeros((RP - RR, D), bf)
        G[tail, :] = jnp.zeros((RP - RR, D), bf)
        act[tail, :] = jnp.zeros((RP - RR, D), bf)
        dinn[tail, :] = jnp.zeros((RP - RR, 512), bf)
        dpk[tail, :] = jnp.zeros((RP - RR, 384), bf)
        small_ref[...] = jnp.zeros((8, D), f32)
        edge_ref[...] = jnp.zeros((16, D), f32)
        for f in range(FR):
            rows = slice(f * T, (f + 1) * T)
            values = mid[rows, :]
            scaled, _ = add_norm_stats(values)
            sec[rows, :] = (scaled * gain2[...] + shift2[...]).astype(bf)
            oacc[rows, :] = values + bout[...]
            gsec[rows, :] = jnp.zeros((T, D), f32)
        fetch(6).wait()
        total = jnp.zeros((1, D), f32)
        for f in range(FR):
            rows = slice(f * T, (f + 1) * T)
            grad = CB[f, 0].astype(f32) * live[f].astype(f32)
            total = total + jnp.sum(grad, 0, keepdims=True)
            G[rows, :] = jnp.concatenate([grad, jnp.zeros((T - 198, D), f32)], 0).astype(bf)
        small_ref[0:1, :] = total
        pl.semaphore_wait(barrier, 5)

    din = lambda: jnp.concatenate([din0[...], din1[...], din2[...], din3[...]], 1)
    dout = lambda: jnp.concatenate([do0[...], do1[...], do2[...], do3[...]], 0)

    def put(slot, index, block):
        q, b = index
        U[slot, q // 2, q % 2, b] = block.astype(bf)

    @pl.when(t < 6)
    def _():
        w_in, w_out = din(), dout()
        bias = bin_[0]
        sums = jnp.zeros((1, 512), f32)
        MB = 416
        for r in range(RR // MB):
            s = slice(r * MB, (r + 1) * MB)
            inner = dot(sec[s, :], w_in) + bias
            ga = dot(G[s, :], w_out, 1, 1)
            sg = 0.5 * jnp.tanh(0.851 * inner) + 0.5
            ac = inner * sg
            act[s, 0:512] = ac.astype(bf)
            di = ga * (sg + 1.702 * ac * (1.0 - sg))
            sums = sums + jnp.sum(di, 0, keepdims=True)
            dinn[s, :] = di.astype(bf)
        gbin_ref[0] = sums
        part = dot(G[...], act[:, 0:512], 0, 0)
        for q in range(4):
            for b in range(4):
                put(0, (q, b), part[b * ROWS : (b + 1) * ROWS, q * 128 : (q + 1) * 128])

    lo = lax.broadcasted_iota(jnp.int32, (T, 128), 1) < 64
    zero = jnp.zeros((T, 128), bf)
    head = jnp.maximum(t - 6, 0)
    lanes = pl.ds(pl.multiple_of(head * 128, 128), 128)

    def attend_back(frames):
        for f in frames:
            s = slice(f * T, (f + 1) * T)
            q, k, v = qkv[0, s, 0:128], qkv[0, s, 128:256], qkv[0, s, 256:384]
            do = G[s, lanes]
            dss, ks, dk, dv = [], [], 0.0, 0.0
            for e in range(2):
                m = lo if e == 0 else jnp.logical_not(lo)
                doe = jnp.where(m, do, zero)
                pb = pt[0, f * 2 + e]
                p = pb.astype(f32)
                dp = dot(v, doe, 1, 1)
                ds = (p * (dp - jnp.sum(dp * p, 0, keepdims=True))).astype(bf)
                dk = dk + dot(ds, jnp.where(m, q, zero))
                dv = dv + dot(pb, doe)
                dss.append(ds)
                ks.append(jnp.where(m, k, zero))
            dq = dot(jnp.concatenate(dss, 0), jnp.concatenate(ks, 0), 0, 0) * 0.125
            dpk[s, 0:128] = dq.astype(bf)
            dpk[s, 128:256] = (dk * 0.125).astype(bf)
            dpk[s, 256:384] = dv.astype(bf)

    @pl.when(t == 6)
    def _():
        gg = jnp.zeros((1, D), f32)
        gs = jnp.zeros((1, D), f32)
        for f in range(FR):
            s = slice(f * T, (f + 1) * T)
            CB[f, 0] = oacc[s, :][:198].astype(bf)
            scaled, inverse = add_norm_stats(mid[s, :])
            grad = gsec[s, :]
            gg = gg + jnp.sum(grad * scaled, 0, keepdims=True)
            gs = gs + jnp.sum(grad, 0, keepdims=True)
            total = G[s, :].astype(f32) + norm_back(grad, scaled, inverse, gain2[...])
            gsec[s, :] = total
            sec[s, :] = total.astype(bf)
            oacc[s, :] = jnp.zeros((T, D), f32)
        small_ref[1:2, :] = gg
        small_ref[2:3, :] = gs
        fetch(4).start()
        fetch(3).start()
        for k in range(3):
            fetch(k).wait()
        G[0:RR, :] = dot(sec[0:RR, :], wo[...], 1, 1).astype(bf)

    @pl.when(t >= 6)
    def _():
        attend_back(range(3))

    tick(2 * t)

    @pl.when(t < 6)
    def _():
        w_in, w_out = din(), dout()
        part = dot(sec[...], dinn[...], 0, 0)
        for q in range(4):
            for b in range(4):
                put(1, (q, b), part[q * ROWS : (q + 1) * ROWS, b * 128 : (b + 1) * 128])
        oacc[...] += dot(act[0:RR, 0:512], w_out)
        gsec[...] += dot(dinn[0:RR, :], w_in, 1, 1)

    @pl.when(t >= 6)
    def _():
        attend_back(range(3, 6))
        slot = lax.rem(head, 2)
        part = dot(first[...], dpk[...], 0, 0)
        for q in range(4):
            for b in range(3):
                put(slot, (q, b), part[q * ROWS : (q + 1) * ROWS, b * 128 : (b + 1) * 128])
        part = dot(mixed[...], sec[:, lanes], 0, 0)
        for q in range(4):
            put(slot, (q, 3), part[q * ROWS : (q + 1) * ROWS, :])

    tick(2 * t + 1)

    @pl.when(t >= 6)
    def _():
        w = jnp.concatenate([wq[...], wk[...], wv[...]], 1)
        oacc[...] += dot(dpk[0:RR, :], w, 1, 1)

    @pl.when(t == STEPS - 1)
    def _():
        fetch(3).wait()
        gg = jnp.zeros((1, D), f32)
        gs = jnp.zeros((1, D), f32)
        last_row = lax.broadcasted_iota(jnp.int32, (16, D), 0) == 5
        for f in range(FR):
            s = slice(f * T, (f + 1) * T)
            values = act[s, :].astype(f32)
            low = jnp.where(last_row, mnext[f : f + 1, :], values[192:])
            values = jnp.concatenate([values[:192], low], 0)
            scaled, inverse = add_norm_stats(values)
            grad = oacc[s, :]
            gg = gg + jnp.sum(grad * scaled, 0, keepdims=True)
            gs = gs + jnp.sum(grad, 0, keepdims=True)
            total = gsec[s, :] + norm_back(grad, scaled, inverse, gain1[...])
            sec[s, :] = total.astype(bf)
            edge_ref[f : f + 1, :] = total[0:1]
            edge_ref[8 + f : 9 + f, :] = total[197:198]
        small_ref[3:4, :] = gg
        small_ref[4:5, :] = gs
        fetch(5).start()

        def step(n, carry):
            tick(n)
            return carry

        lax.fori_loop(2 * STEPS, TICKS, step, 0)

        def finish(g, carry):
            pltpu.make_async_copy(F.at[g], F_out.at[g], fsem.at[g]).wait()
            return carry

        lax.fori_loop(0, UNITS, finish, 0)
        fetch(4).wait()
        fetch(5).wait()


def call_main(mid, cot, live, din, dout, bin_, bout, gain2, shift2, qkv, pt, wqkv, first, mixed, wo, tok, mnext, gain1):
    one = pl.Buffered(1)
    full = lambda *s: pl.BlockSpec(s, lambda t: (0,) * len(s), pipeline_mode=one)
    keep = lambda *s: pl.BlockSpec(s, lambda t: (0,) * len(s))
    hbm = pl.BlockSpec(memory_space=pl.ANY)
    dense = lambda t: jnp.minimum(t, 5)
    head = lambda t: jnp.maximum(t - 6, 0)
    specs = [full(RR, D), hbm, pl.BlockSpec(memory_space=pltpu.SMEM)]
    specs += [pl.BlockSpec((D, 128), lambda t, q=q: (0, q * 6 + dense(t))) for q in range(4)]
    specs += [pl.BlockSpec((128, D), lambda t, q=q: (q * 6 + dense(t), 0)) for q in range(4)]
    specs += [pl.BlockSpec((1, 1, 512), lambda t: (dense(t), 0, 0)), full(1, D), full(1, D), full(1, D)]
    specs += [pl.BlockSpec((1, RP, 384), lambda t: (head(t), 0, 0)), pl.BlockSpec((1, 12, T, T), lambda t: (head(t), 0, 0, 0))]
    specs += [pl.BlockSpec((D, 128), lambda t, o=o: (0, o * 6 + head(t))) for o in range(3)]
    specs += [hbm, hbm, hbm, hbm, full(6, D), full(1, D)]
    bias = bin_.reshape(4, 6, 128).transpose(1, 0, 2).reshape(6, 1, 512)
    row = lambda a: a.reshape(1, D)
    shape = jax.ShapeDtypeStruct
    dma = pltpu.SemaphoreType.DMA
    return pl.pallas_call(
        main_kernel,
        grid=(STEPS,),
        in_specs=specs,
        out_specs=[hbm, hbm, hbm, pl.BlockSpec((1, 1, 512), lambda t: (dense(t), 0, 0)), keep(8, D), keep(16, D)],
        out_shape=[
            shape((FR, 1, 198, D), bf),
            shape((RR, D), bf),
            shape((UNITS, 4, ROWS, 128), bf),
            shape((6, 1, 512), f32),
            shape((8, D), f32),
            shape((16, D), f32),
        ],
        scratch_shapes=[
            pltpu.VMEM((RP, D), bf),
            pltpu.VMEM((RP, D), bf),
            pltpu.VMEM((RP, D), bf),
            pltpu.VMEM((RP, 512), bf),
            pltpu.VMEM((RR, D), f32),
            pltpu.VMEM((RR, D), f32),
            pltpu.VMEM((FR, 1, 198, D), bf),
            pltpu.VMEM((RP, D), bf),
            pltpu.VMEM((RP, D), bf),
            pltpu.VMEM((D, D), bf),
            pltpu.VMEM((RP, 384), bf),
            pltpu.VMEM((2, 2, 2, 4, ROWS, 128), bf),
            pltpu.VMEM((UNITS, 2, 2, 2, ROWS, 128), bf),
            pltpu.VMEM((UNITS, 2, 2, ROWS, 128), bf),
            pltpu.VMEM((UNITS, 2, ROWS, 128), bf),
            pltpu.VMEM((UNITS, ROWS, 128), bf),
            pltpu.VMEM((UNITS, ROWS // 2, 128), bf),
            pltpu.VMEM((UNITS, 4, ROWS, 128), bf),
            dma((UNITS, 10)),
            dma((UNITS, 10)),
            dma((UNITS,)),
            dma((7,)),
        ],
        compiler_params=pltpu.CompilerParams(
            vmem_limit_bytes=VMEM_LIMIT,
            dimension_semantics=("arbitrary",),
            collective_id=1,
            has_side_effects=True,
        ),
    )(mid, cot, live, din, din, din, din, dout, dout, dout, dout, bias, row(bout), row(gain2), row(shift2),
      qkv, pt, wqkv, wqkv, wqkv, first, mixed, wo, tok, mnext, row(gain1))


def final_kernel(F, gt, edge, gclass, left, right, *outs):
    (gvid, gproj, gmqkv, gmout, gfqkv, gfout, gdin, gdout) = outs
    for f in range(FR):
        gvid[f, 0] = gt[f * T : (f + 1) * T, :][:197]
        gvid[f, 0, 0:1] = (edge[f : f + 1, :] + gclass[f : f + 1, :]).astype(bf)
    for j in range(6):
        for b in range(4):
            at = b * D + j * 128
            gdin[:, at : at + 128] = F[2 * j + 1, b].astype(f32)
            gdout[j * 128 : (j + 1) * 128, b * ROWS : (b + 1) * ROWS] = F[2 * j, b].astype(f32).T
            if b < 3:
                gfqkv[:, at : at + 128] = F[12 + j, b].astype(f32)
            else:
                gfout[:, j * 128 : (j + 1) * 128] = F[12 + j, b].astype(f32)
    gproj[...] = dot(left[0], right[:, 0:D], 0, 0)
    gmqkv[...] = dot(left[1], right[:, D : 4 * D], 0, 0)
    gmout[...] = dot(left[2], right[:, 4 * D : 5 * D], 0, 0)


def call_final(F, gt, edge, gclass, left, right):
    vm = pl.BlockSpec(memory_space=pltpu.VMEM)
    shape = jax.ShapeDtypeStruct
    cut = ROWS
    return pl.pallas_call(
        final_kernel,
        in_specs=[vm] * 6,
        out_specs=[vm] * 8,
        out_shape=[
            shape((FR, 1, 197, D), bf),
            shape((cut, D), f32),
            shape((cut, 3 * D), f32),
            shape((cut, D), f32),
            shape((cut, 3 * D), f32),
            shape((cut, D), f32),
            shape((cut, 4 * D), f32),
            shape((4 * cut, D), f32),
        ],
        compiler_params=pltpu.CompilerParams(vmem_limit_bytes=VMEM_LIMIT),
    )(F, gt, edge, gclass, left, right)


def column_sum(values):
    return jnp.sum(values.reshape(-1, values.shape[-1]), axis=0)


def matmul(left, right):
    return jnp.dot(left, right, preferred_element_type=f32)


def back_matmul(grad_low, weight):
    return lax.dot_general(grad_low, weight, (((grad_low.ndim - 1,), (1,)), ((), ())), preferred_element_type=f32)


def weight_grad(inputs_low, grad_low):
    left = inputs_low.reshape(-1, inputs_low.shape[-1])
    right = grad_low.reshape(-1, grad_low.shape[-1])
    return lax.dot_general(left, right, (((0,), (0,)), ((), ())), preferred_element_type=f32)


def norm_forward(values, gain, shift):
    center = values - jnp.mean(values, axis=-1, keepdims=True)
    inverse = lax.rsqrt(jnp.mean(center * center, axis=-1, keepdims=True) + EPS)
    scaled = center * inverse
    return (scaled * gain + shift, scaled, inverse)


def norm_backward(grad_out, scaled, inverse, gain):
    grad_scaled = grad_out * gain
    grad_in = inverse * (
        grad_scaled
        - jnp.mean(grad_scaled, axis=-1, keepdims=True)
        - scaled * jnp.mean(grad_scaled * scaled, axis=-1, keepdims=True)
    )
    return (grad_in, column_sum(grad_out * scaled), column_sum(grad_out))


def split_heads(values):
    return values.reshape(values.shape[:-1] + (HEADS, HEAD_DIM))


def attend_forward(query_rows, key_rows, value_rows):
    scores = jnp.einsum("bqhd,bkhd->bhqk", query_rows, key_rows, preferred_element_type=f32) * 0.125
    largest = jnp.max(scores, axis=-1, keepdims=True)
    raised = jnp.exp(scores - largest)
    total = jnp.sum(raised, axis=-1, keepdims=True)
    probs_low = (raised / total).astype(bf)
    mixed = jnp.einsum("bhqk,bkhd->bqhd", probs_low, value_rows, preferred_element_type=f32)
    return (mixed, largest + jnp.log(total))


def attend_backward(query_rows, key_rows, value_rows, log_total, grad_mixed):
    scores = jnp.einsum("bqhd,bkhd->bhqk", query_rows, key_rows, preferred_element_type=f32) * 0.125
    probs = jnp.exp(scores - log_total)
    grad_probs = jnp.einsum("bqhd,bkhd->bhqk", grad_mixed, value_rows, preferred_element_type=f32)
    grad_scores = probs * (grad_probs - jnp.sum(grad_probs * probs, axis=-1, keepdims=True))
    grad_low = grad_scores.astype(bf)
    grad_query = jnp.einsum("bhqk,bkhd->bqhd", grad_low, key_rows, preferred_element_type=f32) * 0.125
    grad_key = jnp.einsum("bhqk,bqhd->bkhd", grad_low, query_rows, preferred_element_type=f32) * 0.125
    grad_value = jnp.einsum("bhqk,bqhd->bkhd", probs.astype(bf), grad_mixed, preferred_element_type=f32)
    return (grad_query, grad_key, grad_value)


def message_forward(video, message_proj, message_bias, message_gain, message_shift, message_qkv, message_out):
    width = video.shape[-1]
    batch, frames_local = video.shape[:2]
    class_rows = video[:, :, 0, :]
    message = (matmul(class_rows, message_proj) + message_bias).astype(bf)
    message_wide = message.astype(f32)
    normed_own, scaled_own, inverse_own = norm_forward(message_wide, message_gain, message_shift)
    normed_low = normed_own.astype(bf)
    everyone = lax.all_gather(message, "frame", axis=1, tiled=True)
    normed_all = norm_forward(everyone.astype(f32), message_gain, message_shift)[0]
    key_value = matmul(normed_all.astype(bf), message_qkv[:, width:]).astype(bf)
    query = split_heads(matmul(normed_low, message_qkv[:, :width]).astype(bf))
    key = split_heads(key_value[..., :width])
    value = split_heads(key_value[..., width:])
    mixed, total = attend_forward(query, key, value)
    mixed_low = mixed.reshape(batch, frames_local, width).astype(bf)
    message_next = message_wide + matmul(mixed_low, message_out)
    return message_next, (class_rows, normed_low, scaled_own, inverse_own, query, key, value, mixed_low, total)


def message_backward(kept, grad_next, message_proj, message_gain, message_qkv, message_out):
    class_rows, normed_low, scaled_own, inverse_own, query, key, value, mixed_low, total = kept
    batch, frames_local, width = grad_next.shape
    frames_all = key.shape[1]
    grad_next_low = grad_next.astype(bf)
    grad_mixed = split_heads(back_matmul(grad_next_low, message_out).astype(bf))
    grad_q, grad_k, grad_v = attend_backward(query, key, value, total, grad_mixed)
    key_value_grad = jnp.concatenate(
        [grad_k.reshape(batch, frames_all, width), grad_v.reshape(batch, frames_all, width)], axis=-1
    )
    own = lax.psum_scatter(key_value_grad.astype(bf), "frame", scatter_dimension=1, tiled=True)
    packed = jnp.concatenate([grad_q.reshape(batch, frames_local, width).astype(bf), own], axis=-1)
    grad_in, grad_gain, grad_shift = norm_backward(
        back_matmul(packed, message_qkv), scaled_own, inverse_own, message_gain
    )
    grad_message = grad_next + grad_in
    grad_message_low = grad_message.astype(bf)
    grad_class = back_matmul(grad_message_low, message_proj)
    rows = jnp.concatenate([class_rows, normed_low, mixed_low, grad_message_low, packed, grad_next_low], axis=-1)
    rows = rows.reshape(batch * frames_local, -1)
    return grad_class, rows, column_sum(grad_message), grad_gain, grad_shift


def reduced_inside(
    video, video_live, cotangent, message_proj, message_gain, message_qkv, message_out, frame_gain, frame_qkv,
    frame_out, dense_gain, dense_shift, dense_in, dense_in_bias, dense_out, dense_out_bias,
    next_rows, kept, packed, probs, first, mixed, middle, tokens,
):
    batch, frames_local, patches, width = video.shape
    hidden = dense_in.shape[1]
    groups = lax.axis_size("video")
    output, grad_rows, reduced, part_bias, small, edge = call_main(
        middle, cotangent, video_live, dense_in, dense_out, dense_in_bias, dense_out_bias, dense_gain, dense_shift,
        packed, probs, frame_qkv, first, mixed, frame_out, tokens, next_rows, frame_gain,
    )
    grad_next = edge[8 : 8 + batch].reshape(batch, frames_local, width)
    grad_class, rows, sum_bias, sum_gain, sum_shift = message_backward(
        kept, grad_next, message_proj, message_gain, message_qkv, message_out
    )
    vector = jnp.concatenate(
        [sum_bias, sum_gain, sum_shift, small[3], small[4], small[1], small[2], small[0],
         part_bias.reshape(6, 4, 128).transpose(1, 0, 2).reshape(hidden)]
    )
    vector = lax.psum(vector, ("video", "frame"))
    place = lax.axis_index("video")
    cut = width // groups

    def mine(start, length):
        return lax.dynamic_slice_in_dim(vector, start + place * (length // groups), length // groups)

    gathered = lax.all_gather(rows, ("video", "frame"), axis=0, tiled=True)
    left = lax.dynamic_slice_in_dim(gathered[:, : 3 * width].reshape(-1, 3, width), place * cut, cut, axis=2)
    grad_input, g_proj, g_mqkv, g_mout, g_fqkv, g_fout, g_in, g_out = call_final(
        reduced, grad_rows, edge, grad_class.reshape(batch, width), left.transpose(1, 0, 2), gathered[:, 3 * width :]
    )
    return (
        output, grad_input, g_proj, mine(0, width), mine(width, width), mine(2 * width, width), g_mqkv, g_mout,
        mine(3 * width, width), mine(4 * width, width), g_fqkv, g_fout, mine(5 * width, width), mine(6 * width, width),
        g_in, mine(8 * width, hidden), g_out, mine(7 * width, width),
    )


def local(
    video,
    video_live,
    cotangent,
    message_proj,
    message_bias,
    message_gain,
    message_shift,
    message_qkv,
    message_out,
    frame_gain,
    frame_shift,
    frame_qkv,
    frame_out,
    dense_gain,
    dense_shift,
    dense_in,
    dense_in_bias,
    dense_out,
    dense_out_bias,
):
    batch, frames_local, patches, width = video.shape
    hidden = dense_in.shape[1]
    groups = lax.axis_size("video")
    message_next, kept = message_forward(
        video, message_proj, message_bias, message_gain, message_shift, message_qkv, message_out
    )
    next_rows = message_next.reshape(batch * frames_local, width)
    packed, probs, first, mixed, middle, tokens = call_k1(video, next_rows, frame_qkv, frame_out, frame_gain, frame_shift)
    if (lax.axis_size("frame"), groups) == (8, 4):
        return reduced_inside(
            video, video_live, cotangent, message_proj, message_gain, message_qkv, message_out, frame_gain, frame_qkv,
            frame_out, dense_gain, dense_shift, dense_in, dense_in_bias, dense_out, dense_out_bias,
            next_rows, kept, packed, probs, first, mixed, middle, tokens,
        )
    output, grad_middle, part_in, part_out, part_bias, dense_small = call_k2(
        middle, cotangent, video_live, dense_in, dense_out, dense_in_bias, dense_out_bias, dense_gain, dense_shift
    )
    grad_tokens, part_frame, frame_small = call_k3(
        video, next_rows, grad_middle, packed, probs, first, mixed, frame_qkv, frame_out, frame_gain
    )
    grad_tokens = grad_tokens.reshape(batch, frames_local, T, width)
    grad_next = grad_tokens[:, :, patches]
    grad_class, rows, sum_bias, sum_gain, sum_shift = message_backward(
        kept, grad_next, message_proj, message_gain, message_qkv, message_out
    )
    grad_input = jnp.concatenate(
        [grad_tokens[:, :, :1] + grad_class[:, :, None, :], grad_tokens[:, :, 1:patches]], axis=2
    ).astype(bf)

    def total(value):
        share = lax.psum_scatter(value, "video", scatter_dimension=0, tiled=True)
        return lax.psum(share, "frame").astype(f32)

    grad_in = total(part_in.reshape(6, width, 4, 128).transpose(1, 2, 0, 3).reshape(width, hidden))
    grad_out = total(part_out.reshape(6, width, 4, 128).transpose(2, 0, 3, 1).reshape(hidden, width))
    part_frame = part_frame.reshape(6, width, 4, 128).transpose(1, 2, 0, 3).reshape(width, 4 * width)
    grad_frame = total(part_frame)
    vector = jnp.concatenate(
        [
            sum_bias,
            sum_gain,
            sum_shift,
            frame_small[0],
            frame_small[1],
            dense_small[1],
            dense_small[2],
            dense_small[0],
            part_bias.reshape(6, 4, 128).transpose(1, 0, 2).reshape(hidden),
        ]
    )
    vector = lax.psum(vector, ("video", "frame"))
    place = lax.axis_index("video")
    cut = width // groups

    def mine(start, length):
        return lax.dynamic_slice_in_dim(vector, start + place * (length // groups), length // groups)

    gathered = lax.all_gather(rows, ("video", "frame"), axis=0, tiled=True)

    def outer(left, first_column, last_column):
        part = lax.dynamic_slice_in_dim(gathered, left * width + place * cut, cut, axis=1)
        return weight_grad(part, gathered[:, first_column:last_column])

    return (
        output,
        grad_input,
        outer(0, 3 * width, 4 * width),
        mine(0, width),
        mine(width, width),
        mine(2 * width, width),
        outer(1, 4 * width, 7 * width),
        outer(2, 7 * width, 8 * width),
        mine(3 * width, width),
        mine(4 * width, width),
        grad_frame[:, : 3 * width],
        grad_frame[:, 3 * width :],
        mine(5 * width, width),
        mine(6 * width, width),
        grad_in,
        mine(8 * width, hidden),
        grad_out,
        mine(7 * width, width),
    )


def solution(mesh):
    in_specs = (
        P("video", "frame", None, None),
        P("video"),
        P("video", "frame", None, None),
        P(),
        P(),
        P(),
        P(),
        P(),
        P(),
        P(),
        P(),
        P(),
        P(),
        P(),
        P(),
        P(),
        P(),
        P(),
        P(),
    )
    out_specs = (
        P("video", "frame", None, None),
        P("video", "frame", None, None),
        P("video", None),
        P("video"),
        P("video"),
        P("video"),
        P("video", None),
        P("video", None),
        P("video"),
        P("video"),
        P("video", None),
        P("video", None),
        P("video"),
        P("video"),
        P("video", None),
        P("video"),
        P("video", None),
        P("video"),
    )
    return jax.shard_map(local, mesh=mesh, in_specs=in_specs, out_specs=out_specs, check_vma=False)
```

```python
import functools
import jax
import jax.numpy as jnp
from jax import lax
from jax.experimental import pallas as pl
from jax.experimental.pallas import tpu as pltpu
bf=jnp.bfloat16; f32=jnp.float32
EPS=1e-5
def dot(a,b,ca=1,cb=0): return lax.dot_general(a,b,(((ca,),(cb,)),((),())),preferred_element_type=f32)
FR=6; T=208; RR=FR*T; RP=1280; D=768
def k2(MB, mid, cot, live, din0,din1,din2,din3, do0,do1,do2,do3, bin_, bout, gain, shift,
       out_ref, gmid_ref, gdi_ref, gdo_ref, gbin_ref, small_ref,
       sec, G, act, dinn, oacc, gsec):
    j=pl.program_id(0)
    @pl.when(j==0)
    def _():
        ob=jnp.zeros((1,D),f32)
        sec[pl.ds(RR,RP-RR),:]=jnp.zeros((RP-RR,D),bf)
        G[pl.ds(RR,RP-RR),:]=jnp.zeros((RP-RR,D),bf)
        act[pl.ds(RR,RP-RR),:]=jnp.zeros((RP-RR,512),bf)
        dinn[pl.ds(RR,RP-RR),:]=jnp.zeros((RP-RR,512),bf)
        for f in range(FR):
            x=mid[f*T:(f+1)*T,:]
            mu=jnp.mean(x,-1,keepdims=True); c=x-mu
            inv=lax.rsqrt(jnp.mean(c*c,-1,keepdims=True)+EPS)
            sec[f*T:(f+1)*T,:]=(c*inv*gain[...]+shift[...]).astype(bf)
            g=cot[f,0].astype(f32)*live[f].astype(f32)
            g=jnp.concatenate([g,jnp.zeros((T-198,D),f32)],0)
            ob=ob+jnp.sum(g,0,keepdims=True)
            G[f*T:(f+1)*T,:]=g.astype(bf)
            oacc[f*T:(f+1)*T,:]=x+bout[...]
            gsec[f*T:(f+1)*T,:]=jnp.zeros((T,D),f32)
        small_ref[0:1,:]=ob
    din=jnp.concatenate([din0[...],din1[...],din2[...],din3[...]],1)
    do=jnp.concatenate([do0[...],do1[...],do2[...],do3[...]],0)
    b=jnp.concatenate([bin_[0:1,:],bin_[1:2,:],bin_[2:3,:],bin_[3:4,:]],1) if False else bin_[0]
    bsum=jnp.zeros((1,512),f32)
    for r in range(RR//MB):
        s=slice(r*MB,(r+1)*MB)
        inner=dot(sec[s,:],din)+b
        ga=dot(G[s,:],do,1,1)
        sg=0.5*jnp.tanh(0.851*inner)+0.5
        ac=inner*sg
        act[s,:]=ac.astype(bf)
        di=ga*(sg+1.702*ac*(1.0-sg))
        bsum=bsum+jnp.sum(di,0,keepdims=True)
        dinn[s,:]=di.astype(bf)
    gbin_ref[0]=bsum
    for r in range(RR//MB):
        s=slice(r*MB,(r+1)*MB)
        oacc[s,:]+=dot(act[s,:],do)
        gsec[s,:]+=dot(dinn[s,:],din,1,1)
    gdo_ref[0]=dot(G[...],act[...],0,0).astype(bf)
    gdi_ref[0]=dot(sec[...],dinn[...],0,0).astype(bf)
    @pl.when(j==pl.num_programs(0)-1)
    def _():
        gg=jnp.zeros((1,D),f32); gs=jnp.zeros((1,D),f32)
        for f in range(FR):
            s=slice(f*T,(f+1)*T)
            out_ref[f,0]=oacc[s,:][:198].astype(bf)
            x=mid[s,:]
            mu=jnp.mean(x,-1,keepdims=True); c=x-mu
            inv=lax.rsqrt(jnp.mean(c*c,-1,keepdims=True)+EPS)
            sc=c*inv
            go=gsec[s,:]
            gg=gg+jnp.sum(go*sc,0,keepdims=True); gs=gs+jnp.sum(go,0,keepdims=True)
            gsc=go*gain[...]
            gi=inv*(gsc-jnp.mean(gsc,-1,keepdims=True)-sc*jnp.mean(gsc*sc,-1,keepdims=True))
            gmid_ref[s,:]=G[s,:].astype(f32)+gi
        small_ref[1:2,:]=gg; small_ref[2:3,:]=gs
def call_k2(mid,cot,live,din,do,bin_,bout,gain,shift,MB=624):
    full=lambda *s: pl.BlockSpec(s,lambda j:(0,)*len(s))
    nq=din.shape[1]//512
    vm=pl.BlockSpec(memory_space=pltpu.VMEM)
    specs=[full(RR,D),full(FR,1,198,D),pl.BlockSpec(memory_space=pltpu.SMEM)]
    for q in range(4): specs.append(pl.BlockSpec((D,128),lambda j,q=q:(0,q*6+j)))
    for q in range(4): specs.append(pl.BlockSpec((128,D),lambda j,q=q:(q*6+j,0)))
    specs+= [pl.BlockSpec((1,1,512),lambda j:(j,0,0)),full(1,D),full(1,D),full(1,D)]
    b3=bin_.reshape(4,6,128).transpose(1,0,2).reshape(6,1,512)
    return pl.pallas_call(functools.partial(k2,MB),grid=(6,),in_specs=specs,
      out_specs=[full(FR,1,198,D),full(RR,D),pl.BlockSpec((1,D,512),lambda j:(j,0,0)),pl.BlockSpec((1,D,512),lambda j:(j,0,0)),pl.BlockSpec((1,1,512),lambda j:(j,0,0)),full(8,D)],
      out_shape=[jax.ShapeDtypeStruct((FR,1,198,D),bf),jax.ShapeDtypeStruct((RR,D),f32),jax.ShapeDtypeStruct((6,D,512),bf),jax.ShapeDtypeStruct((6,D,512),bf),jax.ShapeDtypeStruct((6,1,512),f32),jax.ShapeDtypeStruct((8,D),f32)],
      scratch_shapes=[pltpu.VMEM((RP,D),bf),pltpu.VMEM((RP,D),bf),pltpu.VMEM((RP,512),bf),pltpu.VMEM((RP,512),bf),pltpu.VMEM((RR,D),f32),pltpu.VMEM((RR,D),f32)],
      compiler_params=pltpu.CompilerParams(vmem_limit_bytes=61<<20,dimension_semantics=("arbitrary",)),
    )(mid,cot,live,din,din,din,din,do,do,do,do,b3,bout.reshape(1,D),gain.reshape(1,D),shift.reshape(1,D))
from jax.sharding import PartitionSpec as P
HEADS=12
HEAD_DIM=64
NEG=-1e30
VMEM_LIMIT=63<<20

def half_masks(rows):
    lane=lax.broadcasted_iota(jnp.int32,(rows,128),1)
    return lane<64
def attend_frames(h,wq,wk,wv,wo,qkv_ref,pt_ref,first_ref,mixed_ref,mid_ref):
    w=jnp.concatenate([wq[...],wk[...],wv[...]],1)
    qkv_ref[0,0:RR,:]=dot(first_ref[0:RR,:],w).astype(bf)
    qkv_ref[0,RR:RP,:]=jnp.zeros((RP-RR,384),bf)
    lo=half_masks(T)
    keep=lax.broadcasted_iota(jnp.int32,(16,T),0)<6
    zero=jnp.zeros((T,128),bf)
    for f in range(FR):
        s=slice(f*T,(f+1)*T)
        q=qkv_ref[0,s,0:128]*jnp.asarray(0.125,bf); k=qkv_ref[0,s,128:256]; v=qkv_ref[0,s,256:384]
        ps=[]; vs=[]
        for e in range(2):
            m=lo if e==0 else jnp.logical_not(lo)
            st=dot(k,jnp.where(m,q,zero),1,1)
            top=st[:192]; bot=jnp.where(keep,st[192:],NEG)
            mx=jnp.maximum(jnp.max(top,0,keepdims=True),jnp.max(bot,0,keepdims=True))
            top=jnp.exp(top-mx); bot=jnp.exp(bot-mx)
            tot=jnp.sum(top,0,keepdims=True)+jnp.sum(bot,0,keepdims=True)
            p=(jnp.concatenate([top,bot],0)*(1.0/tot)).astype(bf)
            pt_ref[0,f*2+e]=p
            ps.append(p); vs.append(jnp.where(m,v,zero))
        o=dot(jnp.concatenate(ps,0),jnp.concatenate(vs,0),0,0)
        mixed_ref[s,pl.ds(pl.multiple_of(h*128,128),128)]=o.astype(bf)
    @pl.when(h==5)
    def _():
        mid_ref[...]+=dot(mixed_ref[0:RR,:],wo[...])
def k1(vid, mnext, wq, wk, wv, wo, gain, shift,
       qkv_ref, pt_ref, first_ref, mixed_ref, mid_ref, tok_ref):
    h=pl.program_id(0)
    @pl.when(h==0)
    def _():
        first_ref[pl.ds(RR,RP-RR),:]=jnp.zeros((RP-RR,D),bf)
        mixed_ref[pl.ds(RR,RP-RR),:]=jnp.zeros((RP-RR,D),bf)
        for f in range(FR):
            mid_ref[f*T+192:(f+1)*T,:]=jnp.zeros((T-192,D),f32)
            mid_ref[f*T:f*T+197,:]=vid[f,0].astype(f32)
            mid_ref[f*T+197:f*T+198,:]=mnext[f:f+1,:]
            x=mid_ref[f*T:(f+1)*T,:]
            tok_ref[f*T:(f+1)*T,:]=x.astype(bf)
            mu=jnp.mean(x,-1,keepdims=True); c=x-mu
            inv=lax.rsqrt(jnp.mean(c*c,-1,keepdims=True)+EPS)
            first_ref[f*T:(f+1)*T,:]=(c*inv*gain[...]+shift[...]).astype(bf)
    attend_frames(h,wq,wk,wv,wo,qkv_ref,pt_ref,first_ref,mixed_ref,mid_ref)
def call_k1(video,mnext,qkv,wo,gain,shift):
    full=lambda *s: pl.BlockSpec(s,lambda j:(0,)*len(s))
    blk=lambda *s: pl.BlockSpec((1,)+s,lambda j:(j,)+(0,)*len(s))
    specs=[full(FR,1,197,D),full(FR,D)]+[pl.BlockSpec((D,128),lambda j,o=o:(0,o*6+j)) for o in range(3)]+[full(D,D),full(1,D),full(1,D)]
    return pl.pallas_call(k1,grid=(6,),in_specs=specs,
      out_specs=[blk(RP,384),blk(12,T,T),full(RP,D),full(RP,D),full(RR,D),full(RR,D)],
      out_shape=[jax.ShapeDtypeStruct((6,RP,384),bf),jax.ShapeDtypeStruct((6,12,T,T),bf),jax.ShapeDtypeStruct((RP,D),bf),jax.ShapeDtypeStruct((RP,D),bf),jax.ShapeDtypeStruct((RR,D),f32),jax.ShapeDtypeStruct((RR,D),bf)],
      compiler_params=pltpu.CompilerParams(vmem_limit_bytes=61<<20,dimension_semantics=("arbitrary",)),
    )(video,mnext,qkv,qkv,qkv,wo,gain.reshape(1,D),shift.reshape(1,D))
def k3(vid, mnext, gmid, qkv, pt, first, mixed, wq, wk, wv, wo, gain, shift,
       gtok_ref, gf_ref, small_ref, glow, dO, dpk, wqkv):
    h=pl.program_id(0)
    @pl.when(h==0)
    def _():
        glow[pl.ds(RR,RP-RR),:]=jnp.zeros((RP-RR,D),bf)
        dpk[:,pl.ds(RR,RP-RR),:]=jnp.zeros((6,RP-RR,384),bf)
        glow[0:RR,:]=gmid[...].astype(bf)
        d=dot(glow[0:RR,:],wo[...],1,1).astype(bf)
        for i in range(6): dO[i]=d[:,i*128:(i+1)*128]
    lo=half_masks(T)
    zero=jnp.zeros((T,128),bf)
    for f in range(FR):
        s=slice(f*T,(f+1)*T)
        q=qkv[0,s,0:128]; k=qkv[0,s,128:256]; v=qkv[0,s,256:384]
        do=dO[h,s,:]
        dss=[]; ks=[]; dk=0.; dv=0.
        for e in range(2):
            m=lo if e==0 else jnp.logical_not(lo)
            doe=jnp.where(m,do,zero)
            pb=pt[0,f*2+e]
            p=pb.astype(f32)
            dp=dot(v,doe,1,1)
            delta=jnp.sum(dp*p,0,keepdims=True)
            ds=(p*(dp-delta)).astype(bf)
            dk=dk+dot(ds,jnp.where(m,q,zero))
            dv=dv+dot(pb,doe)
            dss.append(ds); ks.append(jnp.where(m,k,zero))
        dq=dot(jnp.concatenate(dss,0),jnp.concatenate(ks,0),0,0)*0.125
        dpk[h,s,0:128]=dq.astype(bf)
        dpk[h,s,128:256]=(dk*0.125).astype(bf)
        dpk[h,s,256:384]=dv.astype(bf)
    for i in range(6):
        @pl.when(h==i)
        def _():
            wqkv[:,i*128:(i+1)*128]=wq[...]; wqkv[:,D+i*128:D+(i+1)*128]=wk[...]; wqkv[:,2*D+i*128:2*D+(i+1)*128]=wv[...]
            gf_ref[0,:,384:512]=dot(mixed[...],glow[:,i*128:(i+1)*128],0,0).astype(bf)
    gf_ref[0,:,0:384]=dot(first[...],dpk[h],0,0).astype(bf)
    @pl.when(h==5)
    def _():
        dx=jnp.concatenate([dpk[i,0:RR,g*128:(g+1)*128] for g in range(3) for i in range(6)],1)
        gtok_ref[...]=dot(dx,wqkv[...],1,1)
        gg=jnp.zeros((1,D),f32); gs=jnp.zeros((1,D),f32)
        for f in range(FR):
            s=slice(f*T,(f+1)*T)
            x=jnp.concatenate([vid[f,0].astype(f32),mnext[f:f+1,:],jnp.zeros((T-198,D),f32)],0)
            mu=jnp.mean(x,-1,keepdims=True); c=x-mu
            inv=lax.rsqrt(jnp.mean(c*c,-1,keepdims=True)+EPS)
            sc=c*inv
            go=gtok_ref[s,:]
            gg=gg+jnp.sum(go*sc,0,keepdims=True); gs=gs+jnp.sum(go,0,keepdims=True)
            gsc=go*gain[...]
            gi=inv*(gsc-jnp.mean(gsc,-1,keepdims=True)-sc*jnp.mean(gsc*sc,-1,keepdims=True))
            gtok_ref[s,:]=gmid[s,:]+gi
        small_ref[0:1,:]=gg; small_ref[1:2,:]=gs
def call_k3(video,mnext,gmid,qkvs,pt,first,mixed,qkv,wo,gain):
    full=lambda *s: pl.BlockSpec(s,lambda j:(0,)*len(s))
    blk=lambda *s: pl.BlockSpec((1,)+s,lambda j:(j,)+(0,)*len(s))
    specs=[full(FR,1,197,D),full(FR,D),full(RR,D),blk(RP,384),blk(12,T,T),full(RP,D),full(RP,D)]+[pl.BlockSpec((D,128),lambda j,o=o:(0,o*6+j)) for o in range(3)]+[full(D,D),full(1,D),full(1,D)]
    return pl.pallas_call(k3,grid=(6,),in_specs=specs,
      out_specs=[full(RR,D),blk(D,512),full(8,D)],
      out_shape=[jax.ShapeDtypeStruct((RR,D),f32),jax.ShapeDtypeStruct((6,D,512),bf),jax.ShapeDtypeStruct((8,D),f32)],
      scratch_shapes=[pltpu.VMEM((RP,D),bf),pltpu.VMEM((6,RR,128),bf),pltpu.VMEM((6,RP,384),bf),pltpu.VMEM((D,3*D),bf)],
      compiler_params=pltpu.CompilerParams(vmem_limit_bytes=61<<20,dimension_semantics=("arbitrary",)),
    )(video,mnext,gmid,qkvs,pt,first,mixed,qkv,qkv,qkv,wo,gain.reshape(1,D),gain.reshape(1,D))


UNITS = 18
DENSE_UNITS = 12
STEPS = 12
TICKS = 39
ROWS = 192


def add_norm_stats(values):
    mean = jnp.mean(values, -1, keepdims=True)
    center = values - mean
    inverse = lax.rsqrt(jnp.mean(center * center, -1, keepdims=True) + EPS)
    return center * inverse, inverse


def norm_back(grad, scaled, inverse, gain):
    grad_scaled = grad * gain
    return inverse * (
        grad_scaled
        - jnp.mean(grad_scaled, -1, keepdims=True)
        - scaled * jnp.mean(grad_scaled * scaled, -1, keepdims=True)
    )


def pack_rows(values):
    return jnp.concatenate([values[:, : D // 2], values[:, D // 2 :]], 0).astype(bf)


def unpack_rows(blocks):
    wide = blocks.astype(f32)
    rows = jnp.concatenate([wide[:, :8], wide[:, 8:]], 2)
    return rows.reshape(rows.shape[0] * 8, D)


def gather_moves(B, ssem, rsem, f_at, v_at):
    me = v_at * 8 + f_at

    def move(k, src, target):
        return pltpu.make_async_remote_copy(
            src_ref=src,
            dst_ref=src,
            send_sem=ssem.at[k],
            recv_sem=rsem.at[k],
            device_id=target,
            device_id_type=pl.DeviceIdType.MESH,
        )

    def near():
        return [move(i - 1, B.at[me], (lax.rem(f_at + i, 8), v_at)) for i in range(1, 8)]

    def far():
        x, y = lax.rem(v_at, 2), lax.div(v_at, 2)
        block = B.at[pl.ds(v_at * 8, 8)]
        xo, yo = v_at + 1 - 2 * x, v_at + 2 - 4 * y
        return [move(7 + i, block, (f_at, to)) for i, to in enumerate((xo, yo, 3 - v_at))]

    return near, far


def greet(f_at, v_at):
    x, y = lax.rem(v_at, 2), lax.div(v_at, 2)
    barrier = pltpu.get_barrier_semaphore()
    others = [(lax.rem(f_at + i, 8), v_at) for i in range(1, 8)]
    others += [(f_at, to) for to in (v_at + 1 - 2 * x, v_at + 2 - 4 * y, 3 - v_at)]
    for other in others:
        pl.semaphore_signal(barrier, inc=1, device_id=other, device_id_type=pl.DeviceIdType.MESH)
    return lambda: pl.semaphore_wait(barrier, 10)


def message_rows(cls, proj, bias):
    return (dot(cls, proj) + bias).astype(bf).astype(f32)


def attend_rows(packed, mask, rows):
    lo = lax.broadcasted_iota(jnp.int32, (rows, 128), 1) < 64
    zero = jnp.zeros((rows, 128), bf)
    out, kept = [], []
    for h in range(6):
        q = packed[:, h * 128 : (h + 1) * 128] * jnp.asarray(0.125, bf)
        k = packed[:, D + h * 128 : D + (h + 1) * 128]
        v = packed[:, 2 * D + h * 128 : 2 * D + (h + 1) * 128]
        ps, vs = [], []
        for e in range(2):
            m = lo if e == 0 else jnp.logical_not(lo)
            st = jnp.where(mask, dot(k, jnp.where(m, q, zero), 1, 1), NEG)
            raised = jnp.exp(st - jnp.max(st, 0, keepdims=True))
            p = (raised * (1.0 / jnp.sum(raised, 0, keepdims=True))).astype(bf)
            ps.append(p)
            vs.append(jnp.where(m, v, zero))
        kept += ps
        out.append(dot(jnp.concatenate(ps, 0), jnp.concatenate(vs, 0), 0, 0).astype(bf))
    return jnp.concatenate(out, 1), kept


def first_kernel(
    vid, wq, wk, wv, wo, gain, shift, mproj_h, mqkv_h, mout_h, mbias, mgain, mshift,
    qkv_ref, pt_ref, first_ref, mixed_ref, mid_ref, tok_ref, mnext_ref, cls_ref,
    mproj, mqkv, mout, B, mrows, wsem, ssem, rsem,
):
    h = pl.program_id(0)
    f_at, v_at = lax.axis_index("frame"), lax.axis_index("video")
    near, far = gather_moves(B, ssem, rsem, f_at, v_at)

    def put_rows(rows, values):
        scaled, _ = add_norm_stats(values)
        first_ref[rows, :] = (scaled * gain[...] + shift[...]).astype(bf)
        tok_ref[rows, :] = values.astype(bf)

    @pl.when(h == 0)
    def _():
        loads = [
            pltpu.make_async_copy(src, dst, wsem.at[i])
            for i, (src, dst) in enumerate(((mproj_h, mproj), (mqkv_h, mqkv), (mout_h, mout)))
        ]
        arrived = greet(f_at, v_at)
        for load in loads:
            load.start()
        own = jnp.concatenate([vid[f, 0, 0:1].astype(f32) for f in range(FR)] + [jnp.zeros((8 - FR, D), f32)], 0)
        B[v_at * 8 + f_at] = pack_rows(own)
        arrived()
        sends = near()
        for send in sends:
            send.start()
        first_ref[pl.ds(RR, RP - RR), :] = jnp.zeros((RP - RR, D), bf)
        mixed_ref[pl.ds(RR, RP - RR), :] = jnp.zeros((RP - RR, D), bf)
        for f in range(FR):
            mid_ref[f * T + 192 : (f + 1) * T, :] = jnp.zeros((T - 192, D), f32)
            mid_ref[f * T : f * T + 197, :] = vid[f, 0].astype(f32)
            rows = slice(f * T, f * T + 192)
            put_rows(rows, mid_ref[rows, :])
        for load in loads:
            load.wait()
        for send in sends:
            send.wait()
        for send in far():
            send.start()
        cls = unpack_rows(B[pl.ds(v_at * 8, 8)]).astype(bf)
        message = message_rows(cls, mproj[...], mbias[...])
        scaled, _ = add_norm_stats(message)
        packed = dot((scaled * mgain[...] + mshift[...]).astype(bf), mqkv[...]).astype(bf)
        same = lax.rem(lax.broadcasted_iota(jnp.int32, (64, 64), 0), 8) == lax.rem(
            lax.broadcasted_iota(jnp.int32, (64, 64), 1), 8
        )
        mixed, _ = attend_rows(packed, same, 64)
        mrows[...] = message + dot(mixed, mout[...])
        mnext_ref[...] = mrows[pl.ds(pl.multiple_of(f_at * 8, 8), 8), :]
        for f in range(FR):
            mid_ref[f * T + 197 : f * T + 198, :] = mnext_ref[f : f + 1, :]
            rows = slice(f * T + 192, (f + 1) * T)
            put_rows(rows, mid_ref[rows, :])

    attend_frames(h, wq, wk, wv, wo, qkv_ref, pt_ref, first_ref, mixed_ref, mid_ref)

    @pl.when(h == 5)
    def _():
        for send in far():
            send.wait()
        cls_ref[...] = B[...]


def call_first(video, qkv, wo, gain, shift, mproj, mbias, mgain, mshift, mqkv, mout):
    one = pl.Buffered(1)
    full = lambda *s: pl.BlockSpec(s, lambda j: (0,) * len(s), pipeline_mode=one)
    keep = lambda *s: pl.BlockSpec(s, lambda j: (0,) * len(s))
    blk = lambda *s: pl.BlockSpec((1,) + s, lambda j: (j,) + (0,) * len(s))
    hbm = pl.BlockSpec(memory_space=pl.ANY)
    specs = [full(FR, 1, 197, D)] + [pl.BlockSpec((D, 128), lambda j, o=o: (0, o * 6 + j)) for o in range(3)]
    specs += [full(D, D), full(D), full(D), hbm, hbm, hbm, full(D), full(D), full(D)]
    shape = jax.ShapeDtypeStruct
    dma = pltpu.SemaphoreType.DMA
    return pl.pallas_call(
        first_kernel,
        grid=(6,),
        in_specs=specs,
        out_specs=[
            blk(RP, 384), blk(12, T, T), keep(RP, D), keep(RP, D), keep(RR, D), keep(RR, D), keep(8, D),
            keep(32, 16, D // 2),
        ],
        out_shape=[
            shape((6, RP, 384), bf),
            shape((6, 12, T, T), bf),
            shape((RP, D), bf),
            shape((RP, D), bf),
            shape((RR, D), f32),
            shape((RR, D), bf),
            shape((8, D), f32),
            shape((32, 16, D // 2), bf),
        ],
        scratch_shapes=[
            pltpu.VMEM((D, D), bf),
            pltpu.VMEM((D, 3 * D), bf),
            pltpu.VMEM((D, D), bf),
            pltpu.VMEM((32, 16, D // 2), bf),
            pltpu.VMEM((64, D), f32),
            dma((3,)),
            dma((10,)),
            dma((10,)),
        ],
        compiler_params=pltpu.CompilerParams(
            vmem_limit_bytes=VMEM_LIMIT, dimension_semantics=("arbitrary",), collective_id=2, has_side_effects=True
        ),
    )(video, qkv, qkv, qkv, wo, gain, shift, mproj, mqkv, mout, mbias, mgain, mshift)


def exchange(tick, where, U, RA, RB, RC, RD, RE, F, ssem, rsem, fsem, F_out):
    c, x, y, z0, z1, core, xn, yn, zn, zf = where

    def at(lag, body):
        s = tick - lag
        late = jnp.maximum(s - 13, 0)
        half = lax.div(late, 2)
        is_dense = jnp.logical_and(s >= 0, s < 12)
        is_frame = jnp.logical_and(jnp.logical_and(s >= 13, lax.rem(late, 2) == 0), half < 6)
        g = jnp.where(s < 12, jnp.maximum(s, 0), jnp.minimum(12 + half, UNITS - 1))

        @pl.when(jnp.logical_or(is_dense, is_frame))
        def _():
            body(g)

    def move(g, k, src, dst, target):
        return pltpu.make_async_remote_copy(
            src_ref=src,
            dst_ref=dst,
            send_sem=ssem.at[g, k],
            recv_sem=rsem.at[g, k],
            device_id=target,
            device_id_type=pl.DeviceIdType.MESH,
        )

    def a(g):
        return move(g, 0, U.at[lax.rem(g, 2), :, :, pl.ds(2 * (1 - c), 2)], RA.at[g], core)

    def b0(g):
        return move(g, 1, RA.at[g, :, 1 - x, 0], RB.at[g, 0], xn)

    def b1(g):
        return move(g, 2, RA.at[g, 1 - y, :, 1], RB.at[g, 1], yn)

    def c0(g):
        return move(g, 3, RB.at[g, 0, 1 - y], RC.at[g, 0], yn)

    def c1(g):
        return move(g, 4, RB.at[g, 1, 1 - x], RC.at[g, 1], xn)

    def d1(g):
        return move(g, 5, RC.at[g, 1 - z0], RD.at[g], zn)

    def d2(g):
        return move(g, 6, RD.at[g, pl.ds((1 - z1) * 96, 96)], RE.at[g], zf)

    def e2(g):
        piece = F.at[g, 2 * c + z0, pl.ds(z1 * 96, 96)]
        return move(g, 7, piece, piece, zf)

    def e1(g):
        piece = F.at[g, 2 * c + z0]
        return move(g, 8, piece, piece, zn)

    def last(g):
        piece = F.at[g, pl.ds(2 * c, 2)]
        return move(g, 9, piece, piece, core)

    def on_done(g):
        last(g).wait()
        pltpu.make_async_copy(F.at[g], F_out.at[g], fsem.at[g]).start()

    def on_last(g):
        e1(g).wait()
        last(g).start()

    def on_e1(g):
        e2(g).wait()
        e1(g).start()

    def on_e2(g):
        d2(g).wait()
        own = pl.ds(z1 * 96, 96)
        F[g, 2 * c + z0, own] = RE[g] + RD[g, own]
        e2(g).start()

    def on_d2(g):
        d1(g).wait()
        RD[g] = RD[g] + RC[g, z0]
        d2(g).start()

    def on_d1(g):
        c0(g).wait()
        c1(g).wait()
        RC[g, 0] = RC[g, 0] + RB[g, 0, y]
        RC[g, 1] = RC[g, 1] + RB[g, 1, x]
        d1(g).start()

    def on_c(g):
        b0(g).wait()
        b1(g).wait()
        RB[g, 0] = RB[g, 0] + RA[g, :, x, 0]
        RB[g, 1] = RB[g, 1] + RA[g, y, :, 1]
        c0(g).start()
        c1(g).start()

    def on_b(g):
        a(g).wait()
        RA[g] = RA[g] + U[lax.rem(g, 2), :, :, pl.ds(2 * c, 2)]
        b0(g).start()
        b1(g).start()

    def on_a(g):
        a(g).start()

    for lag, body in zip((0, 1, 3, 5, 7, 9, 11, 13, 15), (on_a, on_b, on_c, on_d1, on_d2, on_e2, on_e1, on_last, on_done)):
        at(lag, body)


def main_kernel(
    mid, cot, live, din0, din1, din2, din3, do0, do1, do2, do3, bin_, bout, gain2, shift2,
    qkv, pt, wq, wk, wv, first_hbm, mixed_hbm, wo_hbm, tok_hbm, mnext, gain1,
    out_hbm, gt_hbm, F_out, small_out, next_out,
    sec, G, act, dinn, oacc, gsec, CB, first, mixed, wo, dpk,
    U, RA, RB, RC, RD, RE, F, BI, SB, NB, AD, AN, ssem, rsem, fsem, lsem, adsem, adrem, ansem, anrem,
):
    t = pl.program_id(0)
    f_at, v_at = lax.axis_index("frame"), lax.axis_index("video")
    c, z = lax.rem(f_at, 2), lax.div(f_at, 2)
    x, y = lax.rem(v_at, 2), lax.div(v_at, 2)
    z0, z1 = lax.rem(z, 2), lax.div(z, 2)
    core = (f_at + 1 - 2 * c, v_at)
    xn = (f_at, v_at + 1 - 2 * x)
    yn = (f_at, v_at + 2 - 4 * y)
    zn = (f_at + 2 - 4 * z0, v_at)
    zf = (f_at + 4 - 8 * z1, v_at)
    where = (c, x, y, z0, z1, core, xn, yn, zn, zf)

    small_near, small_far = gather_moves(AD, adsem, adrem, f_at, v_at)
    next_near, next_far = gather_moves(AN, ansem, anrem, f_at, v_at)

    def tick(n):
        exchange(n, where, U, RA, RB, RC, RD, RE, F, ssem, rsem, fsem, F_out)

    def fetch(k):
        src, dst = (
            (first_hbm, first),
            (mixed_hbm, mixed),
            (wo_hbm, wo),
            (tok_hbm, act.at[pl.ds(0, RR)]),
            (CB, out_hbm),
            (sec.at[pl.ds(0, RR)], gt_hbm),
            (cot, CB),
            (AD, small_out),
            (AN, next_out),
        )[k]
        return pltpu.make_async_copy(src, dst, lsem.at[k])

    tail = pl.ds(RR, RP - RR)

    @pl.when(t == 0)
    def _():
        fetch(6).start()
        arrived = greet(f_at, v_at)
        for k in range(3):
            fetch(k).start()
        sec[tail, :] = jnp.zeros((RP - RR, D), bf)
        G[tail, :] = jnp.zeros((RP - RR, D), bf)
        act[tail, :] = jnp.zeros((RP - RR, D), bf)
        dinn[tail, :] = jnp.zeros((RP - RR, 512), bf)
        dpk[tail, :] = jnp.zeros((RP - RR, 384), bf)
        SB[...] = jnp.zeros((8, D), f32)
        BI[...] = bin_[...].reshape(1, 4 * D)
        for f in range(FR):
            rows = slice(f * T, (f + 1) * T)
            values = mid[rows, :]
            scaled, _ = add_norm_stats(values)
            sec[rows, :] = (scaled * gain2[...] + shift2[...]).astype(bf)
            oacc[rows, :] = values + bout[...]
            gsec[rows, :] = jnp.zeros((T, D), f32)
        fetch(6).wait()
        total = jnp.zeros((1, D), f32)
        for f in range(FR):
            rows = slice(f * T, (f + 1) * T)
            grad = CB[f, 0].astype(f32) * live[f].astype(f32)
            total = total + jnp.sum(grad, 0, keepdims=True)
            G[rows, :] = jnp.concatenate([grad, jnp.zeros((T - 198, D), f32)], 0).astype(bf)
        SB[4:5, :] = total
        arrived()

    din = lambda: jnp.concatenate([din0[...], din1[...], din2[...], din3[...]], 1)
    dout = lambda: jnp.concatenate([do0[...], do1[...], do2[...], do3[...]], 0)

    def put(slot, index, block):
        q, b = index
        U[slot, q // 2, q % 2, b] = block.astype(bf)

    @pl.when(t < 6)
    def _():
        w_in, w_out = din(), dout()
        bias = jnp.concatenate([BI[:, pl.ds(pl.multiple_of(q * D + t * 128, 128), 128)] for q in range(4)], 1)
        sums = jnp.zeros((1, 512), f32)
        MB = 416
        for r in range(RR // MB):
            s = slice(r * MB, (r + 1) * MB)
            inner = dot(sec[s, :], w_in) + bias
            ga = dot(G[s, :], w_out, 1, 1)
            sg = 0.5 * jnp.tanh(0.851 * inner) + 0.5
            ac = inner * sg
            act[s, 0:512] = ac.astype(bf)
            di = ga * (sg + 1.702 * ac * (1.0 - sg))
            sums = sums + jnp.sum(di, 0, keepdims=True)
            dinn[s, :] = di.astype(bf)
        for b in range(4):
            SB[b : b + 1, pl.ds(pl.multiple_of(t * 128, 128), 128)] = sums[:, b * 128 : (b + 1) * 128]
        part = dot(G[...], act[:, 0:512], 0, 0)
        for q in range(4):
            for b in range(4):
                put(0, (q, b), part[b * ROWS : (b + 1) * ROWS, q * 128 : (q + 1) * 128])

    lo = lax.broadcasted_iota(jnp.int32, (T, 128), 1) < 64
    zero = jnp.zeros((T, 128), bf)
    head = jnp.maximum(t - 6, 0)
    lanes = pl.ds(pl.multiple_of(head * 128, 128), 128)

    def attend_back(frames):
        for f in frames:
            s = slice(f * T, (f + 1) * T)
            q, k, v = qkv[0, s, 0:128], qkv[0, s, 128:256], qkv[0, s, 256:384]
            do = G[s, lanes]
            dss, ks, dk, dv = [], [], 0.0, 0.0
            for e in range(2):
                m = lo if e == 0 else jnp.logical_not(lo)
                doe = jnp.where(m, do, zero)
                pb = pt[0, f * 2 + e]
                p = pb.astype(f32)
                dp = dot(v, doe, 1, 1)
                ds = (p * (dp - jnp.sum(dp * p, 0, keepdims=True))).astype(bf)
                dk = dk + dot(ds, jnp.where(m, q, zero))
                dv = dv + dot(pb, doe)
                dss.append(ds)
                ks.append(jnp.where(m, k, zero))
            dq = dot(jnp.concatenate(dss, 0), jnp.concatenate(ks, 0), 0, 0) * 0.125
            dpk[s, 0:128] = dq.astype(bf)
            dpk[s, 128:256] = (dk * 0.125).astype(bf)
            dpk[s, 256:384] = dv.astype(bf)

    @pl.when(t == 6)
    def _():
        gg = jnp.zeros((1, D), f32)
        gs = jnp.zeros((1, D), f32)
        for f in range(FR):
            s = slice(f * T, (f + 1) * T)
            CB[f, 0] = oacc[s, :][:198].astype(bf)
            scaled, inverse = add_norm_stats(mid[s, :])
            grad = gsec[s, :]
            gg = gg + jnp.sum(grad * scaled, 0, keepdims=True)
            gs = gs + jnp.sum(grad, 0, keepdims=True)
            total = G[s, :].astype(f32) + norm_back(grad, scaled, inverse, gain2[...])
            gsec[s, :] = total
            sec[s, :] = total.astype(bf)
            oacc[s, :] = jnp.zeros((T, D), f32)
        SB[5:6, :] = gg
        SB[6:7, :] = gs
        AD[v_at * 8 + f_at] = pack_rows(SB[...])
        for send in small_near():
            send.start()
        fetch(4).start()
        fetch(3).start()
        for k in range(3):
            fetch(k).wait()
        G[0:RR, :] = dot(sec[0:RR, :], wo[...], 1, 1).astype(bf)

    @pl.when(t >= 6)
    def _():
        attend_back(range(3))

    tick(2 * t)

    @pl.when(t < 6)
    def _():
        w_in, w_out = din(), dout()
        part = dot(sec[...], dinn[...], 0, 0)
        for q in range(4):
            for b in range(4):
                put(1, (q, b), part[q * ROWS : (q + 1) * ROWS, b * 128 : (b + 1) * 128])
        oacc[...] += dot(act[0:RR, 0:512], w_out)
        gsec[...] += dot(dinn[0:RR, :], w_in, 1, 1)

    @pl.when(t >= 6)
    def _():
        attend_back(range(3, 6))
        slot = lax.rem(head, 2)
        part = dot(first[...], dpk[...], 0, 0)
        for q in range(4):
            for b in range(3):
                put(slot, (q, b), part[q * ROWS : (q + 1) * ROWS, b * 128 : (b + 1) * 128])
        part = dot(mixed[...], sec[:, lanes], 0, 0)
        for q in range(4):
            put(slot, (q, 3), part[q * ROWS : (q + 1) * ROWS, :])

    tick(2 * t + 1)

    @pl.when(t >= 6)
    def _():
        w = jnp.concatenate([wq[...], wk[...], wv[...]], 1)
        oacc[...] += dot(dpk[0:RR, :], w, 1, 1)

    @pl.when(t == 8)
    def _():
        for send in small_near():
            send.wait()
        for send in small_far():
            send.start()

    @pl.when(t == STEPS - 1)
    def _():
        fetch(3).wait()
        gg = jnp.zeros((1, D), f32)
        gs = jnp.zeros((1, D), f32)
        last_row = lax.broadcasted_iota(jnp.int32, (16, D), 0) == 5
        for f in range(FR):
            s = slice(f * T, (f + 1) * T)
            values = act[s, :].astype(f32)
            low = jnp.where(last_row, mnext[f : f + 1, :], values[192:])
            values = jnp.concatenate([values[:192], low], 0)
            scaled, inverse = add_norm_stats(values)
            grad = oacc[s, :]
            gg = gg + jnp.sum(grad * scaled, 0, keepdims=True)
            gs = gs + jnp.sum(grad, 0, keepdims=True)
            total = gsec[s, :] + norm_back(grad, scaled, inverse, gain1[...])
            sec[s, :] = total.astype(bf)
            NB[f : f + 1, :] = total[197:198]
        NB[6:7, :] = gg
        NB[7:8, :] = gs
        AN[v_at * 8 + f_at] = pack_rows(NB[...])
        for send in next_near():
            send.start()
        fetch(5).start()
        for send in small_far():
            send.wait()
        fetch(7).start()

        def step(n, carry):
            tick(n)
            return carry

        lax.fori_loop(2 * STEPS, 2 * STEPS + 3, step, 0)
        for send in next_near():
            send.wait()
        for send in next_far():
            send.start()
        lax.fori_loop(2 * STEPS + 3, TICKS, step, 0)
        for send in next_far():
            send.wait()
        fetch(8).start()

        def finish(g, carry):
            pltpu.make_async_copy(F.at[g], F_out.at[g], fsem.at[g]).wait()
            return carry

        lax.fori_loop(0, UNITS, finish, 0)
        for k in (4, 5, 7, 8):
            fetch(k).wait()


def call_main(mid, cot, live, din, dout, bin_, bout, gain2, shift2, qkv, pt, wqkv, first, mixed, wo, tok, mnext, gain1):
    one = pl.Buffered(1)
    full = lambda *s: pl.BlockSpec(s, lambda t: (0,) * len(s), pipeline_mode=one)
    hbm = pl.BlockSpec(memory_space=pl.ANY)
    dense = lambda t: jnp.minimum(t, 5)
    head = lambda t: jnp.maximum(t - 6, 0)
    specs = [full(RR, D), hbm, pl.BlockSpec(memory_space=pltpu.SMEM)]
    specs += [pl.BlockSpec((D, 128), lambda t, q=q: (0, q * 6 + dense(t))) for q in range(4)]
    specs += [pl.BlockSpec((128, D), lambda t, q=q: (q * 6 + dense(t), 0)) for q in range(4)]
    specs += [full(bin_.shape[0]), full(D), full(D), full(D)]
    specs += [pl.BlockSpec((1, RP, 384), lambda t: (head(t), 0, 0)), pl.BlockSpec((1, 12, T, T), lambda t: (head(t), 0, 0, 0))]
    specs += [pl.BlockSpec((D, 128), lambda t, o=o: (0, o * 6 + head(t))) for o in range(3)]
    specs += [hbm, hbm, hbm, hbm, full(8, D), full(D)]
    shape = jax.ShapeDtypeStruct
    dma = pltpu.SemaphoreType.DMA
    return pl.pallas_call(
        main_kernel,
        grid=(STEPS,),
        in_specs=specs,
        out_specs=[hbm] * 5,
        out_shape=[
            shape((FR, 1, 198, D), bf),
            shape((RR, D), bf),
            shape((UNITS, 4, ROWS, 128), bf),
            shape((32, 16, D // 2), bf),
            shape((32, 16, D // 2), bf),
        ],
        scratch_shapes=[
            pltpu.VMEM((RP, D), bf),
            pltpu.VMEM((RP, D), bf),
            pltpu.VMEM((RP, D), bf),
            pltpu.VMEM((RP, 512), bf),
            pltpu.VMEM((RR, D), f32),
            pltpu.VMEM((RR, D), f32),
            pltpu.VMEM((FR, 1, 198, D), bf),
            pltpu.VMEM((RP, D), bf),
            pltpu.VMEM((RP, D), bf),
            pltpu.VMEM((D, D), bf),
            pltpu.VMEM((RP, 384), bf),
            pltpu.VMEM((2, 2, 2, 4, ROWS, 128), bf),
            pltpu.VMEM((UNITS, 2, 2, 2, ROWS, 128), bf),
            pltpu.VMEM((UNITS, 2, 2, ROWS, 128), bf),
            pltpu.VMEM((UNITS, 2, ROWS, 128), bf),
            pltpu.VMEM((UNITS, ROWS, 128), bf),
            pltpu.VMEM((UNITS, ROWS // 2, 128), bf),
            pltpu.VMEM((UNITS, 4, ROWS, 128), bf),
            pltpu.VMEM((1, 4 * D), f32),
            pltpu.VMEM((8, D), f32),
            pltpu.VMEM((8, D), f32),
            pltpu.VMEM((32, 16, D // 2), bf),
            pltpu.VMEM((32, 16, D // 2), bf),
            dma((UNITS, 10)),
            dma((UNITS, 10)),
            dma((UNITS,)),
            dma((9,)),
            dma((10,)),
            dma((10,)),
            dma((10,)),
            dma((10,)),
        ],
        compiler_params=pltpu.CompilerParams(
            vmem_limit_bytes=VMEM_LIMIT,
            dimension_semantics=("arbitrary",),
            collective_id=1,
            has_side_effects=True,
        ),
    )(mid, cot, live, din, din, din, din, dout, dout, dout, dout, bin_, bout, gain2, shift2,
      qkv, pt, wqkv, wqkv, wqkv, first, mixed, wo, tok, mnext, gain1)


def final_kernel(
    F, gt, cls_blocks, next_blocks, small_blocks, mproj, mbias, mgain, mshift, mqkv, mout, out_in,
    out, gvid, gproj, gmqkv, gmout, gfqkv, gfout, gdin, gdout, *rest,
):
    vecs, bias_in, held = rest[:8], rest[8], rest[9]
    f_at, v_at = lax.axis_index("frame"), lax.axis_index("video")
    out[...] = out_in[...]
    rows = 256
    cls = unpack_rows(cls_blocks[...]).astype(bf)
    message = message_rows(cls, mproj[...], mbias[...])
    scaled, inverse = add_norm_stats(message)
    normed = (scaled * mgain[...] + mshift[...]).astype(bf)
    packed = dot(normed, mqkv[...]).astype(bf)
    ik = lax.broadcasted_iota(jnp.int32, (rows, rows), 0)
    iq = lax.broadcasted_iota(jnp.int32, (rows, rows), 1)
    same = jnp.logical_and(lax.rem(ik, 8) == lax.rem(iq, 8), lax.div(ik, 64) == lax.div(iq, 64))
    mixed, probs = attend_rows(packed, same, rows)
    arrived = unpack_rows(next_blocks[...])
    kind = lax.rem(lax.broadcasted_iota(jnp.int32, (rows, D), 0), 8)
    gnext = jnp.where(kind < 6, arrived, 0.0)
    gfgain = jnp.sum(jnp.where(kind == 6, arrived, 0.0), 0, keepdims=True)
    gfshift = jnp.sum(jnp.where(kind == 7, arrived, 0.0), 0, keepdims=True)
    gnext_low = gnext.astype(bf)
    gmixed = dot(gnext_low, mout[...], 1, 1).astype(bf)
    lo = lax.broadcasted_iota(jnp.int32, (rows, 128), 1) < 64
    zero = jnp.zeros((rows, 128), bf)
    gq, gk, gv = [], [], []
    for h in range(6):
        q, k, v = (packed[:, o * D + h * 128 : o * D + (h + 1) * 128] for o in range(3))
        do = gmixed[:, h * 128 : (h + 1) * 128]
        dss, ks, dk, dv = [], [], 0.0, 0.0
        for e in range(2):
            m = lo if e == 0 else jnp.logical_not(lo)
            doe = jnp.where(m, do, zero)
            pb = probs[2 * h + e]
            p = pb.astype(f32)
            dp = dot(v, doe, 1, 1)
            ds = (p * (dp - jnp.sum(dp * p, 0, keepdims=True))).astype(bf)
            dk = dk + dot(ds, jnp.where(m, q, zero))
            dv = dv + dot(pb, doe)
            dss.append(ds)
            ks.append(jnp.where(m, k, zero))
        gq.append((dot(jnp.concatenate(dss, 0), jnp.concatenate(ks, 0), 0, 0) * 0.125).astype(bf))
        gk.append((dk * 0.125).astype(bf))
        gv.append(dv.astype(bf))
    gpacked = jnp.concatenate(gq + gk + gv, 1)
    gnormed = dot(gpacked, mqkv[...], 1, 1)
    gmgain = jnp.sum(gnormed * scaled, 0, keepdims=True)
    gmshift = jnp.sum(gnormed, 0, keepdims=True)
    gmessage = gnext + norm_back(gnormed, scaled, inverse, mgain[...])
    gmbias = jnp.sum(gmessage, 0, keepdims=True)
    gmessage_low = gmessage.astype(bf)
    held[...] = dot(gmessage_low, mproj[...], 1, 1)
    place = pl.multiple_of((v_at * 8 + f_at) * 8, 8)
    gclass = held[pl.ds(place, 8), :]

    def mine(values):
        parts = [values[:, i * ROWS : (i + 1) * ROWS] for i in range(4)]
        return jnp.where(v_at == 0, parts[0], jnp.where(v_at == 1, parts[1], jnp.where(v_at == 2, parts[2], parts[3])))

    gproj[...] = dot(mine(cls), gmessage_low, 0, 0)
    gmqkv[...] = dot(mine(normed), gpacked, 0, 0)
    gmout[...] = dot(mine(mixed), gnext_low, 0, 0)
    small = unpack_rows(small_blocks[...])
    small = jnp.sum(small.reshape(32, 8, D), 0)
    lines = [gmbias, gmgain, gmshift, gfgain, gfshift, small[5:6], small[6:7], small[4:5]]
    picked = mine(jnp.concatenate(lines, 0))
    for i, ref in enumerate(vecs):
        ref[...] = picked[i]
    b = [small[i : i + 1] for i in range(4)]
    bias_in[...] = jnp.where(v_at == 0, b[0], jnp.where(v_at == 1, b[1], jnp.where(v_at == 2, b[2], b[3])))[0]
    for f in range(FR):
        gvid[f, 0] = gt[f * T : (f + 1) * T, :][:197]
        gvid[f, 0, 0:1] = (gt[f * T : f * T + 16, :].astype(f32)[0:1] + gclass[f : f + 1, :]).astype(bf)
    for j in range(6):
        for b in range(4):
            at = b * D + j * 128
            gdin[:, at : at + 128] = F[2 * j + 1, b].astype(f32)
            gdout[j * 128 : (j + 1) * 128, b * ROWS : (b + 1) * ROWS] = F[2 * j, b].astype(f32).T
            if b < 3:
                gfqkv[:, at : at + 128] = F[12 + j, b].astype(f32)
            else:
                gfout[:, j * 128 : (j + 1) * 128] = F[12 + j, b].astype(f32)


def call_final(F, gt, cls_blocks, next_blocks, small_blocks, mproj, mbias, mgain, mshift, mqkv, mout, output):
    vm = pl.BlockSpec(memory_space=pltpu.VMEM)
    hbm = pl.BlockSpec(memory_space=pl.ANY)
    shape = jax.ShapeDtypeStruct
    return pl.pallas_call(
        final_kernel,
        in_specs=[vm] * 12,
        out_specs=[vm] * 18,
        out_shape=[
            shape((FR, 1, 198, D), bf),
            shape((FR, 1, 197, D), bf),
            shape((ROWS, D), f32),
            shape((ROWS, 3 * D), f32),
            shape((ROWS, D), f32),
            shape((ROWS, 3 * D), f32),
            shape((ROWS, D), f32),
            shape((ROWS, 4 * D), f32),
            shape((4 * ROWS, D), f32),
        ]
        + [shape((ROWS,), f32)] * 8
        + [shape((D,), f32)],
        scratch_shapes=[pltpu.VMEM((256, D), f32)],
        compiler_params=pltpu.CompilerParams(vmem_limit_bytes=VMEM_LIMIT),
    )(F, gt, cls_blocks, next_blocks, small_blocks, mproj, mbias, mgain, mshift, mqkv, mout, output)


def column_sum(values):
    return jnp.sum(values.reshape(-1, values.shape[-1]), axis=0)


def matmul(left, right):
    return jnp.dot(left, right, preferred_element_type=f32)


def back_matmul(grad_low, weight):
    return lax.dot_general(grad_low, weight, (((grad_low.ndim - 1,), (1,)), ((), ())), preferred_element_type=f32)


def weight_grad(inputs_low, grad_low):
    left = inputs_low.reshape(-1, inputs_low.shape[-1])
    right = grad_low.reshape(-1, grad_low.shape[-1])
    return lax.dot_general(left, right, (((0,), (0,)), ((), ())), preferred_element_type=f32)


def norm_forward(values, gain, shift):
    center = values - jnp.mean(values, axis=-1, keepdims=True)
    inverse = lax.rsqrt(jnp.mean(center * center, axis=-1, keepdims=True) + EPS)
    scaled = center * inverse
    return (scaled * gain + shift, scaled, inverse)


def norm_backward(grad_out, scaled, inverse, gain):
    grad_scaled = grad_out * gain
    grad_in = inverse * (
        grad_scaled
        - jnp.mean(grad_scaled, axis=-1, keepdims=True)
        - scaled * jnp.mean(grad_scaled * scaled, axis=-1, keepdims=True)
    )
    return (grad_in, column_sum(grad_out * scaled), column_sum(grad_out))


def split_heads(values):
    return values.reshape(values.shape[:-1] + (HEADS, HEAD_DIM))


def attend_forward(query_rows, key_rows, value_rows):
    scores = jnp.einsum("bqhd,bkhd->bhqk", query_rows, key_rows, preferred_element_type=f32) * 0.125
    largest = jnp.max(scores, axis=-1, keepdims=True)
    raised = jnp.exp(scores - largest)
    total = jnp.sum(raised, axis=-1, keepdims=True)
    probs_low = (raised / total).astype(bf)
    mixed = jnp.einsum("bhqk,bkhd->bqhd", probs_low, value_rows, preferred_element_type=f32)
    return (mixed, largest + jnp.log(total))


def attend_backward(query_rows, key_rows, value_rows, log_total, grad_mixed):
    scores = jnp.einsum("bqhd,bkhd->bhqk", query_rows, key_rows, preferred_element_type=f32) * 0.125
    probs = jnp.exp(scores - log_total)
    grad_probs = jnp.einsum("bqhd,bkhd->bhqk", grad_mixed, value_rows, preferred_element_type=f32)
    grad_scores = probs * (grad_probs - jnp.sum(grad_probs * probs, axis=-1, keepdims=True))
    grad_low = grad_scores.astype(bf)
    grad_query = jnp.einsum("bhqk,bkhd->bqhd", grad_low, key_rows, preferred_element_type=f32) * 0.125
    grad_key = jnp.einsum("bhqk,bqhd->bkhd", grad_low, query_rows, preferred_element_type=f32) * 0.125
    grad_value = jnp.einsum("bhqk,bqhd->bkhd", probs.astype(bf), grad_mixed, preferred_element_type=f32)
    return (grad_query, grad_key, grad_value)


def message_forward(video, message_proj, message_bias, message_gain, message_shift, message_qkv, message_out):
    width = video.shape[-1]
    batch, frames_local = video.shape[:2]
    class_rows = video[:, :, 0, :]
    message = (matmul(class_rows, message_proj) + message_bias).astype(bf)
    message_wide = message.astype(f32)
    normed_own, scaled_own, inverse_own = norm_forward(message_wide, message_gain, message_shift)
    normed_low = normed_own.astype(bf)
    everyone = lax.all_gather(message, "frame", axis=1, tiled=True)
    normed_all = norm_forward(everyone.astype(f32), message_gain, message_shift)[0]
    key_value = matmul(normed_all.astype(bf), message_qkv[:, width:]).astype(bf)
    query = split_heads(matmul(normed_low, message_qkv[:, :width]).astype(bf))
    key = split_heads(key_value[..., :width])
    value = split_heads(key_value[..., width:])
    mixed, total = attend_forward(query, key, value)
    mixed_low = mixed.reshape(batch, frames_local, width).astype(bf)
    message_next = message_wide + matmul(mixed_low, message_out)
    return message_next, (class_rows, normed_low, scaled_own, inverse_own, query, key, value, mixed_low, total)


def message_backward(kept, grad_next, message_proj, message_gain, message_qkv, message_out):
    class_rows, normed_low, scaled_own, inverse_own, query, key, value, mixed_low, total = kept
    batch, frames_local, width = grad_next.shape
    frames_all = key.shape[1]
    grad_next_low = grad_next.astype(bf)
    grad_mixed = split_heads(back_matmul(grad_next_low, message_out).astype(bf))
    grad_q, grad_k, grad_v = attend_backward(query, key, value, total, grad_mixed)
    key_value_grad = jnp.concatenate(
        [grad_k.reshape(batch, frames_all, width), grad_v.reshape(batch, frames_all, width)], axis=-1
    )
    own = lax.psum_scatter(key_value_grad.astype(bf), "frame", scatter_dimension=1, tiled=True)
    packed = jnp.concatenate([grad_q.reshape(batch, frames_local, width).astype(bf), own], axis=-1)
    grad_in, grad_gain, grad_shift = norm_backward(
        back_matmul(packed, message_qkv), scaled_own, inverse_own, message_gain
    )
    grad_message = grad_next + grad_in
    grad_message_low = grad_message.astype(bf)
    grad_class = back_matmul(grad_message_low, message_proj)
    rows = jnp.concatenate([class_rows, normed_low, mixed_low, grad_message_low, packed, grad_next_low], axis=-1)
    rows = rows.reshape(batch * frames_local, -1)
    return grad_class, rows, column_sum(grad_message), grad_gain, grad_shift


def reduced_inside(
    video, video_live, cotangent, message_proj, message_bias, message_gain, message_shift, message_qkv,
    message_out, frame_gain, frame_shift, frame_qkv, frame_out, dense_gain, dense_shift, dense_in,
    dense_in_bias, dense_out, dense_out_bias,
):
    packed, probs, first, mixed, middle, tokens, next_rows, class_blocks = call_first(
        video, frame_qkv, frame_out, frame_gain, frame_shift,
        message_proj, message_bias, message_gain, message_shift, message_qkv, message_out,
    )
    output, grad_rows, reduced, small_blocks, next_blocks = call_main(
        middle, cotangent, video_live, dense_in, dense_out, dense_in_bias, dense_out_bias, dense_gain, dense_shift,
        packed, probs, frame_qkv, first, mixed, frame_out, tokens, next_rows, frame_gain,
    )
    output, grad_input, g_proj, g_mqkv, g_mout, g_fqkv, g_fout, g_in, g_out, *lines = call_final(
        reduced, grad_rows, class_blocks, next_blocks, small_blocks,
        message_proj, message_bias, message_gain, message_shift, message_qkv, message_out, output,
    )
    return (
        output, grad_input, g_proj, lines[0], lines[1], lines[2], g_mqkv, g_mout, lines[3], lines[4], g_fqkv, g_fout,
        lines[5], lines[6], g_in, lines[8], g_out, lines[7],
    )


def local(
    video,
    video_live,
    cotangent,
    message_proj,
    message_bias,
    message_gain,
    message_shift,
    message_qkv,
    message_out,
    frame_gain,
    frame_shift,
    frame_qkv,
    frame_out,
    dense_gain,
    dense_shift,
    dense_in,
    dense_in_bias,
    dense_out,
    dense_out_bias,
):
    batch, frames_local, patches, width = video.shape
    hidden = dense_in.shape[1]
    groups = lax.axis_size("video")
    if (lax.axis_size("frame"), groups) == (8, 4):
        return reduced_inside(
            video, video_live, cotangent, message_proj, message_bias, message_gain, message_shift, message_qkv,
            message_out, frame_gain, frame_shift, frame_qkv, frame_out, dense_gain, dense_shift, dense_in,
            dense_in_bias, dense_out, dense_out_bias,
        )
    message_next, kept = message_forward(
        video, message_proj, message_bias, message_gain, message_shift, message_qkv, message_out
    )
    next_rows = message_next.reshape(batch * frames_local, width)
    packed, probs, first, mixed, middle, _ = call_k1(video, next_rows, frame_qkv, frame_out, frame_gain, frame_shift)
    output, grad_middle, part_in, part_out, part_bias, dense_small = call_k2(
        middle, cotangent, video_live, dense_in, dense_out, dense_in_bias, dense_out_bias, dense_gain, dense_shift
    )
    grad_tokens, part_frame, frame_small = call_k3(
        video, next_rows, grad_middle, packed, probs, first, mixed, frame_qkv, frame_out, frame_gain
    )
    grad_tokens = grad_tokens.reshape(batch, frames_local, T, width)
    grad_next = grad_tokens[:, :, patches]
    grad_class, rows, sum_bias, sum_gain, sum_shift = message_backward(
        kept, grad_next, message_proj, message_gain, message_qkv, message_out
    )
    grad_input = jnp.concatenate(
        [grad_tokens[:, :, :1] + grad_class[:, :, None, :], grad_tokens[:, :, 1:patches]], axis=2
    ).astype(bf)

    def total(value):
        share = lax.psum_scatter(value, "video", scatter_dimension=0, tiled=True)
        return lax.psum(share, "frame").astype(f32)

    grad_in = total(part_in.reshape(6, width, 4, 128).transpose(1, 2, 0, 3).reshape(width, hidden))
    grad_out = total(part_out.reshape(6, width, 4, 128).transpose(2, 0, 3, 1).reshape(hidden, width))
    part_frame = part_frame.reshape(6, width, 4, 128).transpose(1, 2, 0, 3).reshape(width, 4 * width)
    grad_frame = total(part_frame)
    vector = jnp.concatenate(
        [
            sum_bias,
            sum_gain,
            sum_shift,
            frame_small[0],
            frame_small[1],
            dense_small[1],
            dense_small[2],
            dense_small[0],
            part_bias.reshape(6, 4, 128).transpose(1, 0, 2).reshape(hidden),
        ]
    )
    vector = lax.psum(vector, ("video", "frame"))
    place = lax.axis_index("video")
    cut = width // groups

    def mine(start, length):
        return lax.dynamic_slice_in_dim(vector, start + place * (length // groups), length // groups)

    gathered = lax.all_gather(rows, ("video", "frame"), axis=0, tiled=True)

    def outer(left, first_column, last_column):
        part = lax.dynamic_slice_in_dim(gathered, left * width + place * cut, cut, axis=1)
        return weight_grad(part, gathered[:, first_column:last_column])

    return (
        output,
        grad_input,
        outer(0, 3 * width, 4 * width),
        mine(0, width),
        mine(width, width),
        mine(2 * width, width),
        outer(1, 4 * width, 7 * width),
        outer(2, 7 * width, 8 * width),
        mine(3 * width, width),
        mine(4 * width, width),
        grad_frame[:, : 3 * width],
        grad_frame[:, 3 * width :],
        mine(5 * width, width),
        mine(6 * width, width),
        grad_in,
        mine(8 * width, hidden),
        grad_out,
        mine(7 * width, width),
    )


def solution(mesh):
    in_specs = (
        P("video", "frame", None, None),
        P("video"),
        P("video", "frame", None, None),
        P(),
        P(),
        P(),
        P(),
        P(),
        P(),
        P(),
        P(),
        P(),
        P(),
        P(),
        P(),
        P(),
        P(),
        P(),
        P(),
    )
    out_specs = (
        P("video", "frame", None, None),
        P("video", "frame", None, None),
        P("video", None),
        P("video"),
        P("video"),
        P("video"),
        P("video", None),
        P("video", None),
        P("video"),
        P("video"),
        P("video", None),
        P("video", None),
        P("video"),
        P("video"),
        P("video", None),
        P("video"),
        P("video", None),
        P("video"),
    )
    return jax.shard_map(local, mesh=mesh, in_specs=in_specs, out_specs=out_specs, check_vma=False)
```

```python
import functools
import jax
import jax.numpy as jnp
from jax import lax
from jax.experimental import pallas as pl
from jax.experimental.pallas import tpu as pltpu
bf=jnp.bfloat16; f32=jnp.float32
EPS=1e-5
def dot(a,b,ca=1,cb=0): return lax.dot_general(a,b,(((ca,),(cb,)),((),())),preferred_element_type=f32)
FR=6; T=208; RR=FR*T; RP=1280; D=768
def k2(MB, mid, cot, live, din0,din1,din2,din3, do0,do1,do2,do3, bin_, bout, gain, shift,
       out_ref, gmid_ref, gdi_ref, gdo_ref, gbin_ref, small_ref,
       sec, G, act, dinn, oacc, gsec):
    j=pl.program_id(0)
    @pl.when(j==0)
    def _():
        ob=jnp.zeros((1,D),f32)
        sec[pl.ds(RR,RP-RR),:]=jnp.zeros((RP-RR,D),bf)
        G[pl.ds(RR,RP-RR),:]=jnp.zeros((RP-RR,D),bf)
        act[pl.ds(RR,RP-RR),:]=jnp.zeros((RP-RR,512),bf)
        dinn[pl.ds(RR,RP-RR),:]=jnp.zeros((RP-RR,512),bf)
        for f in range(FR):
            x=mid[f*T:(f+1)*T,:]
            mu=jnp.mean(x,-1,keepdims=True); c=x-mu
            inv=lax.rsqrt(jnp.mean(c*c,-1,keepdims=True)+EPS)
            sec[f*T:(f+1)*T,:]=(c*inv*gain[...]+shift[...]).astype(bf)
            g=cot[f,0].astype(f32)*live[f].astype(f32)
            g=jnp.concatenate([g,jnp.zeros((T-198,D),f32)],0)
            ob=ob+jnp.sum(g,0,keepdims=True)
            G[f*T:(f+1)*T,:]=g.astype(bf)
            oacc[f*T:(f+1)*T,:]=x+bout[...]
            gsec[f*T:(f+1)*T,:]=jnp.zeros((T,D),f32)
        small_ref[0:1,:]=ob
    din=jnp.concatenate([din0[...],din1[...],din2[...],din3[...]],1)
    do=jnp.concatenate([do0[...],do1[...],do2[...],do3[...]],0)
    b=jnp.concatenate([bin_[0:1,:],bin_[1:2,:],bin_[2:3,:],bin_[3:4,:]],1) if False else bin_[0]
    bsum=jnp.zeros((1,512),f32)
    for r in range(RR//MB):
        s=slice(r*MB,(r+1)*MB)
        inner=dot(sec[s,:],din)+b
        ga=dot(G[s,:],do,1,1)
        sg=0.5*jnp.tanh(0.851*inner)+0.5
        ac=inner*sg
        act[s,:]=ac.astype(bf)
        di=ga*(sg+1.702*ac*(1.0-sg))
        bsum=bsum+jnp.sum(di,0,keepdims=True)
        dinn[s,:]=di.astype(bf)
    gbin_ref[0]=bsum
    for r in range(RR//MB):
        s=slice(r*MB,(r+1)*MB)
        oacc[s,:]+=dot(act[s,:],do)
        gsec[s,:]+=dot(dinn[s,:],din,1,1)
    gdo_ref[0]=dot(G[...],act[...],0,0).astype(bf)
    gdi_ref[0]=dot(sec[...],dinn[...],0,0).astype(bf)
    @pl.when(j==pl.num_programs(0)-1)
    def _():
        gg=jnp.zeros((1,D),f32); gs=jnp.zeros((1,D),f32)
        for f in range(FR):
            s=slice(f*T,(f+1)*T)
            out_ref[f,0]=oacc[s,:][:198].astype(bf)
            x=mid[s,:]
            mu=jnp.mean(x,-1,keepdims=True); c=x-mu
            inv=lax.rsqrt(jnp.mean(c*c,-1,keepdims=True)+EPS)
            sc=c*inv
            go=gsec[s,:]
            gg=gg+jnp.sum(go*sc,0,keepdims=True); gs=gs+jnp.sum(go,0,keepdims=True)
            gsc=go*gain[...]
            gi=inv*(gsc-jnp.mean(gsc,-1,keepdims=True)-sc*jnp.mean(gsc*sc,-1,keepdims=True))
            gmid_ref[s,:]=G[s,:].astype(f32)+gi
        small_ref[1:2,:]=gg; small_ref[2:3,:]=gs
def call_k2(mid,cot,live,din,do,bin_,bout,gain,shift,MB=624):
    full=lambda *s: pl.BlockSpec(s,lambda j:(0,)*len(s))
    nq=din.shape[1]//512
    vm=pl.BlockSpec(memory_space=pltpu.VMEM)
    specs=[full(RR,D),full(FR,1,198,D),pl.BlockSpec(memory_space=pltpu.SMEM)]
    for q in range(4): specs.append(pl.BlockSpec((D,128),lambda j,q=q:(0,q*6+j)))
    for q in range(4): specs.append(pl.BlockSpec((128,D),lambda j,q=q:(q*6+j,0)))
    specs+= [pl.BlockSpec((1,1,512),lambda j:(j,0,0)),full(1,D),full(1,D),full(1,D)]
    b3=bin_.reshape(4,6,128).transpose(1,0,2).reshape(6,1,512)
    return pl.pallas_call(functools.partial(k2,MB),grid=(6,),in_specs=specs,
      out_specs=[full(FR,1,198,D),full(RR,D),pl.BlockSpec((1,D,512),lambda j:(j,0,0)),pl.BlockSpec((1,D,512),lambda j:(j,0,0)),pl.BlockSpec((1,1,512),lambda j:(j,0,0)),full(8,D)],
      out_shape=[jax.ShapeDtypeStruct((FR,1,198,D),bf),jax.ShapeDtypeStruct((RR,D),f32),jax.ShapeDtypeStruct((6,D,512),bf),jax.ShapeDtypeStruct((6,D,512),bf),jax.ShapeDtypeStruct((6,1,512),f32),jax.ShapeDtypeStruct((8,D),f32)],
      scratch_shapes=[pltpu.VMEM((RP,D),bf),pltpu.VMEM((RP,D),bf),pltpu.VMEM((RP,512),bf),pltpu.VMEM((RP,512),bf),pltpu.VMEM((RR,D),f32),pltpu.VMEM((RR,D),f32)],
      compiler_params=pltpu.CompilerParams(vmem_limit_bytes=61<<20,dimension_semantics=("arbitrary",)),
    )(mid,cot,live,din,din,din,din,do,do,do,do,b3,bout.reshape(1,D),gain.reshape(1,D),shift.reshape(1,D))
from jax.sharding import PartitionSpec as P
HEADS=12
HEAD_DIM=64
NEG=-1e30
VMEM_LIMIT=63<<20

def half_masks(rows):
    lane=lax.broadcasted_iota(jnp.int32,(rows,128),1)
    return lane<64
def attend_frames(h,wq,wk,wv,wo,qkv_ref,pt_ref,first_ref,mixed_ref,mid_ref):
    w=jnp.concatenate([wq[...],wk[...],wv[...]],1)
    qkv_ref[0,0:RR,:]=dot(first_ref[0:RR,:],w).astype(bf)
    qkv_ref[0,RR:RP,:]=jnp.zeros((RP-RR,384),bf)
    lo=half_masks(T)
    keep=lax.broadcasted_iota(jnp.int32,(16,T),0)<6
    zero=jnp.zeros((T,128),bf)
    def one(f,carry):
        s=pl.ds(pl.multiple_of(f*T,16),T)
        q=qkv_ref[0,s,0:128]*jnp.asarray(0.125,bf); k=qkv_ref[0,s,128:256]; v=qkv_ref[0,s,256:384]
        ps=[]; vs=[]
        for e in range(2):
            m=lo if e==0 else jnp.logical_not(lo)
            st=dot(k,jnp.where(m,q,zero),1,1)
            top=st[:192]; bot=jnp.where(keep,st[192:],NEG)
            mx=jnp.maximum(jnp.max(top,0,keepdims=True),jnp.max(bot,0,keepdims=True))
            top=jnp.exp(top-mx); bot=jnp.exp(bot-mx)
            tot=jnp.sum(top,0,keepdims=True)+jnp.sum(bot,0,keepdims=True)
            p=(jnp.concatenate([top,bot],0)*(1.0/tot)).astype(bf)
            pt_ref[0,f*2+e]=p
            ps.append(p); vs.append(jnp.where(m,v,zero))
        o=dot(jnp.concatenate(ps,0),jnp.concatenate(vs,0),0,0)
        mixed_ref[s,pl.ds(pl.multiple_of(h*128,128),128)]=o.astype(bf)
        return carry
    lax.fori_loop(0,FR,one,0,unroll=True)
    @pl.when(h==5)
    def _():
        mid_ref[...]+=dot(mixed_ref[0:RR,:],wo[...])
def k1(vid, mnext, wq, wk, wv, wo, gain, shift,
       qkv_ref, pt_ref, first_ref, mixed_ref, mid_ref, tok_ref):
    h=pl.program_id(0)
    @pl.when(h==0)
    def _():
        first_ref[pl.ds(RR,RP-RR),:]=jnp.zeros((RP-RR,D),bf)
        mixed_ref[pl.ds(RR,RP-RR),:]=jnp.zeros((RP-RR,D),bf)
        for f in range(FR):
            mid_ref[f*T+192:(f+1)*T,:]=jnp.zeros((T-192,D),f32)
            mid_ref[f*T:f*T+197,:]=vid[f,0].astype(f32)
            mid_ref[f*T+197:f*T+198,:]=mnext[f:f+1,:]
            x=mid_ref[f*T:(f+1)*T,:]
            tok_ref[f*T:(f+1)*T,:]=x.astype(bf)
            mu=jnp.mean(x,-1,keepdims=True); c=x-mu
            inv=lax.rsqrt(jnp.mean(c*c,-1,keepdims=True)+EPS)
            first_ref[f*T:(f+1)*T,:]=(c*inv*gain[...]+shift[...]).astype(bf)
    attend_frames(h,wq,wk,wv,wo,qkv_ref,pt_ref,first_ref,mixed_ref,mid_ref)
def call_k1(video,mnext,qkv,wo,gain,shift):
    full=lambda *s: pl.BlockSpec(s,lambda j:(0,)*len(s))
    blk=lambda *s: pl.BlockSpec((1,)+s,lambda j:(j,)+(0,)*len(s))
    specs=[full(FR,1,197,D),full(FR,D)]+[pl.BlockSpec((D,128),lambda j,o=o:(0,o*6+j)) for o in range(3)]+[full(D,D),full(1,D),full(1,D)]
    return pl.pallas_call(k1,grid=(6,),in_specs=specs,
      out_specs=[blk(RP,384),blk(12,T,T),full(RP,D),full(RP,D),full(RR,D),full(RR,D)],
      out_shape=[jax.ShapeDtypeStruct((6,RP,384),bf),jax.ShapeDtypeStruct((6,12,T,T),bf),jax.ShapeDtypeStruct((RP,D),bf),jax.ShapeDtypeStruct((RP,D),bf),jax.ShapeDtypeStruct((RR,D),f32),jax.ShapeDtypeStruct((RR,D),bf)],
      compiler_params=pltpu.CompilerParams(vmem_limit_bytes=61<<20,dimension_semantics=("arbitrary",)),
    )(video,mnext,qkv,qkv,qkv,wo,gain.reshape(1,D),shift.reshape(1,D))
def k3(vid, mnext, gmid, qkv, pt, first, mixed, wq, wk, wv, wo, gain, shift,
       gtok_ref, gf_ref, small_ref, glow, dO, dpk, wqkv):
    h=pl.program_id(0)
    @pl.when(h==0)
    def _():
        glow[pl.ds(RR,RP-RR),:]=jnp.zeros((RP-RR,D),bf)
        dpk[:,pl.ds(RR,RP-RR),:]=jnp.zeros((6,RP-RR,384),bf)
        glow[0:RR,:]=gmid[...].astype(bf)
        d=dot(glow[0:RR,:],wo[...],1,1).astype(bf)
        for i in range(6): dO[i]=d[:,i*128:(i+1)*128]
    lo=half_masks(T)
    zero=jnp.zeros((T,128),bf)
    for f in range(FR):
        s=slice(f*T,(f+1)*T)
        q=qkv[0,s,0:128]; k=qkv[0,s,128:256]; v=qkv[0,s,256:384]
        do=dO[h,s,:]
        dss=[]; ks=[]; dk=0.; dv=0.
        for e in range(2):
            m=lo if e==0 else jnp.logical_not(lo)
            doe=jnp.where(m,do,zero)
            pb=pt[0,f*2+e]
            p=pb.astype(f32)
            dp=dot(v,doe,1,1)
            delta=jnp.sum(dp*p,0,keepdims=True)
            ds=(p*(dp-delta)).astype(bf)
            dk=dk+dot(ds,jnp.where(m,q,zero))
            dv=dv+dot(pb,doe)
            dss.append(ds); ks.append(jnp.where(m,k,zero))
        dq=dot(jnp.concatenate(dss,0),jnp.concatenate(ks,0),0,0)*0.125
        dpk[h,s,0:128]=dq.astype(bf)
        dpk[h,s,128:256]=(dk*0.125).astype(bf)
        dpk[h,s,256:384]=dv.astype(bf)
    for i in range(6):
        @pl.when(h==i)
        def _():
            wqkv[:,i*128:(i+1)*128]=wq[...]; wqkv[:,D+i*128:D+(i+1)*128]=wk[...]; wqkv[:,2*D+i*128:2*D+(i+1)*128]=wv[...]
            gf_ref[0,:,384:512]=dot(mixed[...],glow[:,i*128:(i+1)*128],0,0).astype(bf)
    gf_ref[0,:,0:384]=dot(first[...],dpk[h],0,0).astype(bf)
    @pl.when(h==5)
    def _():
        dx=jnp.concatenate([dpk[i,0:RR,g*128:(g+1)*128] for g in range(3) for i in range(6)],1)
        gtok_ref[...]=dot(dx,wqkv[...],1,1)
        gg=jnp.zeros((1,D),f32); gs=jnp.zeros((1,D),f32)
        for f in range(FR):
            s=slice(f*T,(f+1)*T)
            x=jnp.concatenate([vid[f,0].astype(f32),mnext[f:f+1,:],jnp.zeros((T-198,D),f32)],0)
            mu=jnp.mean(x,-1,keepdims=True); c=x-mu
            inv=lax.rsqrt(jnp.mean(c*c,-1,keepdims=True)+EPS)
            sc=c*inv
            go=gtok_ref[s,:]
            gg=gg+jnp.sum(go*sc,0,keepdims=True); gs=gs+jnp.sum(go,0,keepdims=True)
            gsc=go*gain[...]
            gi=inv*(gsc-jnp.mean(gsc,-1,keepdims=True)-sc*jnp.mean(gsc*sc,-1,keepdims=True))
            gtok_ref[s,:]=gmid[s,:]+gi
        small_ref[0:1,:]=gg; small_ref[1:2,:]=gs
def call_k3(video,mnext,gmid,qkvs,pt,first,mixed,qkv,wo,gain):
    full=lambda *s: pl.BlockSpec(s,lambda j:(0,)*len(s))
    blk=lambda *s: pl.BlockSpec((1,)+s,lambda j:(j,)+(0,)*len(s))
    specs=[full(FR,1,197,D),full(FR,D),full(RR,D),blk(RP,384),blk(12,T,T),full(RP,D),full(RP,D)]+[pl.BlockSpec((D,128),lambda j,o=o:(0,o*6+j)) for o in range(3)]+[full(D,D),full(1,D),full(1,D)]
    return pl.pallas_call(k3,grid=(6,),in_specs=specs,
      out_specs=[full(RR,D),blk(D,512),full(8,D)],
      out_shape=[jax.ShapeDtypeStruct((RR,D),f32),jax.ShapeDtypeStruct((6,D,512),bf),jax.ShapeDtypeStruct((8,D),f32)],
      scratch_shapes=[pltpu.VMEM((RP,D),bf),pltpu.VMEM((6,RR,128),bf),pltpu.VMEM((6,RP,384),bf),pltpu.VMEM((D,3*D),bf)],
      compiler_params=pltpu.CompilerParams(vmem_limit_bytes=61<<20,dimension_semantics=("arbitrary",)),
    )(video,mnext,gmid,qkvs,pt,first,mixed,qkv,qkv,qkv,wo,gain.reshape(1,D),gain.reshape(1,D))


UNITS = 18
DENSE_UNITS = 12
STEPS = 12
LAG = (0, 1, 3, 5, 7, 9, 11, 13, 15)
ROWS = 192


def add_norm_stats(values):
    mean = jnp.mean(values, -1, keepdims=True)
    center = values - mean
    inverse = lax.rsqrt(jnp.mean(center * center, -1, keepdims=True) + EPS)
    return center * inverse, inverse


def norm_back(grad, scaled, inverse, gain):
    grad_scaled = grad * gain
    return inverse * (
        grad_scaled
        - jnp.mean(grad_scaled, -1, keepdims=True)
        - scaled * jnp.mean(grad_scaled * scaled, -1, keepdims=True)
    )


def pack_rows(values):
    return jnp.concatenate([values[:, : D // 2], values[:, D // 2 :]], 0).astype(bf)


def unpack_rows(blocks):
    wide = blocks.astype(f32)
    rows = jnp.concatenate([wide[:, :8], wide[:, 8:]], 2)
    return rows.reshape(rows.shape[0] * 8, D)


def gather_moves(B, ssem, rsem, f_at, v_at):
    me = v_at * 8 + f_at

    def move(k, src, target):
        return pltpu.make_async_remote_copy(
            src_ref=src,
            dst_ref=src,
            send_sem=ssem.at[k],
            recv_sem=rsem.at[k],
            device_id=target,
            device_id_type=pl.DeviceIdType.MESH,
        )

    def near():
        return [move(i - 1, B.at[me], (lax.rem(f_at + i, 8), v_at)) for i in range(1, 8)]

    def far():
        x, y = lax.rem(v_at, 2), lax.div(v_at, 2)
        block = B.at[pl.ds(v_at * 8, 8)]
        xo, yo = v_at + 1 - 2 * x, v_at + 2 - 4 * y
        return [move(7 + i, block, (f_at, to)) for i, to in enumerate((xo, yo, 3 - v_at))]

    return near, far


def greet(f_at, v_at):
    x, y = lax.rem(v_at, 2), lax.div(v_at, 2)
    barrier = pltpu.get_barrier_semaphore()
    others = [(lax.rem(f_at + i, 8), v_at) for i in range(1, 8)]
    others += [(f_at, to) for to in (v_at + 1 - 2 * x, v_at + 2 - 4 * y, 3 - v_at)]
    for other in others:
        pl.semaphore_signal(barrier, inc=1, device_id=other, device_id_type=pl.DeviceIdType.MESH)
    return lambda: pl.semaphore_wait(barrier, 10)


def message_rows(cls, proj, bias):
    return (dot(cls, proj) + bias).astype(bf).astype(f32)


def attend_rows(packed, mask, rows):
    lo = lax.broadcasted_iota(jnp.int32, (rows, 128), 1) < 64
    zero = jnp.zeros((rows, 128), bf)
    out, kept = [], []
    for h in range(6):
        q = packed[:, h * 128 : (h + 1) * 128] * jnp.asarray(0.125, bf)
        k = packed[:, D + h * 128 : D + (h + 1) * 128]
        v = packed[:, 2 * D + h * 128 : 2 * D + (h + 1) * 128]
        ps, vs = [], []
        for e in range(2):
            m = lo if e == 0 else jnp.logical_not(lo)
            st = jnp.where(mask, dot(k, jnp.where(m, q, zero), 1, 1), NEG)
            raised = jnp.exp(st - jnp.max(st, 0, keepdims=True))
            p = (raised * (1.0 / jnp.sum(raised, 0, keepdims=True))).astype(bf)
            ps.append(p)
            vs.append(jnp.where(m, v, zero))
        kept += ps
        out.append(dot(jnp.concatenate(ps, 0), jnp.concatenate(vs, 0), 0, 0).astype(bf))
    return jnp.concatenate(out, 1), kept


def first_kernel(
    vid, wq, wk, wv, wo, gain, shift, mproj_h, mqkv_h, mout_h, mbias, mgain, mshift,
    qkv_ref, pt_ref, first_ref, mixed_ref, mid_ref, tok_ref, mnext_ref, cls_ref,
    mproj, mqkv, mout, B, mrows, wsem, ssem, rsem,
):
    h = pl.program_id(0)
    f_at, v_at = lax.axis_index("frame"), lax.axis_index("video")
    near, far = gather_moves(B, ssem, rsem, f_at, v_at)

    def put_rows(rows, values):
        scaled, _ = add_norm_stats(values)
        first_ref[rows, :] = (scaled * gain[...] + shift[...]).astype(bf)
        tok_ref[rows, :] = values.astype(bf)

    @pl.when(h == 0)
    def _():
        loads = [
            pltpu.make_async_copy(src, dst, wsem.at[i])
            for i, (src, dst) in enumerate(((mproj_h, mproj), (mqkv_h, mqkv), (mout_h, mout)))
        ]
        arrived = greet(f_at, v_at)
        for load in loads:
            load.start()
        own = jnp.concatenate([vid[f, 0, 0:1].astype(f32) for f in range(FR)] + [jnp.zeros((8 - FR, D), f32)], 0)
        B[v_at * 8 + f_at] = pack_rows(own)
        arrived()
        sends = near()
        for send in sends:
            send.start()
        first_ref[pl.ds(RR, RP - RR), :] = jnp.zeros((RP - RR, D), bf)
        mixed_ref[pl.ds(RR, RP - RR), :] = jnp.zeros((RP - RR, D), bf)
        def begin(f, rows, carry):
            mid_ref[rows, :] = jnp.concatenate([vid[f, 0].astype(f32), jnp.zeros((T - 197, D), f32)], 0)
            rows = pl.ds(pl.multiple_of(f * T, 16), 192)
            put_rows(rows, mid_ref[rows, :])
            return carry

        frames_loop(begin, 0)
        for load in loads:
            load.wait()
        for send in sends:
            send.wait()
        for send in far():
            send.start()
        cls = unpack_rows(B[pl.ds(v_at * 8, 8)]).astype(bf)
        message = message_rows(cls, mproj[...], mbias[...])
        scaled, _ = add_norm_stats(message)
        packed = dot((scaled * mgain[...] + mshift[...]).astype(bf), mqkv[...]).astype(bf)
        same = lax.rem(lax.broadcasted_iota(jnp.int32, (64, 64), 0), 8) == lax.rem(
            lax.broadcasted_iota(jnp.int32, (64, 64), 1), 8
        )
        mixed, _ = attend_rows(packed, same, 64)
        mrows[...] = message + dot(mixed, mout[...])
        mnext_ref[...] = mrows[pl.ds(pl.multiple_of(f_at * 8, 8), 8), :]
        last_row = lax.broadcasted_iota(jnp.int32, (16, D), 0) == 5

        def finish(f, rows, carry):
            rows = pl.ds(pl.multiple_of(f * T + 192, 16), 16)
            values = jnp.where(last_row, mnext_ref[pl.ds(f, 1), :], mid_ref[rows, :])
            mid_ref[rows, :] = values
            put_rows(rows, values)
            return carry

        frames_loop(finish, 0)

    attend_frames(h, wq, wk, wv, wo, qkv_ref, pt_ref, first_ref, mixed_ref, mid_ref)

    @pl.when(h == 5)
    def _():
        for send in far():
            send.wait()
        cls_ref[...] = B[...]


def call_first(video, qkv, wo, gain, shift, mproj, mbias, mgain, mshift, mqkv, mout):
    one = pl.Buffered(1)
    full = lambda *s: pl.BlockSpec(s, lambda j: (0,) * len(s), pipeline_mode=one)
    keep = lambda *s: pl.BlockSpec(s, lambda j: (0,) * len(s))
    blk = lambda *s: pl.BlockSpec((1,) + s, lambda j: (j,) + (0,) * len(s))
    hbm = pl.BlockSpec(memory_space=pl.ANY)
    specs = [full(FR, 1, 197, D)] + [pl.BlockSpec((D, 128), lambda j, o=o: (0, o * 6 + j)) for o in range(3)]
    specs += [full(D, D), full(D), full(D), hbm, hbm, hbm, full(D), full(D), full(D)]
    shape = jax.ShapeDtypeStruct
    dma = pltpu.SemaphoreType.DMA
    return pl.pallas_call(
        first_kernel,
        grid=(6,),
        in_specs=specs,
        out_specs=[
            blk(RP, 384), blk(12, T, T), keep(RP, D), keep(RP, D), keep(RR, D), keep(RR, D), keep(8, D),
            keep(32, 16, D // 2),
        ],
        out_shape=[
            shape((6, RP, 384), bf),
            shape((6, 12, T, T), bf),
            shape((RP, D), bf),
            shape((RP, D), bf),
            shape((RR, D), f32),
            shape((RR, D), bf),
            shape((8, D), f32),
            shape((32, 16, D // 2), bf),
        ],
        scratch_shapes=[
            pltpu.VMEM((D, D), bf),
            pltpu.VMEM((D, 3 * D), bf),
            pltpu.VMEM((D, D), bf),
            pltpu.VMEM((32, 16, D // 2), bf),
            pltpu.VMEM((64, D), f32),
            dma((3,)),
            dma((10,)),
            dma((10,)),
        ],
        compiler_params=pltpu.CompilerParams(
            vmem_limit_bytes=VMEM_LIMIT, dimension_semantics=("arbitrary",), collective_id=2, has_side_effects=True
        ),
    )(video, qkv, qkv, qkv, wo, gain, shift, mproj, mqkv, mout, mbias, mgain, mshift)


MROWS = 256


def rows_back(MP, PR, GM, GP, heads):
    lo = lax.broadcasted_iota(jnp.int32, (MROWS, 128), 1) < 64
    zero = jnp.zeros((MROWS, 128), bf)
    for h in heads:
        q, k, v = (MP[:, o * D + h * 128 : o * D + (h + 1) * 128] for o in range(3))
        do = GM[:, h * 128 : (h + 1) * 128]
        dss, ks, dk, dv = [], [], 0.0, 0.0
        for e in range(2):
            m = lo if e == 0 else jnp.logical_not(lo)
            doe = jnp.where(m, do, zero)
            pb = PR[2 * h + e]
            p = pb.astype(f32)
            dp = dot(v, doe, 1, 1)
            ds = (p * (dp - jnp.sum(dp * p, 0, keepdims=True))).astype(bf)
            dk = dk + dot(ds, jnp.where(m, q, zero))
            dv = dv + dot(pb, doe)
            dss.append(ds)
            ks.append(jnp.where(m, k, zero))
        dq = dot(jnp.concatenate(dss, 0), jnp.concatenate(ks, 0), 0, 0) * 0.125
        for o, part in enumerate((dq, dk * 0.125, dv)):
            GP[:, o * D + h * 128 : o * D + (h + 1) * 128] = part.astype(bf)


def frames_loop(body, carry):
    def step(f, carry):
        return body(f, pl.ds(pl.multiple_of(f * T, 16), T), carry)

    return lax.fori_loop(0, FR, step, carry)


def exchange(tick, where, U, RA, RB, RC, RD, RE, F, ssem, rsem, fsem, F_out):
    c, x, y, z0, z1, core, xn, yn, zn, zf = where

    def at(lag_dense, lag_frame, body):
        dense = tick - lag_dense
        late = tick - lag_frame - 13
        step = lax.div(jnp.maximum(late, 0), 2)
        is_dense = jnp.logical_and(dense >= 0, dense < 12)
        is_frame = jnp.logical_and(jnp.logical_and(late >= 0, lax.rem(jnp.maximum(late, 0), 2) == 0), step < 6)

        @pl.when(is_dense)
        def _():
            body(jnp.clip(dense, 0, 11))

        @pl.when(is_frame)
        def _():
            body(12 + jnp.minimum(step, 5))

    def move(g, k, src, dst, target):
        return pltpu.make_async_remote_copy(
            src_ref=src,
            dst_ref=dst,
            send_sem=ssem.at[g, k],
            recv_sem=rsem.at[g, k],
            device_id=target,
            device_id_type=pl.DeviceIdType.MESH,
        )

    def a(g):
        return move(g, 0, U.at[lax.rem(g, 2), :, :, pl.ds(2 * (1 - c), 2)], RA.at[lax.rem(g, 6)], core)

    def b0(g):
        return move(g, 1, RA.at[lax.rem(g, 6), :, 1 - x, 0], RB.at[lax.rem(g, 8), 0], xn)

    def b1(g):
        return move(g, 2, RA.at[lax.rem(g, 6), 1 - y, :, 1], RB.at[lax.rem(g, 8), 1], yn)

    def c0(g):
        return move(g, 3, RB.at[lax.rem(g, 8), 0, 1 - y], RC.at[lax.rem(g, 8), 0], yn)

    def c1(g):
        return move(g, 4, RB.at[lax.rem(g, 8), 1, 1 - x], RC.at[lax.rem(g, 8), 1], xn)

    def d1(g):
        return move(g, 5, RC.at[lax.rem(g, 8), 1 - z0], RD.at[g], zn)

    def d2(g):
        return move(g, 6, RD.at[g, pl.ds((1 - z1) * 96, 96)], RE.at[g], zf)

    def e2(g):
        piece = F.at[g, 2 * c + z0, pl.ds(z1 * 96, 96)]
        return move(g, 7, piece, piece, zf)

    def e1(g):
        piece = F.at[g, 2 * c + z0]
        return move(g, 8, piece, piece, zn)

    def last(g):
        piece = F.at[g, pl.ds(2 * c, 2)]
        return move(g, 9, piece, piece, core)

    def on_done(g):
        last(g).wait()
        pltpu.make_async_copy(F.at[g], F_out.at[g], fsem.at[g]).start()

    def on_last(g):
        e1(g).wait()
        last(g).start()

    def on_e1(g):
        e2(g).wait()
        e1(g).start()

    def on_e2(g):
        d2(g).wait()
        own = pl.ds(z1 * 96, 96)
        F[g, 2 * c + z0, own] = RE[g] + RD[g, own]
        e2(g).start()

    def on_d2(g):
        d1(g).wait()
        RD[g] = RD[g] + RC[lax.rem(g, 8), z0]
        d2(g).start()

    def on_d1(g):
        c0(g).wait()
        c1(g).wait()
        RC[lax.rem(g, 8), 0] = RC[lax.rem(g, 8), 0] + RB[lax.rem(g, 8), 0, y]
        RC[lax.rem(g, 8), 1] = RC[lax.rem(g, 8), 1] + RB[lax.rem(g, 8), 1, x]
        d1(g).start()

    def on_c(g):
        b0(g).wait()
        b1(g).wait()
        RB[lax.rem(g, 8), 0] = RB[lax.rem(g, 8), 0] + RA[lax.rem(g, 6), :, x, 0]
        RB[lax.rem(g, 8), 1] = RB[lax.rem(g, 8), 1] + RA[lax.rem(g, 6), y, :, 1]
        c0(g).start()
        c1(g).start()

    def on_b(g):
        a(g).wait()
        RA[lax.rem(g, 6)] = RA[lax.rem(g, 6)] + U[lax.rem(g, 2), :, :, pl.ds(2 * c, 2)]
        b0(g).start()
        b1(g).start()

    def on_a(g):
        a(g).start()

    bodies = (on_a, on_b, on_c, on_d1, on_d2, on_e2, on_e1, on_last, on_done)
    for lag, body in zip(LAG, bodies):
        at(lag, lag, body)


def main_kernel(
    mid, cot, live, din0, din1, din2, din3, do0, do1, do2, do3, bin_, bout, gain2, shift2,
    qkv, pt, wq, wk, wv, first_hbm, mixed_hbm, wo_hbm, tok_hbm, mnext, gain1,
    mproj_hbm, mqkv_hbm, mout_hbm, cls_hbm, mbias, mgain, mshift,
    out_hbm, gt_hbm, F_out, gp_out, lr_out, edge_out,
    sec, G, act, dinn, oacc, gsec, CB, first, mixed, wo, dpk,
    U, RA, RB, RC, RD, RE, F, BI, SB, NB, AD, AN, AS, mv, CLS, MP, PR, MS, GP, GM, LR, EDGE, HELD, ssem, rsem, fsem, lsem, adsem, adrem, ansem, anrem, assem, asrem,
):
    t = pl.program_id(0)
    f_at, v_at = lax.axis_index("frame"), lax.axis_index("video")
    c, z = lax.rem(f_at, 2), lax.div(f_at, 2)
    x, y = lax.rem(v_at, 2), lax.div(v_at, 2)
    z0, z1 = lax.rem(z, 2), lax.div(z, 2)
    core = (f_at + 1 - 2 * c, v_at)
    xn = (f_at, v_at + 1 - 2 * x)
    yn = (f_at, v_at + 2 - 4 * y)
    zn = (f_at + 2 - 4 * z0, v_at)
    zf = (f_at + 4 - 8 * z1, v_at)
    where = (c, x, y, z0, z1, core, xn, yn, zn, zf)

    small_near, small_far = gather_moves(AD, adsem, adrem, f_at, v_at)
    next_near, next_far = gather_moves(AN, ansem, anrem, f_at, v_at)
    sums_near, sums_far = gather_moves(AS, assem, asrem, f_at, v_at)

    def tick(n):
        exchange(n, where, U, RA, RB, RC, RD, RE, F, ssem, rsem, fsem, F_out)

    def fetch(k):
        src, dst = (
            (first_hbm, first),
            (mixed_hbm, mixed),
            (wo_hbm, wo),
            (tok_hbm, act.at[pl.ds(0, RR)]),
            (CB, out_hbm),
            (sec.at[pl.ds(0, RR)], gt_hbm),
            (cot, CB),
            (GP, gp_out),
            (LR, lr_out),
            (EDGE, edge_out),
            (mproj_hbm, G.at[pl.ds(0, D)]),
            (mqkv_hbm.at[:, pl.ds(0, D)], first.at[pl.ds(0, D)]),
            (mqkv_hbm.at[:, pl.ds(D, D)], mixed.at[pl.ds(0, D)]),
            (mqkv_hbm.at[:, pl.ds(2 * D, D)], mv),
            (mout_hbm, wo),
            (cls_hbm, CLS),
        )[k]
        return pltpu.make_async_copy(src, dst, lsem.at[k])

    tail = pl.ds(RR, RP - RR)

    @pl.when(t == 0)
    def _():
        fetch(6).start()
        arrived = greet(f_at, v_at)
        for k in range(3):
            fetch(k).start()
        sec[tail, :] = jnp.zeros((RP - RR, D), bf)
        G[tail, :] = jnp.zeros((RP - RR, D), bf)
        act[tail, :] = jnp.zeros((RP - RR, D), bf)
        dinn[tail, :] = jnp.zeros((RP - RR, 512), bf)
        dpk[tail, :] = jnp.zeros((RP - RR, 384), bf)
        SB[...] = jnp.zeros((8, D), f32)
        BI[...] = bin_[...].reshape(1, 4 * D)
        def begin(f, rows, carry):
            values = mid[rows, :]
            scaled, _ = add_norm_stats(values)
            sec[rows, :] = (scaled * gain2[...] + shift2[...]).astype(bf)
            oacc[rows, :] = values + bout[...]
            gsec[rows, :] = jnp.zeros((T, D), f32)
            return carry

        frames_loop(begin, 0)
        fetch(6).wait()

        def weigh(f, rows, total):
            grad = CB[f, 0].astype(f32) * live[f].astype(f32)
            G[rows, :] = jnp.concatenate([grad, jnp.zeros((T - 198, D), f32)], 0).astype(bf)
            return total + jnp.sum(grad, 0, keepdims=True)

        SB[4:5, :] = frames_loop(weigh, jnp.zeros((1, D), f32))
        arrived()

    din = lambda: jnp.concatenate([din0[...], din1[...], din2[...], din3[...]], 1)
    dout = lambda: jnp.concatenate([do0[...], do1[...], do2[...], do3[...]], 0)

    def put(slot, index, block):
        q, b = index
        U[slot, q // 2, q % 2, b] = block.astype(bf)

    @pl.when(t < 6)
    def _():
        w_in, w_out = din(), dout()
        bias = jnp.concatenate([BI[:, pl.ds(pl.multiple_of(q * D + t * 128, 128), 128)] for q in range(4)], 1)
        sums = jnp.zeros((1, 512), f32)
        MB = 416
        for r in range(RR // MB):
            s = slice(r * MB, (r + 1) * MB)
            inner = dot(sec[s, :], w_in) + bias
            ga = dot(G[s, :], w_out, 1, 1)
            sg = 0.5 * jnp.tanh(0.851 * inner) + 0.5
            ac = inner * sg
            act[s, 0:512] = ac.astype(bf)
            di = ga * (sg + 1.702 * ac * (1.0 - sg))
            sums = sums + jnp.sum(di, 0, keepdims=True)
            dinn[s, :] = di.astype(bf)
        for b in range(4):
            SB[b : b + 1, pl.ds(pl.multiple_of(t * 128, 128), 128)] = sums[:, b * 128 : (b + 1) * 128]
        part = dot(G[...], act[:, 0:512], 0, 0)
        for q in range(4):
            for b in range(4):
                put(0, (q, b), part[b * ROWS : (b + 1) * ROWS, q * 128 : (q + 1) * 128])

    lo = lax.broadcasted_iota(jnp.int32, (T, 128), 1) < 64
    zero = jnp.zeros((T, 128), bf)
    head = jnp.maximum(t - 6, 0)
    lanes = pl.ds(pl.multiple_of(head * 128, 128), 128)

    def attend_back(first_frame, count):
        def one(f, carry):
            s = pl.ds(pl.multiple_of(f * T, 16), T)
            q, k, v = qkv[0, s, 0:128], qkv[0, s, 128:256], qkv[0, s, 256:384]
            do = G[s, lanes]
            dss, ks, dk, dv = [], [], 0.0, 0.0
            for e in range(2):
                m = lo if e == 0 else jnp.logical_not(lo)
                doe = jnp.where(m, do, zero)
                pb = pt[0, f * 2 + e]
                p = pb.astype(f32)
                dp = dot(v, doe, 1, 1)
                ds = (p * (dp - jnp.sum(dp * p, 0, keepdims=True))).astype(bf)
                dk = dk + dot(ds, jnp.where(m, q, zero))
                dv = dv + dot(pb, doe)
                dss.append(ds)
                ks.append(jnp.where(m, k, zero))
            dq = dot(jnp.concatenate(dss, 0), jnp.concatenate(ks, 0), 0, 0) * 0.125
            dpk[s, 0:128] = dq.astype(bf)
            dpk[s, 128:256] = (dk * 0.125).astype(bf)
            dpk[s, 256:384] = dv.astype(bf)
            return carry

        lax.fori_loop(first_frame, first_frame + count, one, 0, unroll=True)

    @pl.when(t == 6)
    def _():
        def turn(f, s, sums):
            CB[f, 0] = oacc[s, :][:198].astype(bf)
            scaled, inverse = add_norm_stats(mid[s, :])
            grad = gsec[s, :]
            total = G[s, :].astype(f32) + norm_back(grad, scaled, inverse, gain2[...])
            gsec[s, :] = total
            sec[s, :] = total.astype(bf)
            oacc[s, :] = jnp.zeros((T, D), f32)
            return sums[0] + jnp.sum(grad * scaled, 0, keepdims=True), sums[1] + jnp.sum(grad, 0, keepdims=True)

        gg, gs = frames_loop(turn, (jnp.zeros((1, D), f32), jnp.zeros((1, D), f32)))
        SB[5:6, :] = gg
        SB[6:7, :] = gs
        AD[v_at * 8 + f_at] = pack_rows(SB[...])
        for send in small_near():
            send.start()
        fetch(4).start()
        fetch(3).start()
        for k in range(3):
            fetch(k).wait()
        G[0:RR, :] = dot(sec[0:RR, :], wo[...], 1, 1).astype(bf)

    @pl.when(t >= 6)
    def _():
        attend_back(0, 3)

    tick(2 * t)

    @pl.when(t < 6)
    def _():
        w_in, w_out = din(), dout()
        part = dot(sec[...], dinn[...], 0, 0)
        for q in range(4):
            for b in range(4):
                put(1, (q, b), part[q * ROWS : (q + 1) * ROWS, b * 128 : (b + 1) * 128])
        oacc[...] += dot(act[0:RR, 0:512], w_out)
        gsec[...] += dot(dinn[0:RR, :], w_in, 1, 1)

    @pl.when(t >= 6)
    def _():
        attend_back(3, 3)
        slot = lax.rem(head, 2)
        part = dot(first[...], dpk[...], 0, 0)
        for q in range(4):
            for b in range(3):
                put(slot, (q, b), part[q * ROWS : (q + 1) * ROWS, b * 128 : (b + 1) * 128])
        part = dot(mixed[...], sec[:, lanes], 0, 0)
        for q in range(4):
            put(slot, (q, 3), part[q * ROWS : (q + 1) * ROWS, :])

    tick(2 * t + 1)

    @pl.when(t >= 6)
    def _():
        w = jnp.concatenate([wq[...], wk[...], wv[...]], 1)
        oacc[...] += dot(dpk[0:RR, :], w, 1, 1)

    @pl.when(t == 8)
    def _():
        for k in (13, 14, 15):
            fetch(k).start()
        for send in small_near():
            send.wait()
        for send in small_far():
            send.start()

    @pl.when(t == STEPS - 1)
    def _():
        for k in (10, 11, 12):
            fetch(k).start()
        fetch(3).wait()
        last_row = lax.broadcasted_iota(jnp.int32, (16, D), 0) == 5

        def next_row(f, s, carry):
            s = pl.ds(pl.multiple_of(f * T + 192, 16), 16)
            values = jnp.where(last_row, mnext[pl.ds(f, 1), :], act[s, :].astype(f32))
            scaled, inverse = add_norm_stats(values)
            total = gsec[s, :] + norm_back(oacc[s, :], scaled, inverse, gain1[...])
            NB[pl.ds(f, 1), :] = total[5:6]
            return carry

        NB[...] = jnp.zeros((8, D), f32)
        frames_loop(next_row, 0)
        AN[v_at * 8 + f_at] = pack_rows(NB[...])
        for send in next_near():
            send.start()
        tick(24)

        def end(f, s, sums):
            values = act[s, :].astype(f32)
            low = jnp.where(last_row, mnext[pl.ds(f, 1), :], values[192:])
            scaled, inverse = add_norm_stats(jnp.concatenate([values[:192], low], 0))
            grad = oacc[s, :]
            total = gsec[s, :] + norm_back(grad, scaled, inverse, gain1[...])
            sec[s, :] = total.astype(bf)
            return sums[0] + jnp.sum(grad * scaled, 0, keepdims=True), sums[1] + jnp.sum(grad, 0, keepdims=True)

        gg, gs = frames_loop(end, (jnp.zeros((1, D), f32), jnp.zeros((1, D), f32)))
        fetch(5).start()
        NB[0:1, :] = gg
        NB[1:2, :] = gs
        AS[v_at * 8 + f_at] = pack_rows(NB[...])
        for send in sums_near():
            send.start()
        tick(25)
        tick(26)
        for send in next_near():
            send.wait()
        for send in next_far():
            send.start()
        for k in range(10, 16):
            fetch(k).wait()
        MS[...] = message_rows(unpack_rows(CLS[...]).astype(bf), G[0:D, :], mbias[...])
        scaled, _ = add_norm_stats(MS[...])
        LR[0] = (scaled * mgain[...] + mshift[...]).astype(bf)
        for o, ref in enumerate((first, mixed, mv)):
            MP[:, o * D : (o + 1) * D] = dot(LR[0], ref[0:D, :]).astype(bf)
        tick(28)
        for send in sums_near():
            send.wait()
        for send in sums_far():
            send.start()
        ik = lax.broadcasted_iota(jnp.int32, (MROWS, MROWS), 0)
        iq = lax.broadcasted_iota(jnp.int32, (MROWS, MROWS), 1)
        same = jnp.logical_and(lax.rem(ik, 8) == lax.rem(iq, 8), lax.div(ik, 64) == lax.div(iq, 64))
        mixed_rows, probs = attend_rows(MP[...], same, MROWS)
        LR[1] = mixed_rows
        for i, p in enumerate(probs):
            PR[i] = p
        tick(30)
        for send in next_far():
            send.wait()
        kind = lax.rem(lax.broadcasted_iota(jnp.int32, (MROWS, D), 0), 8)
        LR[2] = jnp.where(kind < 6, unpack_rows(AN[...]), 0.0).astype(bf)
        GM[...] = dot(LR[2], wo[...], 1, 1).astype(bf)
        rows_back(MP, PR, GM, GP, range(0, 3))
        tick(32)
        rows_back(MP, PR, GM, GP, range(3, 6))
        tick(34)
        grad = dot(GP[:, 0:D], first[0:D, :], 1, 1) + dot(GP[:, D : 2 * D], mixed[0:D, :], 1, 1)
        grad = grad + dot(GP[:, 2 * D : 3 * D], mv[...], 1, 1)
        scaled, inverse = add_norm_stats(MS[...])
        total = LR[2].astype(f32) + norm_back(grad, scaled, inverse, mgain[...])
        LR[3] = total.astype(bf)
        fetch(7).start()
        fetch(8).start()
        tick(36)
        HELD[...] = dot(LR[3], G[0:D, :], 1, 1)
        EDGE[0:8, :] = HELD[pl.ds(pl.multiple_of((v_at * 8 + f_at) * 8, 8), 8), :]
        lines = [jnp.sum(a, 0, keepdims=True) for a in (total, grad * scaled, grad)]
        for send in sums_far():
            send.wait()
        for send in small_far():
            send.wait()
        ends = jnp.sum(unpack_rows(AS[...]).reshape(32, 8, D), 0)
        small = jnp.sum(unpack_rows(AD[...]).reshape(32, 8, D), 0)
        lines += [ends[0:1], ends[1:2], small[5:6], small[6:7], small[4:5]]
        for i, line in enumerate(lines):
            EDGE[8 + i : 9 + i, :] = line
        EDGE[16:24, :] = small
        fetch(9).start()
        tick(38)

        def finish(g, carry):
            pltpu.make_async_copy(F.at[g], F_out.at[g], fsem.at[g]).wait()
            return carry

        lax.fori_loop(0, UNITS, finish, 0)
        for k in (4, 5, 7, 8, 9):
            fetch(k).wait()


def call_main(
    mid, cot, live, din, dout, bin_, bout, gain2, shift2, qkv, pt, wqkv, first, mixed, wo, tok, mnext, gain1,
    mproj, mqkv, mout, cls, mbias, mgain, mshift,
):
    one = pl.Buffered(1)
    full = lambda *s: pl.BlockSpec(s, lambda t: (0,) * len(s), pipeline_mode=one)
    hbm = pl.BlockSpec(memory_space=pl.ANY)
    dense = lambda t: jnp.minimum(t, 5)
    head = lambda t: jnp.maximum(t - 6, 0)
    specs = [full(RR, D), hbm, pl.BlockSpec(memory_space=pltpu.SMEM)]
    specs += [pl.BlockSpec((D, 128), lambda t, q=q: (0, q * 6 + dense(t))) for q in range(4)]
    specs += [pl.BlockSpec((128, D), lambda t, q=q: (q * 6 + dense(t), 0)) for q in range(4)]
    specs += [full(bin_.shape[0]), full(D), full(D), full(D)]
    specs += [pl.BlockSpec((1, RP, 384), lambda t: (head(t), 0, 0)), pl.BlockSpec((1, 12, T, T), lambda t: (head(t), 0, 0, 0))]
    specs += [pl.BlockSpec((D, 128), lambda t, o=o: (0, o * 6 + head(t))) for o in range(3)]
    specs += [hbm, hbm, hbm, hbm, full(8, D), full(D)] + [hbm] * 4 + [full(D)] * 3
    shape = jax.ShapeDtypeStruct
    dma = pltpu.SemaphoreType.DMA
    return pl.pallas_call(
        main_kernel,
        grid=(STEPS,),
        in_specs=specs,
        out_specs=[hbm] * 6,
        out_shape=[
            shape((FR, 1, 198, D), bf),
            shape((RR, D), bf),
            shape((UNITS, 4, ROWS, 128), bf),
            shape((MROWS, 3 * D), bf),
            shape((4, MROWS, D), bf),
            shape((24, D), f32),
        ],
        scratch_shapes=[
            pltpu.VMEM((RP, D), bf),
            pltpu.VMEM((RP, D), bf),
            pltpu.VMEM((RP, D), bf),
            pltpu.VMEM((RP, 512), bf),
            pltpu.VMEM((RR, D), f32),
            pltpu.VMEM((RR, D), f32),
            pltpu.VMEM((FR, 1, 198, D), bf),
            pltpu.VMEM((RP, D), bf),
            pltpu.VMEM((RP, D), bf),
            pltpu.VMEM((D, D), bf),
            pltpu.VMEM((RP, 384), bf),
            pltpu.VMEM((2, 2, 2, 4, ROWS, 128), bf),
            pltpu.VMEM((6, 2, 2, 2, ROWS, 128), bf),
            pltpu.VMEM((8, 2, 2, ROWS, 128), bf),
            pltpu.VMEM((8, 2, ROWS, 128), bf),
            pltpu.VMEM((UNITS, ROWS, 128), bf),
            pltpu.VMEM((UNITS, ROWS // 2, 128), bf),
            pltpu.VMEM((UNITS, 4, ROWS, 128), bf),
            pltpu.VMEM((1, 4 * D), f32),
            pltpu.VMEM((8, D), f32),
            pltpu.VMEM((8, D), f32),
            pltpu.VMEM((32, 16, D // 2), bf),
            pltpu.VMEM((32, 16, D // 2), bf),
            pltpu.VMEM((32, 16, D // 2), bf),
            pltpu.VMEM((D, D), bf),
            pltpu.VMEM((32, 16, D // 2), bf),
            pltpu.VMEM((MROWS, 3 * D), bf),
            pltpu.VMEM((12, MROWS, MROWS), bf),
            pltpu.VMEM((MROWS, D), f32),
            pltpu.VMEM((MROWS, 3 * D), bf),
            pltpu.VMEM((MROWS, D), bf),
            pltpu.VMEM((4, MROWS, D), bf),
            pltpu.VMEM((24, D), f32),
            pltpu.VMEM((MROWS, D), f32),
            dma((UNITS, 10)),
            dma((UNITS, 10)),
            dma((UNITS,)),
            dma((16,)),
            dma((10,)),
            dma((10,)),
            dma((10,)),
            dma((10,)),
            dma((10,)),
            dma((10,)),
        ],
        compiler_params=pltpu.CompilerParams(
            vmem_limit_bytes=VMEM_LIMIT,
            dimension_semantics=("arbitrary",),
            collective_id=1,
            has_side_effects=True,
        ),
    )(mid, cot, live, din, din, din, din, dout, dout, dout, dout, bin_, bout, gain2, shift2,
      qkv, pt, wqkv, wqkv, wqkv, first, mixed, wo, tok, mnext, gain1, mproj, mqkv, mout, cls, mbias, mgain, mshift)


def final_kernel(
    F, gt, cls_blocks, gpacked, lr, edge, out_in,
    out, gvid, gproj, gmqkv, gmout, gfqkv, gfout, gdin, gdout, *rest,
):
    vecs, bias_in = rest[:8], rest[8]
    v_at = lax.axis_index("video")
    out[...] = out_in[...]

    def pick(parts):
        return jnp.where(v_at == 0, parts[0], jnp.where(v_at == 1, parts[1], jnp.where(v_at == 2, parts[2], parts[3])))

    def mine(values):
        return pick([values[:, i * ROWS : (i + 1) * ROWS] for i in range(4)])

    gproj[...] = dot(mine(unpack_rows(cls_blocks[...]).astype(bf)), lr[3], 0, 0)
    gmqkv[...] = dot(mine(lr[0]), gpacked[...], 0, 0)
    gmout[...] = dot(mine(lr[1]), lr[2], 0, 0)
    picked = mine(edge[8:16, :])
    for i, ref in enumerate(vecs):
        ref[...] = picked[i]
    bias_in[...] = pick([edge[16 + i : 17 + i, :] for i in range(4)])[0]
    for f in range(FR):
        gvid[f, 0] = gt[f * T : (f + 1) * T, :][:197]
        gvid[f, 0, 0:1] = (gt[f * T : f * T + 16, :].astype(f32)[0:1] + edge[f : f + 1, :]).astype(bf)
    for j in range(6):
        for b in range(4):
            at = b * D + j * 128
            gdin[:, at : at + 128] = F[2 * j + 1, b].astype(f32)
            gdout[j * 128 : (j + 1) * 128, b * ROWS : (b + 1) * ROWS] = F[2 * j, b].astype(f32).T
            if b < 3:
                gfqkv[:, at : at + 128] = F[12 + j, b].astype(f32)
            else:
                gfout[:, j * 128 : (j + 1) * 128] = F[12 + j, b].astype(f32)


def call_final(F, gt, cls_blocks, gpacked, lr, edge, output):
    vm = pl.BlockSpec(memory_space=pltpu.VMEM)
    shape = jax.ShapeDtypeStruct
    return pl.pallas_call(
        final_kernel,
        in_specs=[vm] * 7,
        out_specs=[vm] * 18,
        out_shape=[
            shape((FR, 1, 198, D), bf),
            shape((FR, 1, 197, D), bf),
            shape((ROWS, D), f32),
            shape((ROWS, 3 * D), f32),
            shape((ROWS, D), f32),
            shape((ROWS, 3 * D), f32),
            shape((ROWS, D), f32),
            shape((ROWS, 4 * D), f32),
            shape((4 * ROWS, D), f32),
        ]
        + [shape((ROWS,), f32)] * 8
        + [shape((D,), f32)],
        compiler_params=pltpu.CompilerParams(vmem_limit_bytes=VMEM_LIMIT),
    )(F, gt, cls_blocks, gpacked, lr, edge, output)


def column_sum(values):
    return jnp.sum(values.reshape(-1, values.shape[-1]), axis=0)


def matmul(left, right):
    return jnp.dot(left, right, preferred_element_type=f32)


def back_matmul(grad_low, weight):
    return lax.dot_general(grad_low, weight, (((grad_low.ndim - 1,), (1,)), ((), ())), preferred_element_type=f32)


def weight_grad(inputs_low, grad_low):
    left = inputs_low.reshape(-1, inputs_low.shape[-1])
    right = grad_low.reshape(-1, grad_low.shape[-1])
    return lax.dot_general(left, right, (((0,), (0,)), ((), ())), preferred_element_type=f32)


def norm_forward(values, gain, shift):
    center = values - jnp.mean(values, axis=-1, keepdims=True)
    inverse = lax.rsqrt(jnp.mean(center * center, axis=-1, keepdims=True) + EPS)
    scaled = center * inverse
    return (scaled * gain + shift, scaled, inverse)


def norm_backward(grad_out, scaled, inverse, gain):
    grad_scaled = grad_out * gain
    grad_in = inverse * (
        grad_scaled
        - jnp.mean(grad_scaled, axis=-1, keepdims=True)
        - scaled * jnp.mean(grad_scaled * scaled, axis=-1, keepdims=True)
    )
    return (grad_in, column_sum(grad_out * scaled), column_sum(grad_out))


def split_heads(values):
    return values.reshape(values.shape[:-1] + (HEADS, HEAD_DIM))


def attend_forward(query_rows, key_rows, value_rows):
    scores = jnp.einsum("bqhd,bkhd->bhqk", query_rows, key_rows, preferred_element_type=f32) * 0.125
    largest = jnp.max(scores, axis=-1, keepdims=True)
    raised = jnp.exp(scores - largest)
    total = jnp.sum(raised, axis=-1, keepdims=True)
    probs_low = (raised / total).astype(bf)
    mixed = jnp.einsum("bhqk,bkhd->bqhd", probs_low, value_rows, preferred_element_type=f32)
    return (mixed, largest + jnp.log(total))


def attend_backward(query_rows, key_rows, value_rows, log_total, grad_mixed):
    scores = jnp.einsum("bqhd,bkhd->bhqk", query_rows, key_rows, preferred_element_type=f32) * 0.125
    probs = jnp.exp(scores - log_total)
    grad_probs = jnp.einsum("bqhd,bkhd->bhqk", grad_mixed, value_rows, preferred_element_type=f32)
    grad_scores = probs * (grad_probs - jnp.sum(grad_probs * probs, axis=-1, keepdims=True))
    grad_low = grad_scores.astype(bf)
    grad_query = jnp.einsum("bhqk,bkhd->bqhd", grad_low, key_rows, preferred_element_type=f32) * 0.125
    grad_key = jnp.einsum("bhqk,bqhd->bkhd", grad_low, query_rows, preferred_element_type=f32) * 0.125
    grad_value = jnp.einsum("bhqk,bqhd->bkhd", probs.astype(bf), grad_mixed, preferred_element_type=f32)
    return (grad_query, grad_key, grad_value)


def message_forward(video, message_proj, message_bias, message_gain, message_shift, message_qkv, message_out):
    width = video.shape[-1]
    batch, frames_local = video.shape[:2]
    class_rows = video[:, :, 0, :]
    message = (matmul(class_rows, message_proj) + message_bias).astype(bf)
    message_wide = message.astype(f32)
    normed_own, scaled_own, inverse_own = norm_forward(message_wide, message_gain, message_shift)
    normed_low = normed_own.astype(bf)
    everyone = lax.all_gather(message, "frame", axis=1, tiled=True)
    normed_all = norm_forward(everyone.astype(f32), message_gain, message_shift)[0]
    key_value = matmul(normed_all.astype(bf), message_qkv[:, width:]).astype(bf)
    query = split_heads(matmul(normed_low, message_qkv[:, :width]).astype(bf))
    key = split_heads(key_value[..., :width])
    value = split_heads(key_value[..., width:])
    mixed, total = attend_forward(query, key, value)
    mixed_low = mixed.reshape(batch, frames_local, width).astype(bf)
    message_next = message_wide + matmul(mixed_low, message_out)
    return message_next, (class_rows, normed_low, scaled_own, inverse_own, query, key, value, mixed_low, total)


def message_backward(kept, grad_next, message_proj, message_gain, message_qkv, message_out):
    class_rows, normed_low, scaled_own, inverse_own, query, key, value, mixed_low, total = kept
    batch, frames_local, width = grad_next.shape
    frames_all = key.shape[1]
    grad_next_low = grad_next.astype(bf)
    grad_mixed = split_heads(back_matmul(grad_next_low, message_out).astype(bf))
    grad_q, grad_k, grad_v = attend_backward(query, key, value, total, grad_mixed)
    key_value_grad = jnp.concatenate(
        [grad_k.reshape(batch, frames_all, width), grad_v.reshape(batch, frames_all, width)], axis=-1
    )
    own = lax.psum_scatter(key_value_grad.astype(bf), "frame", scatter_dimension=1, tiled=True)
    packed = jnp.concatenate([grad_q.reshape(batch, frames_local, width).astype(bf), own], axis=-1)
    grad_in, grad_gain, grad_shift = norm_backward(
        back_matmul(packed, message_qkv), scaled_own, inverse_own, message_gain
    )
    grad_message = grad_next + grad_in
    grad_message_low = grad_message.astype(bf)
    grad_class = back_matmul(grad_message_low, message_proj)
    rows = jnp.concatenate([class_rows, normed_low, mixed_low, grad_message_low, packed, grad_next_low], axis=-1)
    rows = rows.reshape(batch * frames_local, -1)
    return grad_class, rows, column_sum(grad_message), grad_gain, grad_shift


def reduced_inside(
    video, video_live, cotangent, message_proj, message_bias, message_gain, message_shift, message_qkv,
    message_out, frame_gain, frame_shift, frame_qkv, frame_out, dense_gain, dense_shift, dense_in,
    dense_in_bias, dense_out, dense_out_bias,
):
    packed, probs, first, mixed, middle, tokens, next_rows, class_blocks = call_first(
        video, frame_qkv, frame_out, frame_gain, frame_shift,
        message_proj, message_bias, message_gain, message_shift, message_qkv, message_out,
    )
    output, grad_rows, reduced, grad_packed, sides, edge = call_main(
        middle, cotangent, video_live, dense_in, dense_out, dense_in_bias, dense_out_bias, dense_gain, dense_shift,
        packed, probs, frame_qkv, first, mixed, frame_out, tokens, next_rows, frame_gain,
        message_proj, message_qkv, message_out, class_blocks, message_bias, message_gain, message_shift,
    )
    output, grad_input, g_proj, g_mqkv, g_mout, g_fqkv, g_fout, g_in, g_out, *lines = call_final(
        reduced, grad_rows, class_blocks, grad_packed, sides, edge, output
    )
    return (
        output, grad_input, g_proj, lines[0], lines[1], lines[2], g_mqkv, g_mout, lines[3], lines[4], g_fqkv, g_fout,
        lines[5], lines[6], g_in, lines[8], g_out, lines[7],
    )


def local(
    video,
    video_live,
    cotangent,
    message_proj,
    message_bias,
    message_gain,
    message_shift,
    message_qkv,
    message_out,
    frame_gain,
    frame_shift,
    frame_qkv,
    frame_out,
    dense_gain,
    dense_shift,
    dense_in,
    dense_in_bias,
    dense_out,
    dense_out_bias,
):
    batch, frames_local, patches, width = video.shape
    hidden = dense_in.shape[1]
    groups = lax.axis_size("video")
    if (lax.axis_size("frame"), groups) == (8, 4):
        return reduced_inside(
            video, video_live, cotangent, message_proj, message_bias, message_gain, message_shift, message_qkv,
            message_out, frame_gain, frame_shift, frame_qkv, frame_out, dense_gain, dense_shift, dense_in,
            dense_in_bias, dense_out, dense_out_bias,
        )
    message_next, kept = message_forward(
        video, message_proj, message_bias, message_gain, message_shift, message_qkv, message_out
    )
    next_rows = message_next.reshape(batch * frames_local, width)
    packed, probs, first, mixed, middle, _ = call_k1(video, next_rows, frame_qkv, frame_out, frame_gain, frame_shift)
    output, grad_middle, part_in, part_out, part_bias, dense_small = call_k2(
        middle, cotangent, video_live, dense_in, dense_out, dense_in_bias, dense_out_bias, dense_gain, dense_shift
    )
    grad_tokens, part_frame, frame_small = call_k3(
        video, next_rows, grad_middle, packed, probs, first, mixed, frame_qkv, frame_out, frame_gain
    )
    grad_tokens = grad_tokens.reshape(batch, frames_local, T, width)
    grad_next = grad_tokens[:, :, patches]
    grad_class, rows, sum_bias, sum_gain, sum_shift = message_backward(
        kept, grad_next, message_proj, message_gain, message_qkv, message_out
    )
    grad_input = jnp.concatenate(
        [grad_tokens[:, :, :1] + grad_class[:, :, None, :], grad_tokens[:, :, 1:patches]], axis=2
    ).astype(bf)

    def total(value):
        share = lax.psum_scatter(value, "video", scatter_dimension=0, tiled=True)
        return lax.psum(share, "frame").astype(f32)

    grad_in = total(part_in.reshape(6, width, 4, 128).transpose(1, 2, 0, 3).reshape(width, hidden))
    grad_out = total(part_out.reshape(6, width, 4, 128).transpose(2, 0, 3, 1).reshape(hidden, width))
    part_frame = part_frame.reshape(6, width, 4, 128).transpose(1, 2, 0, 3).reshape(width, 4 * width)
    grad_frame = total(part_frame)
    vector = jnp.concatenate(
        [
            sum_bias,
            sum_gain,
            sum_shift,
            frame_small[0],
            frame_small[1],
            dense_small[1],
            dense_small[2],
            dense_small[0],
            part_bias.reshape(6, 4, 128).transpose(1, 0, 2).reshape(hidden),
        ]
    )
    vector = lax.psum(vector, ("video", "frame"))
    place = lax.axis_index("video")
    cut = width // groups

    def mine(start, length):
        return lax.dynamic_slice_in_dim(vector, start + place * (length // groups), length // groups)

    gathered = lax.all_gather(rows, ("video", "frame"), axis=0, tiled=True)

    def outer(left, first_column, last_column):
        part = lax.dynamic_slice_in_dim(gathered, left * width + place * cut, cut, axis=1)
        return weight_grad(part, gathered[:, first_column:last_column])

    return (
        output,
        grad_input,
        outer(0, 3 * width, 4 * width),
        mine(0, width),
        mine(width, width),
        mine(2 * width, width),
        outer(1, 4 * width, 7 * width),
        outer(2, 7 * width, 8 * width),
        mine(3 * width, width),
        mine(4 * width, width),
        grad_frame[:, : 3 * width],
        grad_frame[:, 3 * width :],
        mine(5 * width, width),
        mine(6 * width, width),
        grad_in,
        mine(8 * width, hidden),
        grad_out,
        mine(7 * width, width),
    )


def solution(mesh):
    in_specs = (
        P("video", "frame", None, None),
        P("video"),
        P("video", "frame", None, None),
        P(),
        P(),
        P(),
        P(),
        P(),
        P(),
        P(),
        P(),
        P(),
        P(),
        P(),
        P(),
        P(),
        P(),
        P(),
        P(),
    )
    out_specs = (
        P("video", "frame", None, None),
        P("video", "frame", None, None),
        P("video", None),
        P("video"),
        P("video"),
        P("video"),
        P("video", None),
        P("video", None),
        P("video"),
        P("video"),
        P("video", None),
        P("video", None),
        P("video"),
        P("video"),
        P("video", None),
        P("video"),
        P("video", None),
        P("video"),
    )
    return jax.shard_map(local, mesh=mesh, in_specs=in_specs, out_specs=out_specs, check_vma=False)
```

```python
import functools
import jax
import jax.numpy as jnp
from jax import lax
from jax.experimental import pallas as pl
from jax.experimental.pallas import tpu as pltpu
bf=jnp.bfloat16; f32=jnp.float32
EPS=1e-5
def dot(a,b,ca=1,cb=0): return lax.dot_general(a,b,(((ca,),(cb,)),((),())),preferred_element_type=f32)
FR=6; T=208; RR=FR*T; RP=1280; D=768
def k2(MB, mid, cot, live, din0,din1,din2,din3, do0,do1,do2,do3, bin_, bout, gain, shift,
       out_ref, gmid_ref, gdi_ref, gdo_ref, gbin_ref, small_ref,
       sec, G, act, dinn, oacc, gsec):
    j=pl.program_id(0)
    @pl.when(j==0)
    def _():
        ob=jnp.zeros((1,D),f32)
        sec[pl.ds(RR,RP-RR),:]=jnp.zeros((RP-RR,D),bf)
        G[pl.ds(RR,RP-RR),:]=jnp.zeros((RP-RR,D),bf)
        act[pl.ds(RR,RP-RR),:]=jnp.zeros((RP-RR,512),bf)
        dinn[pl.ds(RR,RP-RR),:]=jnp.zeros((RP-RR,512),bf)
        for f in range(FR):
            x=mid[f*T:(f+1)*T,:]
            mu=jnp.mean(x,-1,keepdims=True); c=x-mu
            inv=lax.rsqrt(jnp.mean(c*c,-1,keepdims=True)+EPS)
            sec[f*T:(f+1)*T,:]=(c*inv*gain[...]+shift[...]).astype(bf)
            g=cot[f,0].astype(f32)*live[f].astype(f32)
            g=jnp.concatenate([g,jnp.zeros((T-198,D),f32)],0)
            ob=ob+jnp.sum(g,0,keepdims=True)
            G[f*T:(f+1)*T,:]=g.astype(bf)
            oacc[f*T:(f+1)*T,:]=x+bout[...]
            gsec[f*T:(f+1)*T,:]=jnp.zeros((T,D),f32)
        small_ref[0:1,:]=ob
    din=jnp.concatenate([din0[...],din1[...],din2[...],din3[...]],1)
    do=jnp.concatenate([do0[...],do1[...],do2[...],do3[...]],0)
    b=jnp.concatenate([bin_[0:1,:],bin_[1:2,:],bin_[2:3,:],bin_[3:4,:]],1) if False else bin_[0]
    bsum=jnp.zeros((1,512),f32)
    for r in range(RR//MB):
        s=slice(r*MB,(r+1)*MB)
        inner=dot(sec[s,:],din)+b
        ga=dot(G[s,:],do,1,1)
        sg=0.5*jnp.tanh(0.851*inner)+0.5
        ac=inner*sg
        act[s,:]=ac.astype(bf)
        di=ga*(sg+1.702*ac*(1.0-sg))
        bsum=bsum+jnp.sum(di,0,keepdims=True)
        dinn[s,:]=di.astype(bf)
    gbin_ref[0]=bsum
    for r in range(RR//MB):
        s=slice(r*MB,(r+1)*MB)
        oacc[s,:]+=dot(act[s,:],do)
        gsec[s,:]+=dot(dinn[s,:],din,1,1)
    gdo_ref[0]=dot(G[...],act[...],0,0).astype(bf)
    gdi_ref[0]=dot(sec[...],dinn[...],0,0).astype(bf)
    @pl.when(j==pl.num_programs(0)-1)
    def _():
        gg=jnp.zeros((1,D),f32); gs=jnp.zeros((1,D),f32)
        for f in range(FR):
            s=slice(f*T,(f+1)*T)
            out_ref[f,0]=oacc[s,:][:198].astype(bf)
            x=mid[s,:]
            mu=jnp.mean(x,-1,keepdims=True); c=x-mu
            inv=lax.rsqrt(jnp.mean(c*c,-1,keepdims=True)+EPS)
            sc=c*inv
            go=gsec[s,:]
            gg=gg+jnp.sum(go*sc,0,keepdims=True); gs=gs+jnp.sum(go,0,keepdims=True)
            gsc=go*gain[...]
            gi=inv*(gsc-jnp.mean(gsc,-1,keepdims=True)-sc*jnp.mean(gsc*sc,-1,keepdims=True))
            gmid_ref[s,:]=G[s,:].astype(f32)+gi
        small_ref[1:2,:]=gg; small_ref[2:3,:]=gs
def call_k2(mid,cot,live,din,do,bin_,bout,gain,shift,MB=624):
    full=lambda *s: pl.BlockSpec(s,lambda j:(0,)*len(s))
    nq=din.shape[1]//512
    vm=pl.BlockSpec(memory_space=pltpu.VMEM)
    specs=[full(RR,D),full(FR,1,198,D),pl.BlockSpec(memory_space=pltpu.SMEM)]
    for q in range(4): specs.append(pl.BlockSpec((D,128),lambda j,q=q:(0,q*6+j)))
    for q in range(4): specs.append(pl.BlockSpec((128,D),lambda j,q=q:(q*6+j,0)))
    specs+= [pl.BlockSpec((1,1,512),lambda j:(j,0,0)),full(1,D),full(1,D),full(1,D)]
    b3=bin_.reshape(4,6,128).transpose(1,0,2).reshape(6,1,512)
    return pl.pallas_call(functools.partial(k2,MB),grid=(6,),in_specs=specs,
      out_specs=[full(FR,1,198,D),full(RR,D),pl.BlockSpec((1,D,512),lambda j:(j,0,0)),pl.BlockSpec((1,D,512),lambda j:(j,0,0)),pl.BlockSpec((1,1,512),lambda j:(j,0,0)),full(8,D)],
      out_shape=[jax.ShapeDtypeStruct((FR,1,198,D),bf),jax.ShapeDtypeStruct((RR,D),f32),jax.ShapeDtypeStruct((6,D,512),bf),jax.ShapeDtypeStruct((6,D,512),bf),jax.ShapeDtypeStruct((6,1,512),f32),jax.ShapeDtypeStruct((8,D),f32)],
      scratch_shapes=[pltpu.VMEM((RP,D),bf),pltpu.VMEM((RP,D),bf),pltpu.VMEM((RP,512),bf),pltpu.VMEM((RP,512),bf),pltpu.VMEM((RR,D),f32),pltpu.VMEM((RR,D),f32)],
      compiler_params=pltpu.CompilerParams(vmem_limit_bytes=61<<20,dimension_semantics=("arbitrary",)),
    )(mid,cot,live,din,din,din,din,do,do,do,do,b3,bout.reshape(1,D),gain.reshape(1,D),shift.reshape(1,D))
from jax.sharding import PartitionSpec as P
HEADS=12
HEAD_DIM=64
NEG=-1e30
VMEM_LIMIT=63<<20

def half_masks(rows):
    lane=lax.broadcasted_iota(jnp.int32,(rows,128),1)
    return lane<64
def attend_frames(h,wq,wk,wv,wo,qkv_ref,pt_ref,first_ref,mixed_ref,mid_ref):
    w=jnp.concatenate([wq[...],wk[...],wv[...]],1)
    qkv_ref[0,0:RR,:]=dot(first_ref[0:RR,:],w).astype(bf)
    qkv_ref[0,RR:RP,:]=jnp.zeros((RP-RR,384),bf)
    lo=half_masks(T)
    keep=lax.broadcasted_iota(jnp.int32,(16,T),0)<6
    zero=jnp.zeros((T,128),bf)
    def one(f,carry):
        s=pl.ds(pl.multiple_of(f*T,16),T)
        q=qkv_ref[0,s,0:128]*jnp.asarray(0.125,bf); k=qkv_ref[0,s,128:256]; v=qkv_ref[0,s,256:384]
        ps=[]; vs=[]
        for e in range(2):
            m=lo if e==0 else jnp.logical_not(lo)
            st=dot(k,jnp.where(m,q,zero),1,1)
            top=st[:192]; bot=jnp.where(keep,st[192:],NEG)
            mx=jnp.maximum(jnp.max(top,0,keepdims=True),jnp.max(bot,0,keepdims=True))
            top=jnp.exp(top-mx); bot=jnp.exp(bot-mx)
            tot=jnp.sum(top,0,keepdims=True)+jnp.sum(bot,0,keepdims=True)
            p=(jnp.concatenate([top,bot],0)*(1.0/tot)).astype(bf)
            pt_ref[0,f*2+e]=p
            ps.append(p); vs.append(jnp.where(m,v,zero))
        o=dot(jnp.concatenate(ps,0),jnp.concatenate(vs,0),0,0)
        mixed_ref[s,pl.ds(pl.multiple_of(h*128,128),128)]=o.astype(bf)
        return carry
    lax.fori_loop(0,FR,one,0,unroll=True)
    @pl.when(h==5)
    def _():
        mid_ref[...]+=dot(mixed_ref[0:RR,:],wo[...])
def k1(vid, mnext, wq, wk, wv, wo, gain, shift,
       qkv_ref, pt_ref, first_ref, mixed_ref, mid_ref, tok_ref):
    h=pl.program_id(0)
    @pl.when(h==0)
    def _():
        first_ref[pl.ds(RR,RP-RR),:]=jnp.zeros((RP-RR,D),bf)
        mixed_ref[pl.ds(RR,RP-RR),:]=jnp.zeros((RP-RR,D),bf)
        for f in range(FR):
            mid_ref[f*T+192:(f+1)*T,:]=jnp.zeros((T-192,D),f32)
            mid_ref[f*T:f*T+197,:]=vid[f,0].astype(f32)
            mid_ref[f*T+197:f*T+198,:]=mnext[f:f+1,:]
            x=mid_ref[f*T:(f+1)*T,:]
            tok_ref[f*T:(f+1)*T,:]=x.astype(bf)
            mu=jnp.mean(x,-1,keepdims=True); c=x-mu
            inv=lax.rsqrt(jnp.mean(c*c,-1,keepdims=True)+EPS)
            first_ref[f*T:(f+1)*T,:]=(c*inv*gain[...]+shift[...]).astype(bf)
    attend_frames(h,wq,wk,wv,wo,qkv_ref,pt_ref,first_ref,mixed_ref,mid_ref)
def call_k1(video,mnext,qkv,wo,gain,shift):
    full=lambda *s: pl.BlockSpec(s,lambda j:(0,)*len(s))
    blk=lambda *s: pl.BlockSpec((1,)+s,lambda j:(j,)+(0,)*len(s))
    specs=[full(FR,1,197,D),full(FR,D)]+[pl.BlockSpec((D,128),lambda j,o=o:(0,o*6+j)) for o in range(3)]+[full(D,D),full(1,D),full(1,D)]
    return pl.pallas_call(k1,grid=(6,),in_specs=specs,
      out_specs=[blk(RP,384),blk(12,T,T),full(RP,D),full(RP,D),full(RR,D),full(RR,D)],
      out_shape=[jax.ShapeDtypeStruct((6,RP,384),bf),jax.ShapeDtypeStruct((6,12,T,T),bf),jax.ShapeDtypeStruct((RP,D),bf),jax.ShapeDtypeStruct((RP,D),bf),jax.ShapeDtypeStruct((RR,D),f32),jax.ShapeDtypeStruct((RR,D),bf)],
      compiler_params=pltpu.CompilerParams(vmem_limit_bytes=61<<20,dimension_semantics=("arbitrary",)),
    )(video,mnext,qkv,qkv,qkv,wo,gain.reshape(1,D),shift.reshape(1,D))
def k3(vid, mnext, gmid, qkv, pt, first, mixed, wq, wk, wv, wo, gain, shift,
       gtok_ref, gf_ref, small_ref, glow, dO, dpk, wqkv):
    h=pl.program_id(0)
    @pl.when(h==0)
    def _():
        glow[pl.ds(RR,RP-RR),:]=jnp.zeros((RP-RR,D),bf)
        dpk[:,pl.ds(RR,RP-RR),:]=jnp.zeros((6,RP-RR,384),bf)
        glow[0:RR,:]=gmid[...].astype(bf)
        d=dot(glow[0:RR,:],wo[...],1,1).astype(bf)
        for i in range(6): dO[i]=d[:,i*128:(i+1)*128]
    lo=half_masks(T)
    zero=jnp.zeros((T,128),bf)
    for f in range(FR):
        s=slice(f*T,(f+1)*T)
        q=qkv[0,s,0:128]; k=qkv[0,s,128:256]; v=qkv[0,s,256:384]
        do=dO[h,s,:]
        dss=[]; ks=[]; dk=0.; dv=0.
        for e in range(2):
            m=lo if e==0 else jnp.logical_not(lo)
            doe=jnp.where(m,do,zero)
            pb=pt[0,f*2+e]
            p=pb.astype(f32)
            dp=dot(v,doe,1,1)
            delta=jnp.sum(dp*p,0,keepdims=True)
            ds=(p*(dp-delta)).astype(bf)
            dk=dk+dot(ds,jnp.where(m,q,zero))
            dv=dv+dot(pb,doe)
            dss.append(ds); ks.append(jnp.where(m,k,zero))
        dq=dot(jnp.concatenate(dss,0),jnp.concatenate(ks,0),0,0)*0.125
        dpk[h,s,0:128]=dq.astype(bf)
        dpk[h,s,128:256]=(dk*0.125).astype(bf)
        dpk[h,s,256:384]=dv.astype(bf)
    for i in range(6):
        @pl.when(h==i)
        def _():
            wqkv[:,i*128:(i+1)*128]=wq[...]; wqkv[:,D+i*128:D+(i+1)*128]=wk[...]; wqkv[:,2*D+i*128:2*D+(i+1)*128]=wv[...]
            gf_ref[0,:,384:512]=dot(mixed[...],glow[:,i*128:(i+1)*128],0,0).astype(bf)
    gf_ref[0,:,0:384]=dot(first[...],dpk[h],0,0).astype(bf)
    @pl.when(h==5)
    def _():
        dx=jnp.concatenate([dpk[i,0:RR,g*128:(g+1)*128] for g in range(3) for i in range(6)],1)
        gtok_ref[...]=dot(dx,wqkv[...],1,1)
        gg=jnp.zeros((1,D),f32); gs=jnp.zeros((1,D),f32)
        for f in range(FR):
            s=slice(f*T,(f+1)*T)
            x=jnp.concatenate([vid[f,0].astype(f32),mnext[f:f+1,:],jnp.zeros((T-198,D),f32)],0)
            mu=jnp.mean(x,-1,keepdims=True); c=x-mu
            inv=lax.rsqrt(jnp.mean(c*c,-1,keepdims=True)+EPS)
            sc=c*inv
            go=gtok_ref[s,:]
            gg=gg+jnp.sum(go*sc,0,keepdims=True); gs=gs+jnp.sum(go,0,keepdims=True)
            gsc=go*gain[...]
            gi=inv*(gsc-jnp.mean(gsc,-1,keepdims=True)-sc*jnp.mean(gsc*sc,-1,keepdims=True))
            gtok_ref[s,:]=gmid[s,:]+gi
        small_ref[0:1,:]=gg; small_ref[1:2,:]=gs
def call_k3(video,mnext,gmid,qkvs,pt,first,mixed,qkv,wo,gain):
    full=lambda *s: pl.BlockSpec(s,lambda j:(0,)*len(s))
    blk=lambda *s: pl.BlockSpec((1,)+s,lambda j:(j,)+(0,)*len(s))
    specs=[full(FR,1,197,D),full(FR,D),full(RR,D),blk(RP,384),blk(12,T,T),full(RP,D),full(RP,D)]+[pl.BlockSpec((D,128),lambda j,o=o:(0,o*6+j)) for o in range(3)]+[full(D,D),full(1,D),full(1,D)]
    return pl.pallas_call(k3,grid=(6,),in_specs=specs,
      out_specs=[full(RR,D),blk(D,512),full(8,D)],
      out_shape=[jax.ShapeDtypeStruct((RR,D),f32),jax.ShapeDtypeStruct((6,D,512),bf),jax.ShapeDtypeStruct((8,D),f32)],
      scratch_shapes=[pltpu.VMEM((RP,D),bf),pltpu.VMEM((6,RR,128),bf),pltpu.VMEM((6,RP,384),bf),pltpu.VMEM((D,3*D),bf)],
      compiler_params=pltpu.CompilerParams(vmem_limit_bytes=61<<20,dimension_semantics=("arbitrary",)),
    )(video,mnext,gmid,qkvs,pt,first,mixed,qkv,qkv,qkv,wo,gain.reshape(1,D),gain.reshape(1,D))


UNITS = 18
DENSE_UNITS = 12
STEPS = 12
LAG = (0, 1, 3, 5, 7, 9, 11, 13, 15)
ROWS = 192


def add_norm_stats(values):
    mean = jnp.mean(values, -1, keepdims=True)
    center = values - mean
    inverse = lax.rsqrt(jnp.mean(center * center, -1, keepdims=True) + EPS)
    return center * inverse, inverse


def norm_back(grad, scaled, inverse, gain):
    grad_scaled = grad * gain
    return inverse * (
        grad_scaled
        - jnp.mean(grad_scaled, -1, keepdims=True)
        - scaled * jnp.mean(grad_scaled * scaled, -1, keepdims=True)
    )


def pack_rows(values):
    return jnp.concatenate([values[:, : D // 2], values[:, D // 2 :]], 0).astype(bf)


def unpack_rows(blocks):
    wide = blocks.astype(f32)
    rows = jnp.concatenate([wide[:, :8], wide[:, 8:]], 2)
    return rows.reshape(rows.shape[0] * 8, D)


def gather_moves(B, ssem, rsem, f_at, v_at):
    me = v_at * 8 + f_at

    def move(k, src, target):
        return pltpu.make_async_remote_copy(
            src_ref=src,
            dst_ref=src,
            send_sem=ssem.at[k],
            recv_sem=rsem.at[k],
            device_id=target,
            device_id_type=pl.DeviceIdType.MESH,
        )

    def near():
        return [move(i - 1, B.at[me], (lax.rem(f_at + i, 8), v_at)) for i in range(1, 8)]

    def far():
        x, y = lax.rem(v_at, 2), lax.div(v_at, 2)
        block = B.at[pl.ds(v_at * 8, 8)]
        xo, yo = v_at + 1 - 2 * x, v_at + 2 - 4 * y
        return [move(7 + i, block, (f_at, to)) for i, to in enumerate((xo, yo, 3 - v_at))]

    return near, far


def greet(f_at, v_at):
    x, y = lax.rem(v_at, 2), lax.div(v_at, 2)
    barrier = pltpu.get_barrier_semaphore()
    others = [(lax.rem(f_at + i, 8), v_at) for i in range(1, 8)]
    others += [(f_at, to) for to in (v_at + 1 - 2 * x, v_at + 2 - 4 * y, 3 - v_at)]
    for other in others:
        pl.semaphore_signal(barrier, inc=1, device_id=other, device_id_type=pl.DeviceIdType.MESH)
    return lambda: pl.semaphore_wait(barrier, 10)


def message_rows(cls, proj, bias):
    return (dot(cls, proj) + bias).astype(bf).astype(f32)


def attend_rows(packed, mask, rows):
    lo = lax.broadcasted_iota(jnp.int32, (rows, 128), 1) < 64
    zero = jnp.zeros((rows, 128), bf)
    out, kept = [], []
    for h in range(6):
        q = packed[:, h * 128 : (h + 1) * 128] * jnp.asarray(0.125, bf)
        k = packed[:, D + h * 128 : D + (h + 1) * 128]
        v = packed[:, 2 * D + h * 128 : 2 * D + (h + 1) * 128]
        ps, vs = [], []
        for e in range(2):
            m = lo if e == 0 else jnp.logical_not(lo)
            st = jnp.where(mask, dot(k, jnp.where(m, q, zero), 1, 1), NEG)
            raised = jnp.exp(st - jnp.max(st, 0, keepdims=True))
            p = (raised * (1.0 / jnp.sum(raised, 0, keepdims=True))).astype(bf)
            ps.append(p)
            vs.append(jnp.where(m, v, zero))
        kept += ps
        out.append(dot(jnp.concatenate(ps, 0), jnp.concatenate(vs, 0), 0, 0).astype(bf))
    return jnp.concatenate(out, 1), kept


def first_kernel(
    vid, wq, wk, wv, wo, gain, shift, mproj_h, mqkv_h, mout_h, mbias, mgain, mshift,
    qkv_ref, pt_ref, first_out, mixed_ref, mid_ref, tok_out, mnext_ref, cls_ref,
    mproj, mqkv, mout, B, mrows, FI, TK, MX, wsem, ssem, rsem, osem,
):
    h = pl.program_id(0)
    f_at, v_at = lax.axis_index("frame"), lax.axis_index("video")
    near, far = gather_moves(B, ssem, rsem, f_at, v_at)

    def put_rows(rows, values):
        scaled, _ = add_norm_stats(values)
        FI[rows, :] = (scaled * gain[...] + shift[...]).astype(bf)
        TK[rows, :] = values.astype(bf)

    @pl.when(h == 0)
    def _():
        loads = [
            pltpu.make_async_copy(src, dst, wsem.at[i])
            for i, (src, dst) in enumerate(((mproj_h, mproj), (mqkv_h, mqkv), (mout_h, mout)))
        ]
        arrived = greet(f_at, v_at)
        for load in loads:
            load.start()
        own = jnp.concatenate([vid[f, 0, 0:1].astype(f32) for f in range(FR)] + [jnp.zeros((8 - FR, D), f32)], 0)
        B[v_at * 8 + f_at] = pack_rows(own)
        arrived()
        sends = near()
        for send in sends:
            send.start()
        FI[pl.ds(RR, RP - RR), :] = jnp.zeros((RP - RR, D), bf)
        MX[pl.ds(RR, RP - RR), :] = jnp.zeros((RP - RR, D), bf)
        def begin(f, rows, carry):
            mid_ref[rows, :] = jnp.concatenate([vid[f, 0].astype(f32), jnp.zeros((T - 197, D), f32)], 0)
            rows = pl.ds(pl.multiple_of(f * T, 16), 192)
            put_rows(rows, mid_ref[rows, :])
            return carry

        frames_loop(begin, 0)
        for load in loads:
            load.wait()
        for send in sends:
            send.wait()
        for send in far():
            send.start()
        cls = unpack_rows(B[pl.ds(v_at * 8, 8)]).astype(bf)
        message = message_rows(cls, mproj[...], mbias[...])
        scaled, _ = add_norm_stats(message)
        packed = dot((scaled * mgain[...] + mshift[...]).astype(bf), mqkv[...]).astype(bf)
        same = lax.rem(lax.broadcasted_iota(jnp.int32, (64, 64), 0), 8) == lax.rem(
            lax.broadcasted_iota(jnp.int32, (64, 64), 1), 8
        )
        mixed, _ = attend_rows(packed, same, 64)
        mrows[...] = message + dot(mixed, mout[...])
        mnext_ref[...] = mrows[pl.ds(pl.multiple_of(f_at * 8, 8), 8), :]
        last_row = lax.broadcasted_iota(jnp.int32, (16, D), 0) == 5

        def finish(f, rows, carry):
            rows = pl.ds(pl.multiple_of(f * T + 192, 16), 16)
            values = jnp.where(last_row, mnext_ref[pl.ds(f, 1), :], mid_ref[rows, :])
            mid_ref[rows, :] = values
            put_rows(rows, values)
            return carry

        frames_loop(finish, 0)

    keeps = [pltpu.make_async_copy(src, dst, osem.at[i]) for i, (src, dst) in enumerate(((FI, first_out), (TK, tok_out)))]

    @pl.when(h == 0)
    def _():
        for copy in keeps:
            copy.start()

    attend_frames(h, wq, wk, wv, wo, qkv_ref, pt_ref, FI, MX, mid_ref)
    mixed_ref[...] = MX[:, pl.ds(pl.multiple_of(h * 128, 128), 128)]

    @pl.when(h == 5)
    def _():
        for copy in keeps:
            copy.wait()
        for send in far():
            send.wait()
        cls_ref[...] = B[...]


def call_first(video, qkv, wo, gain, shift, mproj, mbias, mgain, mshift, mqkv, mout):
    one = pl.Buffered(1)
    full = lambda *s: pl.BlockSpec(s, lambda j: (0,) * len(s), pipeline_mode=one)
    keep = lambda *s: pl.BlockSpec(s, lambda j: (0,) * len(s))
    blk = lambda *s: pl.BlockSpec((1,) + s, lambda j: (j,) + (0,) * len(s))
    hbm = pl.BlockSpec(memory_space=pl.ANY)
    specs = [full(FR, 1, 197, D)] + [pl.BlockSpec((D, 128), lambda j, o=o: (0, o * 6 + j)) for o in range(3)]
    specs += [full(D, D), full(D), full(D), hbm, hbm, hbm, full(D), full(D), full(D)]
    shape = jax.ShapeDtypeStruct
    dma = pltpu.SemaphoreType.DMA
    return pl.pallas_call(
        first_kernel,
        grid=(6,),
        in_specs=specs,
        out_specs=[
            blk(RP, 384), blk(12, T, T), hbm, pl.BlockSpec((RP, 128), lambda j: (0, j)), keep(RR, D), hbm, keep(8, D),
            keep(32, 16, D // 2),
        ],
        out_shape=[
            shape((6, RP, 384), bf),
            shape((6, 12, T, T), bf),
            shape((RP, D), bf),
            shape((RP, D), bf),
            shape((RR, D), f32),
            shape((RR, D), bf),
            shape((8, D), f32),
            shape((32, 16, D // 2), bf),
        ],
        scratch_shapes=[
            pltpu.VMEM((D, D), bf),
            pltpu.VMEM((D, 3 * D), bf),
            pltpu.VMEM((D, D), bf),
            pltpu.VMEM((32, 16, D // 2), bf),
            pltpu.VMEM((64, D), f32),
            pltpu.VMEM((RP, D), bf),
            pltpu.VMEM((RR, D), bf),
            pltpu.VMEM((RP, D), bf),
            dma((3,)),
            dma((10,)),
            dma((10,)),
            dma((2,)),
        ],
        compiler_params=pltpu.CompilerParams(
            vmem_limit_bytes=VMEM_LIMIT, dimension_semantics=("arbitrary",), collective_id=2, has_side_effects=True
        ),
    )(video, qkv, qkv, qkv, wo, gain, shift, mproj, mqkv, mout, mbias, mgain, mshift)


MROWS = 256


def rows_forward(MP, PR, out):
    lo = lax.broadcasted_iota(jnp.int32, (MROWS, 128), 1) < 64
    zero = jnp.zeros((MROWS, 128), bf)
    ik = lax.broadcasted_iota(jnp.int32, (MROWS, MROWS), 0)
    iq = lax.broadcasted_iota(jnp.int32, (MROWS, MROWS), 1)
    same = jnp.logical_and(lax.rem(ik, 8) == lax.rem(iq, 8), lax.div(ik, 64) == lax.div(iq, 64))

    def one(h, carry):
        lanes = lambda o: pl.ds(pl.multiple_of(o * D + h * 128, 128), 128)
        q, k, v = (MP[:, lanes(o)] for o in range(3))
        q = q * jnp.asarray(0.125, bf)
        ps, vs = [], []
        for e in range(2):
            m = lo if e == 0 else jnp.logical_not(lo)
            st = jnp.where(same, dot(k, jnp.where(m, q, zero), 1, 1), NEG)
            raised = jnp.exp(st - jnp.max(st, 0, keepdims=True))
            p = (raised * (1.0 / jnp.sum(raised, 0, keepdims=True))).astype(bf)
            PR[2 * h + e] = p
            ps.append(p)
            vs.append(jnp.where(m, v, zero))
        out[1, :, lanes(0)] = dot(jnp.concatenate(ps, 0), jnp.concatenate(vs, 0), 0, 0).astype(bf)
        return carry

    lax.fori_loop(0, 6, one, 0)


def rows_back(MP, PR, GM, GP, start):
    lo = lax.broadcasted_iota(jnp.int32, (MROWS, 128), 1) < 64
    zero = jnp.zeros((MROWS, 128), bf)

    def one(h, carry):
        lanes = lambda o: pl.ds(pl.multiple_of(o * D + h * 128, 128), 128)
        q, k, v = (MP[:, lanes(o)] for o in range(3))
        do = GM[:, lanes(0)]
        dss, ks, dk, dv = [], [], 0.0, 0.0
        for e in range(2):
            m = lo if e == 0 else jnp.logical_not(lo)
            doe = jnp.where(m, do, zero)
            pb = PR[2 * h + e]
            p = pb.astype(f32)
            dp = dot(v, doe, 1, 1)
            ds = (p * (dp - jnp.sum(dp * p, 0, keepdims=True))).astype(bf)
            dk = dk + dot(ds, jnp.where(m, q, zero))
            dv = dv + dot(pb, doe)
            dss.append(ds)
            ks.append(jnp.where(m, k, zero))
        dq = dot(jnp.concatenate(dss, 0), jnp.concatenate(ks, 0), 0, 0) * 0.125
        for o, part in enumerate((dq, dk * 0.125, dv)):
            GP[:, lanes(o)] = part.astype(bf)
        return carry

    lax.fori_loop(start, start + 3, one, 0)


def frames_loop(body, carry):
    def step(f, carry):
        return body(f, pl.ds(pl.multiple_of(f * T, 16), T), carry)

    return lax.fori_loop(0, FR, step, carry)


def exchange(tick, odd, where, U, RA, RB, RC, RD, RE, F, ssem, rsem, fsem, F_out):
    c, x, y, z0, z1, core, xn, yn, zn, zf = where

    def at(lag, body):
        if isinstance(tick, int):
            late = tick - lag
            if 0 <= late < 12:
                body(late)
            if 0 <= late - 13 <= 10 and late % 2 == 1:
                body(12 + (late - 13) // 2)
            return
        dense = tick - lag

        @pl.when(jnp.logical_and(dense >= 0, dense < 12))
        def _():
            body(jnp.clip(dense, 0, 11))

        if (lag + odd) % 2:
            late = tick - lag - 13

            @pl.when(late >= 0)
            def _():
                body(12 + lax.div(jnp.maximum(late, 0), 2))

    def move(g, k, src, dst, target):
        return pltpu.make_async_remote_copy(
            src_ref=src,
            dst_ref=dst,
            send_sem=ssem.at[g, k],
            recv_sem=rsem.at[g, k],
            device_id=target,
            device_id_type=pl.DeviceIdType.MESH,
        )

    def a(g):
        return move(g, 0, U.at[lax.rem(g, 2), :, :, pl.ds(2 * (1 - c), 2)], RA.at[lax.rem(g, 6)], core)

    def b0(g):
        return move(g, 1, RA.at[lax.rem(g, 6), :, 1 - x, 0], RB.at[lax.rem(g, 8), 0], xn)

    def b1(g):
        return move(g, 2, RA.at[lax.rem(g, 6), 1 - y, :, 1], RB.at[lax.rem(g, 8), 1], yn)

    def c0(g):
        return move(g, 3, RB.at[lax.rem(g, 8), 0, 1 - y], RC.at[lax.rem(g, 8), 0], yn)

    def c1(g):
        return move(g, 4, RB.at[lax.rem(g, 8), 1, 1 - x], RC.at[lax.rem(g, 8), 1], xn)

    def d1(g):
        return move(g, 5, RC.at[lax.rem(g, 8), 1 - z0], RD.at[g], zn)

    def d2(g):
        return move(g, 6, RD.at[g, pl.ds((1 - z1) * 96, 96)], RE.at[g], zf)

    def e2(g):
        piece = F.at[g, 2 * c + z0, pl.ds(z1 * 96, 96)]
        return move(g, 7, piece, piece, zf)

    def e1(g):
        piece = F.at[g, 2 * c + z0]
        return move(g, 8, piece, piece, zn)

    def last(g):
        piece = F.at[g, pl.ds(2 * c, 2)]
        return move(g, 9, piece, piece, core)

    def on_done(g):
        last(g).wait()
        pltpu.make_async_copy(F.at[g], F_out.at[g], fsem.at[g]).start()

    def on_last(g):
        e1(g).wait()
        last(g).start()

    def on_e1(g):
        e2(g).wait()
        e1(g).start()

    def on_e2(g):
        d2(g).wait()
        own = pl.ds(z1 * 96, 96)
        F[g, 2 * c + z0, own] = RE[g] + RD[g, own]
        e2(g).start()

    def on_d2(g):
        d1(g).wait()
        RD[g] = RD[g] + RC[lax.rem(g, 8), z0]
        d2(g).start()

    def on_d1(g):
        c0(g).wait()
        c1(g).wait()
        RC[lax.rem(g, 8), 0] = RC[lax.rem(g, 8), 0] + RB[lax.rem(g, 8), 0, y]
        RC[lax.rem(g, 8), 1] = RC[lax.rem(g, 8), 1] + RB[lax.rem(g, 8), 1, x]
        d1(g).start()

    def on_c(g):
        b0(g).wait()
        b1(g).wait()
        RB[lax.rem(g, 8), 0] = RB[lax.rem(g, 8), 0] + RA[lax.rem(g, 6), :, x, 0]
        RB[lax.rem(g, 8), 1] = RB[lax.rem(g, 8), 1] + RA[lax.rem(g, 6), y, :, 1]
        c0(g).start()
        c1(g).start()

    def on_b(g):
        a(g).wait()
        RA[lax.rem(g, 6)] = RA[lax.rem(g, 6)] + U[lax.rem(g, 2), :, :, pl.ds(2 * c, 2)]
        b0(g).start()
        b1(g).start()

    def on_a(g):
        a(g).start()

    bodies = (on_a, on_b, on_c, on_d1, on_d2, on_e2, on_e1, on_last, on_done)
    for lag, body in zip(LAG, bodies):
        at(lag, body)


def main_kernel(
    mid, cot, live, din0, din1, din2, din3, do0, do1, do2, do3, bin_, bout, gain2, shift2,
    qkv, pt, wqkv_hbm, first_hbm, mixed_hbm, wo_hbm, tok_hbm, mnext, gain1,
    mproj_hbm, mqkv_hbm, mout_hbm, cls_hbm, mbias, mgain, mshift,
    out_hbm, gt_hbm, F_out, gp_out, lr_out, edge_out,
    sec, G, act, dinn, oacc, gsec, CB, first, mixed, wo, dpk,
    U, RA, RB, RC, RD, RE, F, BI, SB, NB, AD, AN, AS, WQ, CLS, MP, PR, GP, GM, LR, EDGE, ssem, rsem, fsem, lsem, adsem, adrem, ansem, anrem, assem, asrem,
):
    t = pl.program_id(0)
    f_at, v_at = lax.axis_index("frame"), lax.axis_index("video")
    c, z = lax.rem(f_at, 2), lax.div(f_at, 2)
    x, y = lax.rem(v_at, 2), lax.div(v_at, 2)
    z0, z1 = lax.rem(z, 2), lax.div(z, 2)
    core = (f_at + 1 - 2 * c, v_at)
    xn = (f_at, v_at + 1 - 2 * x)
    yn = (f_at, v_at + 2 - 4 * y)
    zn = (f_at + 2 - 4 * z0, v_at)
    zf = (f_at + 4 - 8 * z1, v_at)
    where = (c, x, y, z0, z1, core, xn, yn, zn, zf)

    small_near, small_far = gather_moves(AD, adsem, adrem, f_at, v_at)
    next_near, next_far = gather_moves(AN, ansem, anrem, f_at, v_at)
    sums_near, sums_far = gather_moves(AS, assem, asrem, f_at, v_at)

    def tick(n, odd=0):
        exchange(n, odd, where, U, RA, RB, RC, RD, RE, F, ssem, rsem, fsem, F_out)

    def fetch(k):
        src, dst = (
            (first_hbm, first),
            (mixed_hbm, mixed),
            (wo_hbm, wo),
            (tok_hbm, act.at[pl.ds(0, RR)]),
            (CB, out_hbm),
            (sec.at[pl.ds(0, RR)], gt_hbm),
            (cot, CB),
            (GP, gp_out),
            (LR, lr_out),
            (EDGE, edge_out),
            (mproj_hbm, G.at[pl.ds(0, D)]),
            (mqkv_hbm.at[:, pl.ds(0, D)], first.at[pl.ds(0, D)]),
            (mqkv_hbm.at[:, pl.ds(D, D)], mixed.at[pl.ds(0, D)]),
            (mqkv_hbm.at[:, pl.ds(2 * D, D)], act.at[pl.ds(0, D)]),
            (mout_hbm, wo),
            (cls_hbm, CLS),
            (wqkv_hbm, WQ),
        )[k]
        return pltpu.make_async_copy(src, dst, lsem.at[k])

    tail = pl.ds(RR, RP - RR)

    @pl.when(t == 0)
    def _():
        fetch(6).start()
        arrived = greet(f_at, v_at)
        for k in range(3):
            fetch(k).start()
        sec[tail, :] = jnp.zeros((RP - RR, D), bf)
        G[tail, :] = jnp.zeros((RP - RR, D), bf)
        act[tail, :] = jnp.zeros((RP - RR, D), bf)
        dinn[tail, :] = jnp.zeros((RP - RR, 512), bf)
        dpk[tail, :] = jnp.zeros((RP - RR, 3 * D), bf)
        SB[...] = jnp.zeros((8, D), f32)
        BI[...] = bin_[...].reshape(1, 4 * D)
        def begin(f, rows, carry):
            values = mid[rows, :]
            scaled, _ = add_norm_stats(values)
            sec[rows, :] = (scaled * gain2[...] + shift2[...]).astype(bf)
            oacc[rows, :] = values + bout[...]
            gsec[rows, :] = jnp.zeros((T, D), f32)
            return carry

        frames_loop(begin, 0)
        fetch(6).wait()

        def weigh(f, rows, total):
            grad = CB[f, 0].astype(f32) * live[f].astype(f32)
            G[rows, :] = jnp.concatenate([grad, jnp.zeros((T - 198, D), f32)], 0).astype(bf)
            return total + jnp.sum(grad, 0, keepdims=True)

        SB[4:5, :] = frames_loop(weigh, jnp.zeros((1, D), f32))
        arrived()

    din = lambda: jnp.concatenate([din0[...], din1[...], din2[...], din3[...]], 1)
    dout = lambda: jnp.concatenate([do0[...], do1[...], do2[...], do3[...]], 0)

    def put(slot, index, block):
        q, b = index
        U[slot, q // 2, q % 2, b] = block.astype(bf)

    @pl.when(t < 6)
    def _():
        w_in, w_out = din(), dout()
        bias = jnp.concatenate([BI[:, pl.ds(pl.multiple_of(q * D + t * 128, 128), 128)] for q in range(4)], 1)
        sums = jnp.zeros((1, 512), f32)
        MB = 416
        for r in range(RR // MB):
            s = slice(r * MB, (r + 1) * MB)
            inner = dot(sec[s, :], w_in) + bias
            ga = dot(G[s, :], w_out, 1, 1)
            sg = 0.5 * jnp.tanh(0.851 * inner) + 0.5
            ac = inner * sg
            act[s, 0:512] = ac.astype(bf)
            di = ga * (sg + 1.702 * ac * (1.0 - sg))
            sums = sums + jnp.sum(di, 0, keepdims=True)
            dinn[s, :] = di.astype(bf)
        for b in range(4):
            SB[b : b + 1, pl.ds(pl.multiple_of(t * 128, 128), 128)] = sums[:, b * 128 : (b + 1) * 128]
        part = dot(G[...], act[:, 0:512], 0, 0)
        for q in range(4):
            for b in range(4):
                put(0, (q, b), part[b * ROWS : (b + 1) * ROWS, q * 128 : (q + 1) * 128])

    lo = lax.broadcasted_iota(jnp.int32, (T, 128), 1) < 64
    zero = jnp.zeros((T, 128), bf)
    head = jnp.maximum(t - 6, 0)
    lanes = pl.ds(pl.multiple_of(head * 128, 128), 128)
    third = lambda o: pl.ds(pl.multiple_of(o * D + head * 128, 128), 128)

    def attend_back(first_frame, count):
        def one(f, carry):
            s = pl.ds(pl.multiple_of(f * T, 16), T)
            q, k, v = qkv[0, s, 0:128], qkv[0, s, 128:256], qkv[0, s, 256:384]
            do = G[s, lanes]
            dss, ks, dk, dv = [], [], 0.0, 0.0
            for e in range(2):
                m = lo if e == 0 else jnp.logical_not(lo)
                doe = jnp.where(m, do, zero)
                pb = pt[0, f * 2 + e]
                p = pb.astype(f32)
                dp = dot(v, doe, 1, 1)
                ds = (p * (dp - jnp.sum(dp * p, 0, keepdims=True))).astype(bf)
                dk = dk + dot(ds, jnp.where(m, q, zero))
                dv = dv + dot(pb, doe)
                dss.append(ds)
                ks.append(jnp.where(m, k, zero))
            dq = dot(jnp.concatenate(dss, 0), jnp.concatenate(ks, 0), 0, 0) * 0.125
            for o, part in enumerate((dq, dk * 0.125, dv)):
                dpk[s, third(o)] = part.astype(bf)
            return carry

        lax.fori_loop(first_frame, first_frame + count, one, 0, unroll=True)

    @pl.when(t == 6)
    def _():
        def turn(f, s, sums):
            CB[f, 0] = oacc[s, :][:198].astype(bf)
            scaled, inverse = add_norm_stats(mid[s, :])
            grad = gsec[s, :]
            total = G[s, :].astype(f32) + norm_back(grad, scaled, inverse, gain2[...])
            gsec[s, :] = total
            sec[s, :] = total.astype(bf)
            return sums[0] + jnp.sum(grad * scaled, 0, keepdims=True), sums[1] + jnp.sum(grad, 0, keepdims=True)

        gg, gs = frames_loop(turn, (jnp.zeros((1, D), f32), jnp.zeros((1, D), f32)))
        SB[5:6, :] = gg
        SB[6:7, :] = gs
        AD[v_at * 8 + f_at] = pack_rows(SB[...])
        for send in small_near():
            send.start()
        fetch(4).start()
        fetch(3).start()
        for k in range(3):
            fetch(k).wait()
        G[0:RR, :] = dot(sec[0:RR, :], wo[...], 1, 1).astype(bf)

    @pl.when(t >= 6)
    def _():
        attend_back(0, 3)

    tick(2 * t)

    @pl.when(t < 6)
    def _():
        w_in, w_out = din(), dout()
        part = dot(sec[...], dinn[...], 0, 0)
        for q in range(4):
            for b in range(4):
                put(1, (q, b), part[q * ROWS : (q + 1) * ROWS, b * 128 : (b + 1) * 128])
        oacc[...] += dot(act[0:RR, 0:512], w_out)
        gsec[...] += dot(dinn[0:RR, :], w_in, 1, 1)

    @pl.when(t >= 6)
    def _():
        attend_back(3, 3)
        slot = lax.rem(head, 2)
        part = dot(first[...], jnp.concatenate([dpk[:, third(o)] for o in range(3)], 1), 0, 0)
        for q in range(4):
            for b in range(3):
                put(slot, (q, b), part[q * ROWS : (q + 1) * ROWS, b * 128 : (b + 1) * 128])
        part = dot(mixed[...], sec[:, lanes], 0, 0)
        for q in range(4):
            put(slot, (q, 3), part[q * ROWS : (q + 1) * ROWS, :])

    tick(2 * t + 1, 1)

    @pl.when(t == 8)
    def _():
        for k in (14, 15, 16):
            fetch(k).start()
        for send in small_near():
            send.wait()
        for send in small_far():
            send.start()

    @pl.when(t == STEPS - 1)
    def _():
        for k in (10, 11, 12):
            fetch(k).start()
        fetch(3).wait()
        last_row = lax.broadcasted_iota(jnp.int32, (16, D), 0) == 5

        fetch(16).wait()
        grads = dot(jnp.concatenate([dpk[f * T + 192 : (f + 1) * T, :] for f in range(FR)], 0), WQ[...], 1, 1)
        NB[...] = jnp.zeros((8, D), f32)
        for f in range(FR):
            s = slice(f * T + 192, (f + 1) * T)
            values = jnp.where(last_row, mnext[f : f + 1, :], act[s, :].astype(f32))
            scaled, inverse = add_norm_stats(values)
            total = gsec[s, :] + norm_back(grads[16 * f : 16 * f + 16], scaled, inverse, gain1[...])
            NB[f : f + 1, :] = total[5:6]
        AN[v_at * 8 + f_at] = pack_rows(NB[...])
        for send in next_near():
            send.start()
        tick(24)

        def widen(r, carry):
            s = pl.ds(pl.multiple_of(r * 416, 16), 416)
            oacc[s, :] = dot(dpk[s, :], WQ[...], 1, 1)
            return carry

        lax.fori_loop(0, 3, widen, 0)
        tick(25)
        tick(26)
        for send in next_near():
            send.wait()
        for send in next_far():
            send.start()

        def end(f, s, sums):
            values = act[s, :].astype(f32)
            low = jnp.where(last_row, mnext[pl.ds(f, 1), :], values[192:])
            scaled, inverse = add_norm_stats(jnp.concatenate([values[:192], low], 0))
            grad = oacc[s, :]
            total = gsec[s, :] + norm_back(grad, scaled, inverse, gain1[...])
            sec[s, :] = total.astype(bf)
            return sums[0] + jnp.sum(grad * scaled, 0, keepdims=True), sums[1] + jnp.sum(grad, 0, keepdims=True)

        gg, gs = frames_loop(end, (jnp.zeros((1, D), f32), jnp.zeros((1, D), f32)))
        fetch(5).start()
        fetch(13).start()
        NB[0:1, :] = gg
        NB[1:2, :] = gs
        AS[v_at * 8 + f_at] = pack_rows(NB[...])
        for send in sums_near():
            send.start()
        tick(28)
        for k in (10, 11, 12, 14, 15):
            fetch(k).wait()
        gsec[0:MROWS, :] = message_rows(unpack_rows(CLS[...]).astype(bf), G[0:D, :], mbias[...])
        scaled, _ = add_norm_stats(gsec[0:MROWS, :])
        LR[0] = (scaled * mgain[...] + mshift[...]).astype(bf)
        fetch(13).wait()
        for o, ref in enumerate((first, mixed, act)):
            MP[:, o * D : (o + 1) * D] = dot(LR[0], ref[0:D, :]).astype(bf)
        tick(30)
        for send in sums_near():
            send.wait()
        for send in sums_far():
            send.start()
        rows_forward(MP, PR, LR)
        tick(32)
        for send in next_far():
            send.wait()
        kind = lax.rem(lax.broadcasted_iota(jnp.int32, (MROWS, D), 0), 8)
        LR[2] = jnp.where(kind < 6, unpack_rows(AN[...]), 0.0).astype(bf)
        GM[...] = dot(LR[2], wo[...], 1, 1).astype(bf)
        rows_back(MP, PR, GM, GP, 0)
        tick(34)
        rows_back(MP, PR, GM, GP, 3)
        grad = dot(GP[:, 0:D], first[0:D, :], 1, 1) + dot(GP[:, D : 2 * D], mixed[0:D, :], 1, 1)
        grad = grad + dot(GP[:, 2 * D : 3 * D], act[0:D, :], 1, 1)
        scaled, inverse = add_norm_stats(gsec[0:MROWS, :])
        total = LR[2].astype(f32) + norm_back(grad, scaled, inverse, mgain[...])
        LR[3] = total.astype(bf)
        fetch(7).start()
        fetch(8).start()
        tick(36)
        oacc[0:MROWS, :] = dot(LR[3], G[0:D, :], 1, 1)
        EDGE[0:8, :] = oacc[pl.ds(pl.multiple_of((v_at * 8 + f_at) * 8, 8), 8), :]
        lines = [jnp.sum(a, 0, keepdims=True) for a in (total, grad * scaled, grad)]
        for send in sums_far():
            send.wait()
        for send in small_far():
            send.wait()
        ends = jnp.sum(unpack_rows(AS[...]).reshape(32, 8, D), 0)
        small = jnp.sum(unpack_rows(AD[...]).reshape(32, 8, D), 0)
        lines += [ends[0:1], ends[1:2], small[5:6], small[6:7], small[4:5]]
        for i, line in enumerate(lines):
            EDGE[8 + i : 9 + i, :] = line
        EDGE[16:24, :] = small
        fetch(9).start()
        tick(38)

        def finish(g, carry):
            pltpu.make_async_copy(F.at[g], F_out.at[g], fsem.at[g]).wait()
            return carry

        lax.fori_loop(0, UNITS, finish, 0)
        for k in (4, 5, 7, 8, 9):
            fetch(k).wait()


def call_main(
    mid, cot, live, din, dout, bin_, bout, gain2, shift2, qkv, pt, wqkv, first, mixed, wo, tok, mnext, gain1,
    mproj, mqkv, mout, cls, mbias, mgain, mshift,
):
    one = pl.Buffered(1)
    full = lambda *s: pl.BlockSpec(s, lambda t: (0,) * len(s), pipeline_mode=one)
    hbm = pl.BlockSpec(memory_space=pl.ANY)
    dense = lambda t: jnp.minimum(t, 5)
    head = lambda t: jnp.maximum(t - 6, 0)
    specs = [full(RR, D), hbm, pl.BlockSpec(memory_space=pltpu.SMEM)]
    specs += [pl.BlockSpec((D, 128), lambda t, q=q: (0, q * 6 + dense(t))) for q in range(4)]
    specs += [pl.BlockSpec((128, D), lambda t, q=q: (q * 6 + dense(t), 0)) for q in range(4)]
    specs += [full(bin_.shape[0]), full(D), full(D), full(D)]
    specs += [pl.BlockSpec((1, RP, 384), lambda t: (head(t), 0, 0)), pl.BlockSpec((1, 12, T, T), lambda t: (head(t), 0, 0, 0))]
    specs += [hbm, hbm, hbm, hbm, hbm, full(8, D), full(D)] + [hbm] * 4 + [full(D)] * 3
    shape = jax.ShapeDtypeStruct
    dma = pltpu.SemaphoreType.DMA
    return pl.pallas_call(
        main_kernel,
        grid=(STEPS,),
        in_specs=specs,
        out_specs=[hbm] * 6,
        out_shape=[
            shape((FR, 1, 198, D), bf),
            shape((RR, D), bf),
            shape((UNITS, 4, ROWS, 128), bf),
            shape((MROWS, 3 * D), bf),
            shape((4, MROWS, D), bf),
            shape((24, D), f32),
        ],
        scratch_shapes=[
            pltpu.VMEM((RP, D), bf),
            pltpu.VMEM((RP, D), bf),
            pltpu.VMEM((RP, D), bf),
            pltpu.VMEM((RP, 512), bf),
            pltpu.VMEM((RR, D), f32),
            pltpu.VMEM((RR, D), f32),
            pltpu.VMEM((FR, 1, 198, D), bf),
            pltpu.VMEM((RP, D), bf),
            pltpu.VMEM((RP, D), bf),
            pltpu.VMEM((D, D), bf),
            pltpu.VMEM((RP, 3 * D), bf),
            pltpu.VMEM((2, 2, 2, 4, ROWS, 128), bf),
            pltpu.VMEM((6, 2, 2, 2, ROWS, 128), bf),
            pltpu.VMEM((8, 2, 2, ROWS, 128), bf),
            pltpu.VMEM((8, 2, ROWS, 128), bf),
            pltpu.VMEM((UNITS, ROWS, 128), bf),
            pltpu.VMEM((UNITS, ROWS // 2, 128), bf),
            pltpu.VMEM((UNITS, 4, ROWS, 128), bf),
            pltpu.VMEM((1, 4 * D), f32),
            pltpu.VMEM((8, D), f32),
            pltpu.VMEM((8, D), f32),
            pltpu.VMEM((32, 16, D // 2), bf),
            pltpu.VMEM((32, 16, D // 2), bf),
            pltpu.VMEM((32, 16, D // 2), bf),
            pltpu.VMEM((D, 3 * D), bf),
            pltpu.VMEM((32, 16, D // 2), bf),
            pltpu.VMEM((MROWS, 3 * D), bf),
            pltpu.VMEM((12, MROWS, MROWS), bf),
            pltpu.VMEM((MROWS, 3 * D), bf),
            pltpu.VMEM((MROWS, D), bf),
            pltpu.VMEM((4, MROWS, D), bf),
            pltpu.VMEM((24, D), f32),
            dma((UNITS, 10)),
            dma((UNITS, 10)),
            dma((UNITS,)),
            dma((17,)),
            dma((10,)),
            dma((10,)),
            dma((10,)),
            dma((10,)),
            dma((10,)),
            dma((10,)),
        ],
        compiler_params=pltpu.CompilerParams(
            vmem_limit_bytes=VMEM_LIMIT,
            dimension_semantics=("arbitrary",),
            collective_id=1,
            has_side_effects=True,
        ),
    )(mid, cot, live, din, din, din, din, dout, dout, dout, dout, bin_, bout, gain2, shift2,
      qkv, pt, wqkv, first, mixed, wo, tok, mnext, gain1, mproj, mqkv, mout, cls, mbias, mgain, mshift)


def final_kernel(
    F, gt, cls_blocks, gpacked, lr, edge, out_in,
    out, gvid, gproj, gmqkv, gmout, gfqkv, gfout, gdin, gdout, *rest,
):
    vecs, bias_in = rest[:8], rest[8]
    v_at = lax.axis_index("video")
    out[...] = out_in[...]

    def pick(parts):
        return jnp.where(v_at == 0, parts[0], jnp.where(v_at == 1, parts[1], jnp.where(v_at == 2, parts[2], parts[3])))

    def mine(values):
        return pick([values[:, i * ROWS : (i + 1) * ROWS] for i in range(4)])

    gproj[...] = dot(mine(unpack_rows(cls_blocks[...]).astype(bf)), lr[3], 0, 0)
    gmqkv[...] = dot(mine(lr[0]), gpacked[...], 0, 0)
    gmout[...] = dot(mine(lr[1]), lr[2], 0, 0)
    picked = mine(edge[8:16, :])
    for i, ref in enumerate(vecs):
        ref[...] = picked[i]
    bias_in[...] = pick([edge[16 + i : 17 + i, :] for i in range(4)])[0]
    for f in range(FR):
        gvid[f, 0] = gt[f * T : (f + 1) * T, :][:197]
        gvid[f, 0, 0:1] = (gt[f * T : f * T + 16, :].astype(f32)[0:1] + edge[f : f + 1, :]).astype(bf)
    for j in range(6):
        for b in range(4):
            at = b * D + j * 128
            gdin[:, at : at + 128] = F[2 * j + 1, b].astype(f32)
            gdout[j * 128 : (j + 1) * 128, b * ROWS : (b + 1) * ROWS] = F[2 * j, b].astype(f32).T
            if b < 3:
                gfqkv[:, at : at + 128] = F[12 + j, b].astype(f32)
            else:
                gfout[:, j * 128 : (j + 1) * 128] = F[12 + j, b].astype(f32)


def call_final(F, gt, cls_blocks, gpacked, lr, edge, output):
    vm = pl.BlockSpec(memory_space=pltpu.VMEM)
    shape = jax.ShapeDtypeStruct
    return pl.pallas_call(
        final_kernel,
        in_specs=[vm] * 7,
        out_specs=[vm] * 18,
        out_shape=[
            shape((FR, 1, 198, D), bf),
            shape((FR, 1, 197, D), bf),
            shape((ROWS, D), f32),
            shape((ROWS, 3 * D), f32),
            shape((ROWS, D), f32),
            shape((ROWS, 3 * D), f32),
            shape((ROWS, D), f32),
            shape((ROWS, 4 * D), f32),
            shape((4 * ROWS, D), f32),
        ]
        + [shape((ROWS,), f32)] * 8
        + [shape((D,), f32)],
        compiler_params=pltpu.CompilerParams(vmem_limit_bytes=VMEM_LIMIT),
    )(F, gt, cls_blocks, gpacked, lr, edge, output)


def column_sum(values):
    return jnp.sum(values.reshape(-1, values.shape[-1]), axis=0)


def matmul(left, right):
    return jnp.dot(left, right, preferred_element_type=f32)


def back_matmul(grad_low, weight):
    return lax.dot_general(grad_low, weight, (((grad_low.ndim - 1,), (1,)), ((), ())), preferred_element_type=f32)


def weight_grad(inputs_low, grad_low):
    left = inputs_low.reshape(-1, inputs_low.shape[-1])
    right = grad_low.reshape(-1, grad_low.shape[-1])
    return lax.dot_general(left, right, (((0,), (0,)), ((), ())), preferred_element_type=f32)


def norm_forward(values, gain, shift):
    center = values - jnp.mean(values, axis=-1, keepdims=True)
    inverse = lax.rsqrt(jnp.mean(center * center, axis=-1, keepdims=True) + EPS)
    scaled = center * inverse
    return (scaled * gain + shift, scaled, inverse)


def norm_backward(grad_out, scaled, inverse, gain):
    grad_scaled = grad_out * gain
    grad_in = inverse * (
        grad_scaled
        - jnp.mean(grad_scaled, axis=-1, keepdims=True)
        - scaled * jnp.mean(grad_scaled * scaled, axis=-1, keepdims=True)
    )
    return (grad_in, column_sum(grad_out * scaled), column_sum(grad_out))


def split_heads(values):
    return values.reshape(values.shape[:-1] + (HEADS, HEAD_DIM))


def attend_forward(query_rows, key_rows, value_rows):
    scores = jnp.einsum("bqhd,bkhd->bhqk", query_rows, key_rows, preferred_element_type=f32) * 0.125
    largest = jnp.max(scores, axis=-1, keepdims=True)
    raised = jnp.exp(scores - largest)
    total = jnp.sum(raised, axis=-1, keepdims=True)
    probs_low = (raised / total).astype(bf)
    mixed = jnp.einsum("bhqk,bkhd->bqhd", probs_low, value_rows, preferred_element_type=f32)
    return (mixed, largest + jnp.log(total))


def attend_backward(query_rows, key_rows, value_rows, log_total, grad_mixed):
    scores = jnp.einsum("bqhd,bkhd->bhqk", query_rows, key_rows, preferred_element_type=f32) * 0.125
    probs = jnp.exp(scores - log_total)
    grad_probs = jnp.einsum("bqhd,bkhd->bhqk", grad_mixed, value_rows, preferred_element_type=f32)
    grad_scores = probs * (grad_probs - jnp.sum(grad_probs * probs, axis=-1, keepdims=True))
    grad_low = grad_scores.astype(bf)
    grad_query = jnp.einsum("bhqk,bkhd->bqhd", grad_low, key_rows, preferred_element_type=f32) * 0.125
    grad_key = jnp.einsum("bhqk,bqhd->bkhd", grad_low, query_rows, preferred_element_type=f32) * 0.125
    grad_value = jnp.einsum("bhqk,bqhd->bkhd", probs.astype(bf), grad_mixed, preferred_element_type=f32)
    return (grad_query, grad_key, grad_value)


def message_forward(video, message_proj, message_bias, message_gain, message_shift, message_qkv, message_out):
    width = video.shape[-1]
    batch, frames_local = video.shape[:2]
    class_rows = video[:, :, 0, :]
    message = (matmul(class_rows, message_proj) + message_bias).astype(bf)
    message_wide = message.astype(f32)
    normed_own, scaled_own, inverse_own = norm_forward(message_wide, message_gain, message_shift)
    normed_low = normed_own.astype(bf)
    everyone = lax.all_gather(message, "frame", axis=1, tiled=True)
    normed_all = norm_forward(everyone.astype(f32), message_gain, message_shift)[0]
    key_value = matmul(normed_all.astype(bf), message_qkv[:, width:]).astype(bf)
    query = split_heads(matmul(normed_low, message_qkv[:, :width]).astype(bf))
    key = split_heads(key_value[..., :width])
    value = split_heads(key_value[..., width:])
    mixed, total = attend_forward(query, key, value)
    mixed_low = mixed.reshape(batch, frames_local, width).astype(bf)
    message_next = message_wide + matmul(mixed_low, message_out)
    return message_next, (class_rows, normed_low, scaled_own, inverse_own, query, key, value, mixed_low, total)


def message_backward(kept, grad_next, message_proj, message_gain, message_qkv, message_out):
    class_rows, normed_low, scaled_own, inverse_own, query, key, value, mixed_low, total = kept
    batch, frames_local, width = grad_next.shape
    frames_all = key.shape[1]
    grad_next_low = grad_next.astype(bf)
    grad_mixed = split_heads(back_matmul(grad_next_low, message_out).astype(bf))
    grad_q, grad_k, grad_v = attend_backward(query, key, value, total, grad_mixed)
    key_value_grad = jnp.concatenate(
        [grad_k.reshape(batch, frames_all, width), grad_v.reshape(batch, frames_all, width)], axis=-1
    )
    own = lax.psum_scatter(key_value_grad.astype(bf), "frame", scatter_dimension=1, tiled=True)
    packed = jnp.concatenate([grad_q.reshape(batch, frames_local, width).astype(bf), own], axis=-1)
    grad_in, grad_gain, grad_shift = norm_backward(
        back_matmul(packed, message_qkv), scaled_own, inverse_own, message_gain
    )
    grad_message = grad_next + grad_in
    grad_message_low = grad_message.astype(bf)
    grad_class = back_matmul(grad_message_low, message_proj)
    rows = jnp.concatenate([class_rows, normed_low, mixed_low, grad_message_low, packed, grad_next_low], axis=-1)
    rows = rows.reshape(batch * frames_local, -1)
    return grad_class, rows, column_sum(grad_message), grad_gain, grad_shift


def reduced_inside(
    video, video_live, cotangent, message_proj, message_bias, message_gain, message_shift, message_qkv,
    message_out, frame_gain, frame_shift, frame_qkv, frame_out, dense_gain, dense_shift, dense_in,
    dense_in_bias, dense_out, dense_out_bias,
):
    packed, probs, first, mixed, middle, tokens, next_rows, class_blocks = call_first(
        video, frame_qkv, frame_out, frame_gain, frame_shift,
        message_proj, message_bias, message_gain, message_shift, message_qkv, message_out,
    )
    output, grad_rows, reduced, grad_packed, sides, edge = call_main(
        middle, cotangent, video_live, dense_in, dense_out, dense_in_bias, dense_out_bias, dense_gain, dense_shift,
        packed, probs, frame_qkv, first, mixed, frame_out, tokens, next_rows, frame_gain,
        message_proj, message_qkv, message_out, class_blocks, message_bias, message_gain, message_shift,
    )
    output, grad_input, g_proj, g_mqkv, g_mout, g_fqkv, g_fout, g_in, g_out, *lines = call_final(
        reduced, grad_rows, class_blocks, grad_packed, sides, edge, output
    )
    return (
        output, grad_input, g_proj, lines[0], lines[1], lines[2], g_mqkv, g_mout, lines[3], lines[4], g_fqkv, g_fout,
        lines[5], lines[6], g_in, lines[8], g_out, lines[7],
    )


def local(
    video,
    video_live,
    cotangent,
    message_proj,
    message_bias,
    message_gain,
    message_shift,
    message_qkv,
    message_out,
    frame_gain,
    frame_shift,
    frame_qkv,
    frame_out,
    dense_gain,
    dense_shift,
    dense_in,
    dense_in_bias,
    dense_out,
    dense_out_bias,
):
    batch, frames_local, patches, width = video.shape
    hidden = dense_in.shape[1]
    groups = lax.axis_size("video")
    if (lax.axis_size("frame"), groups) == (8, 4):
        return reduced_inside(
            video, video_live, cotangent, message_proj, message_bias, message_gain, message_shift, message_qkv,
            message_out, frame_gain, frame_shift, frame_qkv, frame_out, dense_gain, dense_shift, dense_in,
            dense_in_bias, dense_out, dense_out_bias,
        )
    message_next, kept = message_forward(
        video, message_proj, message_bias, message_gain, message_shift, message_qkv, message_out
    )
    next_rows = message_next.reshape(batch * frames_local, width)
    packed, probs, first, mixed, middle, _ = call_k1(video, next_rows, frame_qkv, frame_out, frame_gain, frame_shift)
    output, grad_middle, part_in, part_out, part_bias, dense_small = call_k2(
        middle, cotangent, video_live, dense_in, dense_out, dense_in_bias, dense_out_bias, dense_gain, dense_shift
    )
    grad_tokens, part_frame, frame_small = call_k3(
        video, next_rows, grad_middle, packed, probs, first, mixed, frame_qkv, frame_out, frame_gain
    )
    grad_tokens = grad_tokens.reshape(batch, frames_local, T, width)
    grad_next = grad_tokens[:, :, patches]
    grad_class, rows, sum_bias, sum_gain, sum_shift = message_backward(
        kept, grad_next, message_proj, message_gain, message_qkv, message_out
    )
    grad_input = jnp.concatenate(
        [grad_tokens[:, :, :1] + grad_class[:, :, None, :], grad_tokens[:, :, 1:patches]], axis=2
    ).astype(bf)

    def total(value):
        share = lax.psum_scatter(value, "video", scatter_dimension=0, tiled=True)
        return lax.psum(share, "frame").astype(f32)

    grad_in = total(part_in.reshape(6, width, 4, 128).transpose(1, 2, 0, 3).reshape(width, hidden))
    grad_out = total(part_out.reshape(6, width, 4, 128).transpose(2, 0, 3, 1).reshape(hidden, width))
    part_frame = part_frame.reshape(6, width, 4, 128).transpose(1, 2, 0, 3).reshape(width, 4 * width)
    grad_frame = total(part_frame)
    vector = jnp.concatenate(
        [
            sum_bias,
            sum_gain,
            sum_shift,
            frame_small[0],
            frame_small[1],
            dense_small[1],
            dense_small[2],
            dense_small[0],
            part_bias.reshape(6, 4, 128).transpose(1, 0, 2).reshape(hidden),
        ]
    )
    vector = lax.psum(vector, ("video", "frame"))
    place = lax.axis_index("video")
    cut = width // groups

    def mine(start, length):
        return lax.dynamic_slice_in_dim(vector, start + place * (length // groups), length // groups)

    gathered = lax.all_gather(rows, ("video", "frame"), axis=0, tiled=True)

    def outer(left, first_column, last_column):
        part = lax.dynamic_slice_in_dim(gathered, left * width + place * cut, cut, axis=1)
        return weight_grad(part, gathered[:, first_column:last_column])

    return (
        output,
        grad_input,
        outer(0, 3 * width, 4 * width),
        mine(0, width),
        mine(width, width),
        mine(2 * width, width),
        outer(1, 4 * width, 7 * width),
        outer(2, 7 * width, 8 * width),
        mine(3 * width, width),
        mine(4 * width, width),
        grad_frame[:, : 3 * width],
        grad_frame[:, 3 * width :],
        mine(5 * width, width),
        mine(6 * width, width),
        grad_in,
        mine(8 * width, hidden),
        grad_out,
        mine(7 * width, width),
    )


def solution(mesh):
    in_specs = (
        P("video", "frame", None, None),
        P("video"),
        P("video", "frame", None, None),
        P(),
        P(),
        P(),
        P(),
        P(),
        P(),
        P(),
        P(),
        P(),
        P(),
        P(),
        P(),
        P(),
        P(),
        P(),
        P(),
    )
    out_specs = (
        P("video", "frame", None, None),
        P("video", "frame", None, None),
        P("video", None),
        P("video"),
        P("video"),
        P("video"),
        P("video", None),
        P("video", None),
        P("video"),
        P("video"),
        P("video", None),
        P("video", None),
        P("video"),
        P("video"),
        P("video", None),
        P("video"),
        P("video", None),
        P("video"),
    )
    return jax.shard_map(local, mesh=mesh, in_specs=in_specs, out_specs=out_specs, check_vma=False)
```
